32 devices in a mesh: dp: 16 (over z, y, core), mp: 2 (over x).
Axes of the slice: x: 2, y: 2, z: 4, core: 2. Of those that a mesh axis runs over, the one named last changes fastest.
Arguments:
- tokens: bfloat16 [16384, 768], P('dp'), may hold values from -6 to 6
- document_lengths: int32 [1, 8], replicated, may hold values from 0 to 16384, as said below
- feature_maps: bfloat16 [12, 64, 256], replicated, may hold values from -5 to 5
- joint_weight: bfloat16 [768, 2304], P(('dp', 'mp')), may hold values from -0.21875 to 0.21875
- joint_bias: bfloat16 [2304], P(('dp', 'mp')), may hold values from -1.25 to 1.25
- output_weight: bfloat16 [768, 768], P(('dp', 'mp')), may hold values from -1.75 to 1.75
- output_bias: bfloat16 [768], P(('dp', 'mp')), may hold values from -1.25 to 1.25
- first_gain: bfloat16 [768], P(('dp', 'mp')), may hold values from 0.25 to 1.75
- first_shift: bfloat16 [768], P(('dp', 'mp')), may hold values from -1.25 to 1.25
- up_weight: bfloat16 [768, 3072], P(None, 'mp'), may hold values from -0.21875 to 0.21875
- up_bias: bfloat16 [3072], P('mp'), may hold values from -1.25 to 1.25
- down_weight: bfloat16 [3072, 768], P('mp'), may hold values from -0.109375 to 0.109375
- down_bias: bfloat16 [768], replicated, may hold values from -1.25 to 1.25
- second_gain: bfloat16 [768], P(('dp', 'mp')), may hold values from 0.25 to 1.75
- second_shift: bfloat16 [768], P(('dp', 'mp')), may hold values from -1.25 to 1.25
- cotangent: bfloat16 [16384, 768], P('dp'), may hold values from -6 to 6
Outputs:
- layer_output: bfloat16 [16384, 768], P('dp')
- tokens_grad: bfloat16 [16384, 768], P('dp')
- joint_weight_grad: float32 [768, 2304], P(('dp', 'mp'))
- joint_bias_grad: float32 [2304], P(('dp', 'mp'))
- output_weight_grad: float32 [768, 768], P(('dp', 'mp'))
- output_bias_grad: float32 [768], P(('dp', 'mp'))
- first_gain_grad: float32 [768], P(('dp', 'mp'))
- first_shift_grad: float32 [768], P(('dp', 'mp'))
- up_weight_grad: float32 [768, 3072], P(None, 'mp')
- up_bias_grad: float32 [3072], P('mp')
- down_weight_grad: float32 [3072, 768], P('mp')
- down_bias_grad: float32 [768], replicated
- second_gain_grad: float32 [768], P(('dp', 'mp'))
- second_shift_grad: float32 [768], P(('dp', 'mp'))
The draws below stay inside these ranges and needn't reach their ends.
Inputs may be any that keep to these rules, and one draw needn't show every extreme that they name: `document_lengths`: each row of 16384 positions holds its 8 documents in order from its first position, then padding. In every row one document has more than 15360 tokens and the others together with the padding fewer than 1024.
All inputs are finite; a program needn't handle non-finite values.
Results may differ from the reference program's by a relative error of at most 0.033.
Values may be sent and summed in bfloat16 or wider, within the bound.
No kernel may reach another device: no remote copies, remote signals or barrier semaphores. Data moves between devices by JAX's collectives and lax.ppermute only.
A program may use at most 576 MiB of HBM per device.

```python
import math
import jax
import jax.numpy as jnp
from jax import lax

D = 768
HEADS = 12
HD = 64
FEAT = 256
FF = 3072
TOK_DEV = 1024
DOCS = 8
ROW = 16384
TOKENS = 16384
ROWS = 1


def draw_document_lengths(key, part):
    key = jax.random.fold_in(key, 7)
    keys_all = jax.random.split(key, 3)
    short_most = TOK_DEV // DOCS
    rolled = jax.random.randint(keys_all[0], (ROWS, DOCS), 0, short_most + 1)
    short_lengths = rolled * rolled * rolled // (short_most * short_most)
    main_slot = jax.random.randint(keys_all[1], (ROWS, 1), 0, DOCS)
    padding = jax.random.randint(keys_all[2], (ROWS, 1), 0, short_most)
    is_main = jnp.arange(DOCS, dtype=jnp.int32)[None, :] == main_slot
    others = jnp.sum(jnp.where(is_main, 0, short_lengths), axis=1, keepdims=True)
    return jnp.where(is_main, ROW - others - padding, short_lengths).astype(jnp.int32)


def levels(key, shape, shards, low, top_value):
    def one(dim, blocks):
        draws = jax.random.uniform(jax.random.fold_in(jax.random.fold_in(key, 6), dim), (blocks,), jnp.float32, low / len(shards), top_value / len(shards))
        return jnp.repeat(jnp.exp(draws), shape[dim] // blocks).reshape((-1,) + (1,) * (len(shape) - dim - 1))

    gain = one(*shards[0])
    for cut in shards[1:]:
        gain = gain * one(*cut)
    return gain


def normal_values(key, extent, deviation, reach, cuts=(), kind=jnp.bfloat16):
    loudness = levels(key, extent, cuts, -0.22, 0.18) if cuts else 1.0
    values = jax.random.normal(key, extent, jnp.float32) * deviation * loudness
    return jnp.minimum(jnp.maximum(values, -reach), reach).astype(kind)


def setup_inputs(seed: int = 0) -> dict:
    key_list = jax.random.split(jax.random.key(seed), 17)
    return {
        "tokens": normal_values(key_list[0], (TOKENS, D), 1.0, 6.0, ((0, 16),)),
        "document_lengths": draw_document_lengths(jax.random.fold_in(key_list[16], 71), 0),
        "feature_maps": normal_values(key_list[2], (HEADS, HD, FEAT), 1.0, 5.0),
        "joint_weight": normal_values(key_list[3], (D, 3 * D), D ** -0.5, 0.21875, ((0, 32),)),
        "joint_bias": normal_values(key_list[4], (3 * D,), 0.2, 1.25, ((0, 32),)),
        "output_weight": normal_values(key_list[5], (D, D), (D // 64) ** -0.5, 1.75, ((0, 32),)),
        "output_bias": normal_values(key_list[6], (D,), 0.2, 1.25, ((0, 32),)),
        "first_gain": jnp.clip(1.0 + 0.15 * jax.random.normal(key_list[7], (D,), jnp.float32), 0.25, 1.75).astype(jnp.bfloat16),
        "first_shift": normal_values(key_list[8], (D,), 0.2, 1.25, ((0, 32),)),
        "up_weight": normal_values(key_list[9], (D, FF), D ** -0.5, 0.21875, ((1, 2),)),
        "up_bias": normal_values(key_list[10], (FF,), 0.2, 1.25, ((0, 2),)),
        "down_weight": normal_values(key_list[11], (FF, D), FF ** -0.5, 0.109375, ((0, 2),)),
        "down_bias": normal_values(key_list[12], (D,), 0.2, 1.25),
        "second_gain": jnp.clip(1.0 + 0.15 * jax.random.normal(key_list[13], (D,), jnp.float32), 0.25, 1.75).astype(jnp.bfloat16),
        "second_shift": normal_values(key_list[14], (D,), 0.2, 1.25, ((0, 32),)),
        "cotangent": normal_values(key_list[15], (TOKENS, D), 1.0, 6.0, ((0, 16),)),
    }


@jax.custom_vjp
def low(v):
    return lax.optimization_barrier(v.astype(jnp.bfloat16)).astype(jnp.float32)

@jax.custom_vjp
def low_back(v):
    return v

def low_keep(v):
    return (low(v), None)

def low_pass(kept, grad):
    return (grad,)

def back_keep(v):
    return (v, None)

def back_low(kept, grad):
    return (low(grad),)
low.defvjp(low_keep, low_pass)
low_back.defvjp(back_keep, back_low)
EPSILON = 1e-05
HIGHEST = lax.Precision.HIGHEST

def layer_norm(values, scale_gain, shift_bias):
    average = lax.optimization_barrier(jnp.mean(values, axis=-1, keepdims=True))
    centered = values - average
    inverse = lax.rsqrt(lax.optimization_barrier(jnp.mean(centered * centered, axis=-1, keepdims=True)) + EPSILON)
    return centered * inverse * scale_gain + shift_bias

def document_table(document_lengths):
    row_ends = jnp.cumsum(document_lengths, axis=1)
    places = jnp.arange(ROW, dtype=jnp.int32)
    document = lax.optimization_barrier(jnp.sum((row_ends[:, None, :] <= places[None, :, None]).astype(jnp.int32), axis=2))
    slot_ids = jnp.arange(DOCS, dtype=jnp.int32)
    return (document[:, :, None] == slot_ids[None, None, :]).astype(jnp.float32)

def feature_map(unscaled, feature_table):
    scaled = unscaled * HD ** (-0.25)
    projected = low_back(jnp.dot(low(scaled), feature_table, precision=HIGHEST))
    positive = jnp.exp(projected - 0.5 * lax.optimization_barrier(jnp.sum(scaled * scaled, axis=-1, keepdims=True))) / math.sqrt(FEAT)
    return low(positive)

def head_attention(pieces):
    queries, key_rows, values, feature_table, onehot = pieces
    query_feat = feature_map(queries, feature_table)
    key_feat = feature_map(key_rows, feature_table)
    spread_values = onehot[:, :, None] * low(values)[:, None, :]
    moments = jnp.einsum('jf,jde->fde', key_feat, spread_values, precision=HIGHEST)
    moments = low(low_back(moments))
    masses = jnp.dot(key_feat.T, onehot, precision=HIGHEST)
    spread = jnp.einsum('jf,fde->jde', query_feat, moments, precision=HIGHEST)
    numerator = low_back(lax.optimization_barrier(jnp.sum(spread * onehot[:, :, None], axis=1)))
    denominator = lax.optimization_barrier(jnp.sum(jnp.dot(query_feat, masses, precision=HIGHEST) * onehot, axis=1))
    live_mask = lax.optimization_barrier(jnp.sum(onehot, axis=1))
    safe_total = jnp.where(live_mask > 0.5, denominator, 1.0)
    return numerator / safe_total[:, None] * live_mask[:, None]

def per_head(block):
    return block.reshape(ROWS, ROW, HEADS, HD).transpose(0, 2, 1, 3).reshape(ROWS * HEADS, ROW, HD)

def forward(inputs, joint_weight, joint_bias, output_weight, output_bias, first_gain, first_shift, up_weight, up_bias, down_weight, down_bias, second_gain, second_shift, feature_table, onehot):
    joint_value = low_back(jnp.dot(inputs, joint_weight, precision=HIGHEST) + joint_bias)
    queries = per_head(joint_value[:, :D])
    key_rows = per_head(joint_value[:, D:2 * D])
    values = per_head(joint_value[:, 2 * D:])
    tables = jnp.tile(feature_table, (ROWS, 1, 1))
    row_masks = jnp.repeat(onehot, HEADS, axis=0)
    heads_out = lax.map(jax.checkpoint(head_attention), (queries, key_rows, values, tables, row_masks))
    attention = heads_out.reshape(ROWS, HEADS, ROW, HD).transpose(0, 2, 1, 3).reshape(TOKENS, D)
    branch = low_back(jnp.dot(low(attention), output_weight, precision=HIGHEST) + output_bias)
    hidden = layer_norm(inputs + branch, first_gain, first_shift)
    up_value = low_back(jnp.dot(low(hidden), up_weight, precision=HIGHEST) + up_bias)
    active = low(jax.nn.gelu(up_value, approximate=False))
    feedforward = low_back(jnp.dot(active, down_weight, precision=HIGHEST) + down_bias)
    return layer_norm(hidden + feedforward, second_gain, second_shift)

def reference(tokens, document_lengths, feature_maps, joint_weight, joint_bias, output_weight, output_bias, first_gain, first_shift, up_weight, up_bias, down_weight, down_bias, second_gain, second_shift, cotangent):
    onehot = document_table(document_lengths)
    feature_table = feature_maps.astype(jnp.float32)
    params = tuple((argument.astype(jnp.float32) for argument in (tokens, joint_weight, joint_bias, output_weight, output_bias, first_gain, first_shift, up_weight, up_bias, down_weight, down_bias, second_gain, second_shift)))

    def run(*weights):
        return forward(*weights, feature_table, onehot)
    result, pullback = jax.vjp(run, *params)
    gradients = pullback(cotangent.astype(jnp.float32))
    return (result.astype(jnp.bfloat16), gradients[0].astype(jnp.bfloat16), gradients[1], gradients[2], gradients[3], gradients[4], gradients[5], gradients[6], gradients[7], gradients[8], gradients[9], gradients[10], gradients[11], gradients[12])
```

```python
from functools import partial
import math

import jax
import jax.numpy as jnp
from jax import lax
from jax.experimental import pallas as pl
from jax.experimental.pallas import tpu as pltpu
from jax.sharding import PartitionSpec as P

EPSILON = 1e-05
F32 = jnp.float32
BF16 = jnp.bfloat16
LOG2E = math.log2(math.e)
VMEM_LIMIT = 56 * 1024 * 1024
SLOTS = 8


def nn(a, b):
    return lax.dot_general(a, b, (((1,), (0,)), ((), ())), preferred_element_type=F32)


def nt(a, b):
    return lax.dot_general(a, b, (((1,), (1,)), ((), ())), preferred_element_type=F32)


def tn(a, b):
    return lax.dot_general(a, b, (((0,), (0,)), ((), ())), preferred_element_type=F32)


def fold_rows(a):
    return jnp.sum(a.reshape(a.shape[0] // 8, 8, a.shape[1]), axis=0)


def bit_pairs(count, bit):
    return [(i, i ^ bit) for i in range(count)]


def dp_bits():
    count = lax.axis_size("dp")
    bits = []
    bit = count // 2
    while bit:
        bits.append(bit)
        bit //= 2
    return bits


def swap_dp(a, bit):
    return lax.ppermute(a, "dp", bit_pairs(lax.axis_size("dp"), bit))


def swap_mp(a):
    return lax.ppermute(a, "mp", [(0, 1), (1, 0)])


def mine(bit):
    return (lax.axis_index("dp") // bit) % 2


def join_pair(own, other, bit, axis):
    low = jnp.stack([own, other], axis)
    high = jnp.stack([other, own], axis)
    return jnp.where(bit == 0, low, high)


def gather_all(a):
    bits = dp_bits()
    rank = a.ndim
    for place, bit in enumerate(bits[:-1]):
        a = join_pair(a, swap_dp(a, bit), mine(bit), place)
    place = len(bits) - 1
    a = join_pair(a, swap_mp(a), lax.axis_index("mp"), place)
    a = join_pair(a, swap_dp(a, 1), mine(1), place)
    return a.reshape((-1,) + a.shape[a.ndim - rank + 1 :])


def scatter_sum(a):
    bits = dp_bits()
    count = lax.axis_size("dp")
    a = a.reshape((2,) * len(bits) + (a.shape[0] // count,) + a.shape[1:])
    left = list(bits)
    for bit in reversed(bits):
        axis = left.index(bit)
        left.pop(axis)
        own = lax.dynamic_index_in_dim(a, mine(bit), axis, False)
        send = lax.dynamic_index_in_dim(a, 1 - mine(bit), axis, False)
        got = swap_dp(send, bit)
        a = (own.astype(F32) + got.astype(F32)).astype(a.dtype)
    return a


def gather_dp(a):
    bits = dp_bits()
    for place, bit in enumerate(bits):
        a = join_pair(a, swap_dp(a, bit), mine(bit), place)
    return a.reshape((-1,) + a.shape[len(bits) + 1 :])


def sum_dp(a):
    return gather_dp(scatter_sum(a))


def other_half(a):
    rows = a.shape[0] // 2
    core = mine(1)
    part = lax.dynamic_slice_in_dim(a, core * rows, rows, 0)
    part = swap_mp(part)
    whole = join_pair(part, swap_dp(part, 1), core, 0)
    return whole.reshape(a.shape)


def full(shape):
    return pl.BlockSpec(shape, lambda t, *_: (0,) * len(shape), pipeline_mode=pl.Buffered(1))


def rows(tile, width):
    return pl.BlockSpec((tile, width), lambda t, *_: (t, 0))


def held(shape):
    return pl.BlockSpec(shape, lambda t, *_: (0,) * len(shape))


def call(kernel, tiles, in_specs, outs, scratch, flops):
    return pl.pallas_call(
        kernel,
        grid_spec=pltpu.PrefetchScalarGridSpec(
            num_scalar_prefetch=1,
            grid=(tiles,),
            in_specs=in_specs,
            out_specs=[spec for spec, _, _ in outs],
            scratch_shapes=scratch,
        ),
        out_shape=[jax.ShapeDtypeStruct(shape, kind) for _, shape, kind in outs],
        compiler_params=pltpu.CompilerParams(
            vmem_limit_bytes=VMEM_LIMIT, dimension_semantics=("arbitrary",)
        ),
        cost_estimate=pl.CostEstimate(flops=int(flops), bytes_accessed=20_000_000, transcendentals=0),
    )


def features(scaled, table):
    lhs = jnp.concatenate([scaled.astype(BF16), (-0.5 * scaled * scaled).astype(BF16)], axis=1)
    return jnp.exp2(nn(lhs, table) * LOG2E - 4.0)


def pack_tables(source, base, mass_base, table, masses, acc, macc):
    pairs = acc.shape[0]
    for p in range(pairs):
        for k in range(2):
            head = 2 * p + k
            table[pl.ds(base + head * 64, 64), :] = acc[
                p, k * 64 : (k + 1) * 64, k * 256 : (k + 1) * 256
            ].astype(table.dtype)
            masses[pl.ds(mass_base + head, 1), :] = jnp.sum(
                macc[p, :, k * 256 : (k + 1) * 256], axis=0, keepdims=True
            )


def unpack_tables(tabs, slot, table, base, masses, mass_base, repeat):
    pairs = tabs.shape[1]
    for p in range(pairs):
        for k in range(2):
            head = 2 * p + k
            span = slice(k * 256, (k + 1) * 256)
            tabs[slot, p, k * 64 : (k + 1) * 64, span] = table[pl.ds(base + head * 64, 64), :]
            mass = masses[pl.ds(mass_base + head, 1), :]
            if repeat:
                tabs[slot, p, 128 + k * 64 : 192 + k * 64, span] = jnp.broadcast_to(
                    mass, (64, 256)
                ).astype(BF16)
            else:
                high = mass.astype(BF16).astype(F32)
                index = lax.broadcasted_iota(jnp.int32, (64, 256), 0)
                spread = jnp.where(
                    index == 0,
                    jnp.broadcast_to(high, (64, 256)),
                    jnp.where(index == 1, jnp.broadcast_to(mass - high, (64, 256)), 0.0),
                )
                tabs[slot, p, 128 + k * 64 : 192 + k * 64, span] = spread.astype(BF16)


def fill_tables(flags, tabs, main, main_masses, small, small_masses, repeat):
    heads_rows = main.shape[0]
    mass_rows = main_masses.shape[0]
    tabs[...] = jnp.zeros_like(tabs)
    unpack_tables(tabs, 0, main, 0, main_masses, 0, repeat)

    @pl.when(flags[0, 9] > 0)
    def _():
        for j in range(1, SLOTS):
            unpack_tables(
                tabs, j, small, (j - 1) * heads_rows, small_masses, (j - 1) * mass_rows, repeat
            )


def keys_kernel(
    flags, x, weight, bias, table, slot,
    phi, values, scaled_out, main, main_masses, small, small_masses,
    acc, macc, sacc, smacc,
):
    t = pl.program_id(0)
    pairs = table.shape[0]
    width = pairs * 128
    slow_any = flags[0, 9] > 0

    @pl.when(t == 0)
    def _():
        acc[...] = jnp.zeros_like(acc)
        macc[...] = jnp.zeros_like(macc)

        @pl.when(slow_any)
        def _():
            sacc[...] = jnp.zeros_like(sacc)
            smacc[...] = jnp.zeros_like(smacc)

    both = nn(x[...], weight[...]) + bias[...]
    values[...] = both[:, width:].astype(BF16)
    for p in range(pairs):
        scaled = both[:, p * 128 : (p + 1) * 128] * 64 ** (-0.25)
        scaled_out[:, p * 128 : (p + 1) * 128] = scaled.astype(BF16)
        phi[:, p * 512 : (p + 1) * 512] = features(scaled, table[p]).astype(BF16)

    @pl.when(flags[t, 0] > 0)
    def _():
        for p in range(pairs):
            part = phi[:, p * 512 : (p + 1) * 512]
            acc[p] += tn(values[:, p * 128 : (p + 1) * 128], part)
            macc[p] += fold_rows(part.astype(F32))

    @pl.when(flags[t, 0] == 0)
    def _():
        def one(j, carry):
            @pl.when(flags[t, 1 + j] > 0)
            def _():
                mask = slot[...] == j
                wide = jnp.concatenate([mask] * 4, axis=1)
                for p in range(pairs):
                    part = phi[:, p * 512 : (p + 1) * 512]
                    value = values[:, p * 128 : (p + 1) * 128].astype(F32)
                    moment = tn(jnp.where(mask, value, 0.0).astype(BF16), part)
                    mass = fold_rows(jnp.where(wide, part.astype(F32), 0.0))

                    @pl.when(j == 0)
                    def _():
                        acc[p] += moment
                        macc[p] += mass

                    @pl.when(j > 0)
                    def _():
                        sacc[j - 1, p] += moment
                        smacc[j - 1, p] += mass

            return carry

        lax.fori_loop(0, SLOTS, one, 0)

    @pl.when(t == pl.num_programs(0) - 1)
    def _():
        pack_tables(None, 0, 0, main, main_masses, acc, macc)

        @pl.when(slow_any)
        def _():
            for j in range(SLOTS - 1):
                pack_tables(
                    None, j * main.shape[0], j * main_masses.shape[0], small, small_masses,
                    sacc.at[j], smacc.at[j],
                )


def queries_kernel(flags, x, weight, bias, table, select, phi, scaled_out, chosen):
    pairs = table.shape[0]
    query = nn(x[...], weight[...]) + bias[...]
    chosen[...] = nn(x[...], select[...]).astype(BF16)
    for p in range(pairs):
        scaled = query[:, p * 128 : (p + 1) * 128] * 64 ** (-0.25)
        scaled_out[:, p * 128 : (p + 1) * 128] = scaled.astype(BF16)
        phi[:, p * 512 : (p + 1) * 512] = features(scaled, table[p]).astype(BF16)


def center(z):
    average = jnp.mean(z, axis=1, keepdims=True)
    centered = z - average
    inverse = lax.rsqrt(jnp.mean(centered * centered, axis=1, keepdims=True) + EPSILON)
    return centered * inverse, inverse


def center_back(e, normed, inverse):
    first = jnp.mean(e, axis=1, keepdims=True)
    second = jnp.mean(e * normed, axis=1, keepdims=True)
    return inverse * (e - first - normed * second)


def middle_kernel(
    flags, x, cot, slot, phi, main, main_masses, small, small_masses,
    out_weight, up_own, up_other, down_own, down_other, bias_own, bias_other, vectors,
    layer_out, hidden_grad, normed_out, inverse_out, att_out, invden_out,
    active_out, dup_out, hidden_out, dffn_out, sums, up_sum,
    tabs, spread, gates,
):
    t = pl.program_id(0)
    pairs = tabs.shape[1]
    width = pairs * 128

    @pl.when(t == 0)
    def _():
        fill_tables(flags, tabs, main, main_masses, small, small_masses, True)
        sums[...] = jnp.zeros_like(sums)
        up_sum[...] = jnp.zeros_like(up_sum)

    @pl.when(flags[t, 0] > 0)
    def _():
        for p in range(pairs):
            spread[:, p * 256 : (p + 1) * 256] = nt(phi[:, p * 512 : (p + 1) * 512], tabs[0, p])

    @pl.when(flags[t, 0] == 0)
    def _():
        spread[...] = jnp.zeros_like(spread)

        def one(j, carry):
            @pl.when(flags[t, 1 + j] > 0)
            def _():
                mask = slot[...] == j
                wide = jnp.concatenate([mask] * 2, axis=1)
                for p in range(pairs):
                    got = nt(phi[:, p * 512 : (p + 1) * 512], tabs[j, p])
                    old = spread[:, p * 256 : (p + 1) * 256]
                    spread[:, p * 256 : (p + 1) * 256] = jnp.where(wide, got, old)

            return carry

        lax.fori_loop(0, SLOTS, one, 0)

    live = slot[...] < SLOTS
    for p in range(pairs):
        numerator = spread[:, p * 256 : p * 256 + 128]
        denominator = spread[:, p * 256 + 128 : (p + 1) * 256]
        inverse = jnp.where(live, 1.0 / jnp.where(live, denominator, 1.0), 0.0)
        invden_out[:, p * 128 : (p + 1) * 128] = inverse
        att_out[:, p * 128 : (p + 1) * 128] = (numerator * inverse).astype(BF16)

    def vector(i):
        return vectors[i : i + 1, :]

    branch = nn(att_out[...], out_weight[...]) + vector(0)
    first, first_inverse = center(x[...].astype(F32) + branch)
    normed_out[...] = first
    inverse_out[...] = jnp.broadcast_to(first_inverse, inverse_out.shape)
    hidden = first * vector(1) + vector(2)
    hidden_low = hidden.astype(BF16)
    hidden_out[...] = hidden_low
    step = 512
    half = up_own.shape[1]
    chunks = [(up_own, down_own, bias_own, 0, c, c) for c in range(0, half, step)]
    chunks += [(up_other, down_other, bias_other, 1, c, half + c) for c in range(0, half, step)]
    total = hidden + vector(3)
    other_active = []
    for up, down, bias, which, c, place in chunks:
        value = nn(hidden_low, up[:, c : c + step]) + bias[:, c : c + step]
        cdf = 0.5 + 0.5 * lax.erf(value * math.sqrt(0.5))
        gates[:, place : place + step] = cdf + value * jnp.exp2(
            value * value * (-0.5 * LOG2E)
        ) * (1.0 / math.sqrt(2.0 * math.pi))
        active = (value * cdf).astype(BF16)
        if which == 0:
            active_out[:, c : c + step] = active
        total = total + nn(active, down[c : c + step, :])
    second, second_inverse = center(total)
    layer_out[...] = (second * vector(4) + vector(5)).astype(BF16)
    g = cot[...].astype(F32)
    sums[0:8, :] += fold_rows(g * second)
    sums[8:16, :] += fold_rows(g)
    dsecond = center_back(g * vector(4), second, second_inverse)
    dffn = dsecond.astype(BF16)
    dffn_out[...] = dffn
    sums[16:24, :] += fold_rows(dffn.astype(F32))
    for up, down, bias, which, c, place in chunks:
        dup = (nt(dffn, down[c : c + step, :]) * gates[:, place : place + step]).astype(BF16)
        if which == 0:
            dup_out[:, c : c + step] = dup
            up_sum[:, c : c + step] += fold_rows(dup.astype(F32))
        dsecond = dsecond + nt(dup, up[:, c : c + step])
    hidden_grad[...] = dsecond


def attention_back_kernel(
    flags, hidden_grad, normed, inverse, att, invden, phi, slot, out_weight, gain, select,
    dfirst_out, dbranch_out, mixed, chosen, sums, main, main_masses, small, small_masses,
    acc, sacc,
):
    t = pl.program_id(0)
    pairs = acc.shape[0]
    slow_any = flags[0, 9] > 0

    @pl.when(t == 0)
    def _():
        acc[...] = jnp.zeros_like(acc)
        sums[...] = jnp.zeros_like(sums)

        @pl.when(slow_any)
        def _():
            sacc[...] = jnp.zeros_like(sacc)

    grad = hidden_grad[...]
    first = normed[...]
    sums[0:8, :] += fold_rows(grad * first)
    sums[8:16, :] += fold_rows(grad)
    dfirst = center_back(grad * gain[...], first, inverse[:, 0:1])
    dfirst_out[...] = dfirst
    dbranch = dfirst.astype(BF16)
    dbranch_out[...] = dbranch
    sums[16:24, :] += fold_rows(dbranch.astype(F32))
    chosen[...] = nn(att[...], select[...]).astype(BF16)
    datt = nt(dbranch, out_weight[...])
    ratio = datt * invden[...]
    dden = -ratio * att[...].astype(F32)
    for p in range(pairs):
        mixed[:, p * 256 : p * 256 + 128] = ratio[:, p * 128 : (p + 1) * 128].astype(BF16)
        mixed[:, p * 256 + 128 : (p + 1) * 256] = dden[:, p * 128 : (p + 1) * 128].astype(BF16)

    @pl.when(flags[t, 0] > 0)
    def _():
        for p in range(pairs):
            acc[p] += tn(mixed[:, p * 256 : (p + 1) * 256], phi[:, p * 512 : (p + 1) * 512])

    @pl.when(flags[t, 0] == 0)
    def _():
        def one(j, carry):
            @pl.when(flags[t, 1 + j] > 0)
            def _():
                mask = slot[...] == j
                wide = jnp.concatenate([mask] * 2, axis=1)
                for p in range(pairs):
                    part = mixed[:, p * 256 : (p + 1) * 256].astype(F32)
                    moment = tn(
                        jnp.where(wide, part, 0.0).astype(BF16), phi[:, p * 512 : (p + 1) * 512]
                    )

                    @pl.when(j == 0)
                    def _():
                        acc[p] += moment

                    @pl.when(j > 0)
                    def _():
                        sacc[j - 1, p] += moment

            return carry

        lax.fori_loop(0, SLOTS, one, 0)

    def pack(table, base, masses, mass_base, source):
        for p in range(pairs):
            for k in range(2):
                head = 2 * p + k
                span = slice(k * 256, (k + 1) * 256)
                table[pl.ds(base + head * 64, 64), :] = source[
                    p, k * 64 : (k + 1) * 64, span
                ].astype(BF16)
                masses[pl.ds(mass_base + head, 1), :] = jnp.sum(
                    source[p, 128 + k * 64 : 192 + k * 64, span], axis=0, keepdims=True
                )

    @pl.when(t == pl.num_programs(0) - 1)
    def _():
        pack(main, 0, main_masses, 0, acc)

        @pl.when(slow_any)
        def _():
            for j in range(SLOTS - 1):
                pack(small, j * main.shape[0], small_masses, j * main_masses.shape[0], sacc.at[j])


def masked_product(flags, t, slot, left, tabs, p, result):
    result[...] = jnp.zeros_like(result)

    def one(j, carry):
        @pl.when(flags[t, 1 + j] > 0)
        def _():
            mask = slot[...] == j
            wide = jnp.concatenate([mask] * 2, axis=1)
            part = jnp.where(wide, left.astype(F32), 0.0).astype(BF16)
            result[...] += nn(part, tabs[j, p])

        return carry

    lax.fori_loop(0, SLOTS, one, 0)


def queries_back_kernel(
    flags, mixed, phi, scaled, slot, main, main_masses, small, small_masses, table, weight, dfirst,
    dquery_out, partial_out, sums, tabs, work,
):
    t = pl.program_id(0)
    pairs = tabs.shape[1]

    @pl.when(t == 0)
    def _():
        fill_tables(flags, tabs, main, main_masses, small, small_masses, True)
        sums[...] = jnp.zeros_like(sums)

    def finish(p, grad):
        span = slice(p * 128, (p + 1) * 128)
        e = (grad * phi[:, p * 512 : (p + 1) * 512].astype(F32)).astype(BF16)
        back = nt(e, table[p])
        du = (back[:, :128] - scaled[:, span].astype(F32) * back[:, 128:]) * 64 ** (-0.25)
        dquery_out[:, span] = du.astype(BF16)

    @pl.when(flags[t, 0] > 0)
    def _():
        for p in range(pairs):
            finish(p, nn(mixed[:, p * 256 : (p + 1) * 256], tabs[0, p]))

    @pl.when(flags[t, 0] == 0)
    def _():
        for p in range(pairs):
            masked_product(flags, t, slot, mixed[:, p * 256 : (p + 1) * 256], tabs, p, work)
            finish(p, work[...])

    sums[...] += fold_rows(dquery_out[...].astype(F32))
    partial_out[...] = dfirst[...] + nt(dquery_out[...], weight[...])


def keys_back_kernel(
    flags, phi, values, scaled, slot, main, main_masses, small, small_masses, table, weight, partial_in,
    djoint_out, tokens_out, sums, tabs, work, vwork,
):
    t = pl.program_id(0)
    pairs = tabs.shape[1]
    width = pairs * 128

    @pl.when(t == 0)
    def _():
        fill_tables(flags, tabs, main, main_masses, small, small_masses, False)
        sums[...] = jnp.zeros_like(sums)

    def extended(p):
        value = values[:, p * 128 : (p + 1) * 128]
        return jnp.concatenate([value, jnp.ones_like(value)], axis=1)

    def finish(p, grad):
        span = slice(p * 128, (p + 1) * 128)
        e = (grad * phi[:, p * 512 : (p + 1) * 512].astype(F32)).astype(BF16)
        back = nt(e, table[p])
        du = (back[:, :128] - scaled[:, span].astype(F32) * back[:, 128:]) * 64 ** (-0.25)
        djoint_out[:, span] = du.astype(BF16)

    @pl.when(flags[t, 0] > 0)
    def _():
        for p in range(pairs):
            finish(p, nn(extended(p), tabs[0, p]))
            dvalue = nt(phi[:, p * 512 : (p + 1) * 512], tabs[0, p, :128, :])
            djoint_out[:, width + p * 128 : width + (p + 1) * 128] = dvalue.astype(BF16)

    @pl.when(flags[t, 0] == 0)
    def _():
        for p in range(pairs):
            masked_product(flags, t, slot, extended(p), tabs, p, work)
            finish(p, work[...])
            vwork[...] = jnp.zeros_like(vwork)

            def one(j, carry):
                @pl.when(flags[t, 1 + j] > 0)
                def _():
                    got = nt(phi[:, p * 512 : (p + 1) * 512], tabs[j, p, :128, :])
                    vwork[...] = jnp.where(slot[...] == j, got, vwork[...])

                return carry

            lax.fori_loop(0, SLOTS, one, 0)
            djoint_out[:, width + p * 128 : width + (p + 1) * 128] = vwork[...].astype(BF16)

    sums[...] += fold_rows(djoint_out[...].astype(F32))
    tokens_out[...] = (partial_in[...] + nt(djoint_out[...], weight[...])).astype(BF16)


def local(
    tokens, document_lengths, feature_maps, joint_weight, joint_bias, output_weight, output_bias,
    first_gain, first_shift, up_weight, up_bias, down_weight, down_bias, second_gain, second_shift,
    cotangent,
):
    count, width = tokens.shape
    heads, head_size, feature_count = feature_maps.shape
    pairs = heads // 2
    half = up_weight.shape[1]
    tile = 256
    tiles = count // tile
    rank = lax.axis_index("dp")
    dp = lax.axis_size("dp")
    mp = lax.axis_size("mp")
    mp_rank = lax.axis_index("mp")

    lengths = document_lengths[0]
    ends = jnp.cumsum(lengths)
    place = rank * count + jnp.arange(count, dtype=jnp.int32)
    document = jnp.sum((ends[None, :] <= place[:, None]).astype(jnp.int32), axis=1)
    longest = jnp.argmax(lengths).astype(jnp.int32)
    slot = jnp.where(
        document == longest,
        0,
        jnp.where(document >= SLOTS, SLOTS, jnp.where(document < longest, document + 1, document)),
    )
    slots = jnp.broadcast_to(slot[:, None], (count, 128))
    present = jnp.max(
        (slot.reshape(tiles, tile)[:, :, None] == jnp.arange(SLOTS)[None, None, :]).astype(jnp.int32),
        axis=1,
    )
    all_main = jnp.max(slot.reshape(tiles, tile), axis=1, keepdims=True) == 0
    any_slow = jnp.broadcast_to(jnp.max(slot) > 0, (tiles, 1))
    flags = jnp.concatenate(
        [all_main.astype(jnp.int32), present, any_slow.astype(jnp.int32), jnp.zeros((tiles, 6), jnp.int32)],
        axis=1,
    )

    shard = joint_weight.shape[0]
    small_vectors = jnp.concatenate(
        [joint_bias, output_bias, first_gain, first_shift, second_gain, second_shift]
    )
    small_vectors = jnp.pad(small_vectors, (0, 256 - small_vectors.shape[0]))[None, :]
    vectors_all = gather_all(small_vectors)
    key_value = gather_all(joint_weight[:, width:])
    query_out = gather_all(jnp.concatenate([joint_weight[:, :width], output_weight], axis=1))
    query_weight = query_out[:, :width]
    out_weight = query_out[:, width:]
    bias_part = joint_bias.shape[0]
    joint_offset = vectors_all[:, :bias_part].reshape(1, -1).astype(F32)
    parts = [
        vectors_all[:, bias_part + i * shard : bias_part + (i + 1) * shard].reshape(-1).astype(F32)
        for i in range(5)
    ]
    vectors = jnp.stack(
        [parts[0], parts[1], parts[2], down_bias.astype(F32), parts[3], parts[4], parts[4], parts[4]]
    )
    up_other = other_half(up_weight)
    down_other = other_half(down_weight)
    bias_own = up_bias[None, :].astype(F32)
    bias_other = swap_mp(up_bias[None, :]).astype(F32)

    pair_maps = feature_maps.reshape(pairs, 2, head_size, feature_count)
    blank = jnp.zeros_like(pair_maps[:, 0])
    table = jnp.concatenate(
        [
            jnp.concatenate([pair_maps[:, 0], blank], axis=2),
            jnp.concatenate([blank, pair_maps[:, 1]], axis=2),
            jnp.concatenate([blank + 1, blank], axis=2),
            jnp.concatenate([blank, blank + 1], axis=2),
        ],
        axis=1,
    )
    own_rows = width // mp
    index = jnp.arange(own_rows, dtype=jnp.int32)
    source = index // shard * (shard * mp) + mp_rank * shard + index % shard
    select = (jnp.arange(width, dtype=jnp.int32)[:, None] == source[None, :]).astype(BF16)

    mass_rows = 16
    wide = pairs * 512
    table_spec = full((pairs, 256, 512))
    sm_rows = (SLOTS - 1) * width
    sm_mass = (SLOTS - 1) * mass_rows

    phi_k, values, scaled_k, moments, masses, small_moments, small_masses = call(
        keys_kernel,
        tiles,
        [rows(tile, width), full((width, 2 * width)), full((1, 2 * width)), table_spec, rows(tile, 128)],
        [
            (rows(tile, wide), (count, wide), BF16),
            (rows(tile, width), (count, width), BF16),
            (rows(tile, width), (count, width), BF16),
            (held((width, 256)), (width, 256), BF16),
            (held((mass_rows, 256)), (mass_rows, 256), F32),
            (held((sm_rows, 256)), (sm_rows, 256), BF16),
            (held((sm_mass, 256)), (sm_mass, 256), F32),
        ],
        [
            pltpu.VMEM((pairs, 128, 512), F32),
            pltpu.VMEM((pairs, 8, 512), F32),
            pltpu.VMEM((SLOTS - 1, pairs, 128, 512), F32),
            pltpu.VMEM((SLOTS - 1, pairs, 8, 512), F32),
        ],
        10e9,
    )(flags, tokens, key_value, joint_offset[:, width:], table, slots)

    def sum_tables(main, main_masses):
        pad = -(width + mass_rows) % (8 * dp)
        packed = jnp.concatenate(
            [main, main_masses.astype(BF16), jnp.zeros((pad, 256), BF16)], axis=0
        )
        packed = sum_dp(packed)
        return packed[:width], packed[width : width + mass_rows].astype(F32)

    moments, masses = sum_tables(moments, masses)

    phi_q, scaled_q, tokens_own = call(
        queries_kernel,
        tiles,
        [rows(tile, width), full((width, width)), full((1, width)), table_spec, full((width, own_rows))],
        [
            (rows(tile, wide), (count, wide), BF16),
            (rows(tile, width), (count, width), BF16),
            (rows(tile, own_rows), (count, own_rows), BF16),
        ],
        [],
        6e9,
    )(flags, tokens, query_weight, joint_offset[:, :width], table, select)

    moment_specs = [
        full((width, 256)),
        full((mass_rows, 256)),
        full((sm_rows, 256)),
        full((sm_mass, 256)),
    ]
    (
        layer_output, hidden_grad, normed, inverse, att, invden, active, dup, hidden_low, dffn, sums, up_sum,
    ) = call(
        middle_kernel,
        tiles,
        [rows(tile, width), rows(tile, width), rows(tile, 128), rows(tile, wide)]
        + moment_specs
        + [
            full((width, width)),
            full((width, half)),
            full((width, half)),
            full((half, width)),
            full((half, width)),
            full((1, half)),
            full((1, half)),
            full((8, width)),
        ],
        [
            (rows(tile, width), (count, width), BF16),
            (rows(tile, width), (count, width), F32),
            (rows(tile, width), (count, width), F32),
            (rows(tile, 128), (count, 128), F32),
            (rows(tile, width), (count, width), BF16),
            (rows(tile, width), (count, width), F32),
            (rows(tile, half), (count, half), BF16),
            (rows(tile, half), (count, half), BF16),
            (rows(tile, width), (count, width), BF16),
            (rows(tile, width), (count, width), BF16),
            (held((24, width)), (24, width), F32),
            (held((8, half)), (8, half), F32),
        ],
        [
            pltpu.VMEM((SLOTS, pairs, 256, 512), BF16),
            pltpu.VMEM((tile, pairs * 256), F32),
            pltpu.VMEM((tile, 2 * half), F32),
        ],
        30e9,
    )(
        flags, tokens, cotangent, slots, phi_q, moments, masses, small_moments, small_masses,
        out_weight, up_weight, up_other, down_weight, down_other, bias_own, bias_other, vectors,
    )

    down_grad = tn(active, dffn).astype(BF16)
    up_grad = tn(hidden_low, dup).astype(BF16)

    dfirst, dbranch, mixed, att_own, first_sums, dmoments, dmasses, small_dmoments, small_dmasses = call(
        attention_back_kernel,
        tiles,
        [
            rows(tile, width), rows(tile, width), rows(tile, 128), rows(tile, width), rows(tile, width),
            rows(tile, wide), rows(tile, 128), full((width, width)), full((1, width)), full((width, own_rows)),
        ],
        [
            (rows(tile, width), (count, width), F32),
            (rows(tile, width), (count, width), BF16),
            (rows(tile, 2 * width), (count, 2 * width), BF16),
            (rows(tile, own_rows), (count, own_rows), BF16),
            (held((24, width)), (24, width), F32),
            (held((width, 256)), (width, 256), BF16),
            (held((mass_rows, 256)), (mass_rows, 256), F32),
            (held((sm_rows, 256)), (sm_rows, 256), BF16),
            (held((sm_mass, 256)), (sm_mass, 256), F32),
        ],
        [
            pltpu.VMEM((pairs, 256, 512), F32),
            pltpu.VMEM((SLOTS - 1, pairs, 256, 512), F32),
        ],
        6e9,
    )(flags, hidden_grad, normed, inverse, att, invden, phi_q, slots, out_weight, vectors[1:2], select)

    dmoments, dmasses = sum_tables(dmoments, dmasses)

    dquery, partial_tokens, query_sums = call(
        queries_back_kernel,
        tiles,
        [rows(tile, 2 * width), rows(tile, wide), rows(tile, width), rows(tile, 128)]
        + moment_specs
        + [table_spec, full((width, width)), rows(tile, width)],
        [
            (rows(tile, width), (count, width), BF16),
            (rows(tile, width), (count, width), F32),
            (held((8, width)), (8, width), F32),
        ],
        [pltpu.VMEM((SLOTS, pairs, 256, 512), BF16), pltpu.VMEM((tile, 512), F32)],
        8e9,
    )(
        flags, mixed, phi_q, scaled_q, slots, moments, masses, small_moments, small_masses, table,
        query_weight, dfirst,
    )

    out_grad = tn(att_own, dbranch).astype(BF16)
    query_grad = tn(tokens_own, dquery).astype(BF16)

    dkey_value, tokens_grad, key_sums = call(
        keys_back_kernel,
        tiles,
        [rows(tile, wide), rows(tile, width), rows(tile, width), rows(tile, 128)]
        + moment_specs
        + [table_spec, full((width, 2 * width)), rows(tile, width)],
        [
            (rows(tile, 2 * width), (count, 2 * width), BF16),
            (rows(tile, width), (count, width), BF16),
            (held((8, 2 * width)), (8, 2 * width), F32),
        ],
        [
            pltpu.VMEM((SLOTS, pairs, 256, 512), BF16),
            pltpu.VMEM((tile, 512), F32),
            pltpu.VMEM((tile, 128), F32),
        ],
        12e9,
    )(
        flags, phi_k, values, scaled_k, slots, dmoments, dmasses, small_dmoments, small_dmasses, table,
        key_value, partial_tokens,
    )
    key_value_grad = tn(tokens_own, dkey_value).astype(BF16)

    down_total = sum_dp(down_grad)
    up_total = sum_dp(up_grad)
    small_sums = jnp.concatenate(
        [
            jnp.sum(query_sums, axis=0),
            jnp.sum(key_sums, axis=0),
            jnp.sum(first_sums.reshape(3, 8, width), axis=1).reshape(-1),
            jnp.sum(sums.reshape(3, 8, width), axis=1).reshape(-1),
            jnp.sum(up_sum, axis=0),
        ]
    )
    pad = -small_sums.shape[0] % (dp * 8 * 128)
    small_sums = sum_dp(jnp.pad(small_sums, (0, pad)).reshape(-1, 128)).reshape(-1)
    attention_total = scatter_sum(
        jnp.concatenate([query_grad, key_value_grad, out_grad], axis=1)
    ).astype(F32)

    def owned(start, size):
        part = size // (dp * mp)
        return lax.dynamic_slice_in_dim(small_sums, start + (rank * mp + mp_rank) * part, part, 0)

    return (
        layer_output,
        tokens_grad,
        attention_total[:, : 3 * width],
        owned(0, 3 * width),
        attention_total[:, 3 * width :],
        owned(5 * width, width),
        owned(3 * width, width),
        owned(4 * width, width),
        up_total.astype(F32),
        small_sums[9 * width : 9 * width + half],
        down_total.astype(F32),
        small_sums[8 * width : 9 * width],
        owned(6 * width, width),
        owned(7 * width, width),
    )


def solution(mesh):
    shared = P(("dp", "mp"))
    in_specs = (
        P("dp", None), P(), P(), P(("dp", "mp"), None), shared, P(("dp", "mp"), None), shared, shared,
        shared, P(None, "mp"), P("mp"), P("mp", None), P(), shared, shared, P("dp", None),
    )
    out_specs = (
        P("dp", None), P("dp", None), P(("dp", "mp"), None), shared, P(("dp", "mp"), None), shared,
        shared, shared, P(None, "mp"), P("mp"), P("mp", None), P(), shared, shared,
    )
    return jax.shard_map(local, mesh=mesh, in_specs=in_specs, out_specs=out_specs, check_vma=False)
```

```python
from functools import partial
import math

import jax
import jax.numpy as jnp
from jax import lax
from jax.experimental import pallas as pl
from jax.experimental.pallas import tpu as pltpu
from jax.sharding import PartitionSpec as P

EPSILON = 1e-05
F32 = jnp.float32
BF16 = jnp.bfloat16
LOG2E = math.log2(math.e)
VMEM_LIMIT = 56 * 1024 * 1024
SLOTS = 8
SUB = 64


def nn(a, b):
    return lax.dot_general(a, b, (((1,), (0,)), ((), ())), preferred_element_type=F32)


def nt(a, b):
    return lax.dot_general(a, b, (((1,), (1,)), ((), ())), preferred_element_type=F32)


def tn(a, b):
    return lax.dot_general(a, b, (((0,), (0,)), ((), ())), preferred_element_type=F32)


def fold_rows(a):
    return jnp.sum(a.reshape(a.shape[0] // 8, 8, a.shape[1]), axis=0)


def after(value, *deps):
    return lax.optimization_barrier((value, deps))[0]


def dp_bits():
    count = lax.axis_size("dp")
    bits = []
    bit = count // 2
    while bit:
        bits.append(bit)
        bit //= 2
    return bits


def far_first():
    return dp_bits()


def near_first():
    bits = dp_bits()
    if len(bits) < 3:
        return bits
    return [bits[-2]] + bits[:-2] + [bits[-1]]


def swap_dp(a, bit):
    count = lax.axis_size("dp")
    return lax.ppermute(a, "dp", [(i, i ^ bit) for i in range(count)])


def swap_mp(a):
    return lax.ppermute(a, "mp", [(0, 1), (1, 0)])


def mine(bit):
    return (lax.axis_index("dp") // bit) % 2


def join_pair(own, other, bit, axis):
    low = jnp.stack([own, other], axis)
    high = jnp.stack([other, own], axis)
    return jnp.where(bit == 0, low, high)


class Gather:
    def __init__(self, a, order):
        self.a = a
        self.tail = a.shape
        self.order = list(order)
        self.done = []
        self.got = None

    def start(self, *deps):
        if deps:
            self.a = after(self.a, *deps)
        self.got = swap_dp(self.a, self.order[0])
        return self

    def finish(self, *deps):
        bit = self.order.pop(0)
        got = after(self.got, *deps) if deps else self.got
        place = sum(1 for d in self.done if d > bit)
        self.a = join_pair(self.a, got, mine(bit), place)
        self.done.append(bit)
        return self

    def rest(self):
        while self.order:
            self.start().finish()
        return self.result()

    def result(self):
        return self.a.reshape((-1,) + self.tail[1:])


class Scatter:
    def __init__(self, a, order):
        count = lax.axis_size("dp")
        self.left = dp_bits()
        self.a = a.reshape((2,) * len(self.left) + (a.shape[0] // count,) + a.shape[1:])
        self.order = list(order)

    def start(self, *deps):
        bit = self.order[0]
        axis = self.left.index(bit)
        a = after(self.a, *deps) if deps else self.a
        self.own = lax.dynamic_index_in_dim(a, mine(bit), axis, False)
        self.got = swap_dp(lax.dynamic_index_in_dim(a, 1 - mine(bit), axis, False), bit)
        return self

    def finish(self, *deps):
        self.left.remove(self.order.pop(0))
        got = after(self.got, *deps) if deps else self.got
        self.a = (self.own.astype(F32) + got.astype(F32)).astype(self.a.dtype)
        return self

    def rest(self):
        while self.order:
            self.start().finish()
        return self.a


def sum_tables(packed):
    bits = dp_bits()
    core = mine(1)
    halves = packed.reshape(2, packed.shape[0] // 2, packed.shape[1])
    own = lax.dynamic_index_in_dim(halves, core, 0, False)
    got = swap_dp(lax.dynamic_index_in_dim(halves, 1 - core, 0, False), 1)
    a = (own.astype(F32) + got.astype(F32)).astype(packed.dtype)
    for bit in reversed(bits[:-1]):
        got = swap_dp(a, bit)
        a = (a.astype(F32) + got.astype(F32)).astype(packed.dtype)
    return join_pair(a, swap_dp(a, 1), core, 0).reshape(packed.shape)


def sum_small(a, *deps):
    for bit in reversed(dp_bits()):
        a = a + swap_dp(a, bit)
    return a


def full(shape):
    return pl.BlockSpec(shape, lambda t, *_: (0,) * len(shape), pipeline_mode=pl.Buffered(1))


def rows(tile, width):
    return pl.BlockSpec((tile, width), lambda t, *_: (t, 0))


def held(shape):
    return pl.BlockSpec(shape, lambda t, *_: (0,) * len(shape))


def call(kernel, tiles, in_specs, outs, scratch, flops):
    return pl.pallas_call(
        kernel,
        grid_spec=pltpu.PrefetchScalarGridSpec(
            num_scalar_prefetch=1,
            grid=(tiles,),
            in_specs=in_specs,
            out_specs=[spec for spec, _, _ in outs],
            scratch_shapes=scratch,
        ),
        out_shape=[jax.ShapeDtypeStruct(shape, kind) for _, shape, kind in outs],
        compiler_params=pltpu.CompilerParams(
            vmem_limit_bytes=VMEM_LIMIT, dimension_semantics=("arbitrary",)
        ),
        cost_estimate=pl.CostEstimate(flops=int(flops), bytes_accessed=20_000_000, transcendentals=0),
    )


def features(scaled, table):
    lhs = jnp.concatenate([scaled.astype(BF16), (-0.5 * scaled * scaled).astype(BF16)], axis=1)
    return jnp.exp2(nn(lhs, table) * LOG2E - 4.0)


def each_small(flags, t, subs, body):
    def block(i, carry):
        line = t * subs + i

        @pl.when(flags[line, 8] > 0)
        def _():
            def one(j, carry):
                @pl.when(flags[line, j] > 0)
                def _():
                    body(pl.ds(pl.multiple_of(i * SUB, SUB), SUB), j)

                return carry

            lax.fori_loop(1, SLOTS, one, 0)

        return carry

    lax.fori_loop(0, subs, block, 0)


def pack_tables(table, base, acc, macc):
    pairs = acc.shape[0]
    masses = []
    for p in range(pairs):
        for k in range(2):
            head = 2 * p + k
            span = slice(k * 256, (k + 1) * 256)
            table[pl.ds(base + head * 64, 64), :] = acc[p, k * 64 : (k + 1) * 64, span].astype(BF16)
            source = macc[p, :, span] if macc is not None else acc[p, 128 + k * 64 : 192 + k * 64, span]
            masses.append(jnp.sum(source, axis=0, keepdims=True))
    masses.append(jnp.zeros((16 - 2 * pairs, 256), F32))
    table[pl.ds(base + pairs * 128, 16), :] = jnp.concatenate(masses, axis=0).astype(BF16)


def fill_tables(tabs, main, repeat):
    pairs = tabs.shape[0]
    tabs[...] = jnp.zeros_like(tabs)
    masses = main[pl.ds(pairs * 128, 16), :].astype(F32)
    for p in range(pairs):
        for k in range(2):
            head = 2 * p + k
            span = slice(k * 256, (k + 1) * 256)
            tabs[p, k * 64 : (k + 1) * 64, span] = main[pl.ds(head * 64, 64), :]
            mass = jnp.broadcast_to(masses[head : head + 1, :], (64, 256))
            if not repeat:
                mass = jnp.where(lax.broadcasted_iota(jnp.int32, (64, 256), 0) == 0, mass, 0.0)
            tabs[p, 128 + k * 64 : 192 + k * 64, span] = mass.astype(BF16)


def small_table(small, j, p, pairs, repeat, with_masses=True):
    stride = pairs * 128 + 16
    base = (j - 1) * stride
    zero = jnp.zeros((64, 256), BF16)
    tops, bottoms = [], []
    if with_masses:
        masses = small[pl.ds(pl.multiple_of(base + pairs * 128, 16), 16), :].astype(F32)
    for k in range(2):
        head = 2 * p + k
        top = small[pl.ds(pl.multiple_of(base + head * 64, 16), 64), :]
        tops.append(jnp.concatenate([top, zero] if k == 0 else [zero, top], axis=1))
        if with_masses:
            mass = jnp.broadcast_to(masses[head : head + 1, :], (64, 256))
            if not repeat:
                mass = jnp.where(lax.broadcasted_iota(jnp.int32, (64, 256), 0) == 0, mass, 0.0)
            mass = mass.astype(BF16)
            bottoms.append(jnp.concatenate([mass, zero] if k == 0 else [zero, mass], axis=1))
    return jnp.concatenate(tops + bottoms, axis=0)


def masked(mask, value):
    wide = jnp.concatenate([mask] * (value.shape[1] // 128), axis=1)
    return jnp.where(wide, value.astype(F32), 0.0)


def keys_kernel(
    flags, x, key_weight, value_weight, bias, table, slot,
    phi, values, scaled_out, main, small,
    acc, macc, sacc, smacc,
):
    t = pl.program_id(0)
    pairs = table.shape[0]
    width = pairs * 128
    subs = x.shape[0] // SUB
    slow = flags[t * subs, 10] == 0

    @pl.when(t == 0)
    def _():
        acc[...] = jnp.zeros_like(acc)
        macc[...] = jnp.zeros_like(macc)

        for j in range(1, SLOTS):

            @pl.when(flags[j, 11] > 0)
            def _():
                sacc[j - 1] = jnp.zeros_like(sacc[j - 1])
                smacc[j - 1] = jnp.zeros_like(smacc[j - 1])

    keys = nn(x[...], key_weight[:, :width]) + bias[:, :width]
    values[...] = (nn(x[...], value_weight[...]) + bias[:, width:]).astype(BF16)
    for p in range(pairs):
        scaled = keys[:, p * 128 : (p + 1) * 128] * 64 ** (-0.25)
        scaled_out[:, p * 128 : (p + 1) * 128] = scaled.astype(BF16)
        phi[:, p * 512 : (p + 1) * 512] = features(scaled, table[p]).astype(BF16)

    @pl.when(jnp.logical_not(slow))
    def _():
        for p in range(pairs):
            part = phi[:, p * 512 : (p + 1) * 512]
            acc[p] += tn(values[:, p * 128 : (p + 1) * 128], part)
            macc[p] += fold_rows(part.astype(F32))

    @pl.when(slow)
    def _():
        mask = slot[...] == 0
        for p in range(pairs):
            part = phi[:, p * 512 : (p + 1) * 512]
            acc[p] += tn(masked(mask, values[:, p * 128 : (p + 1) * 128]).astype(BF16), part)
            macc[p] += fold_rows(masked(mask, part))

        def body(rows, j):
            mask = slot[rows, :] == j
            for p in range(pairs):
                part = phi[rows, p * 512 : (p + 1) * 512]
                value = masked(mask, values[rows, p * 128 : (p + 1) * 128]).astype(BF16)
                sacc[j - 1, p] += tn(value, part)
                smacc[j - 1, p] += fold_rows(masked(mask, part))

        each_small(flags, t, subs, body)

    @pl.when(t == pl.num_programs(0) - 1)
    def _():
        pack_tables(main, 0, acc, macc)

        for j in range(1, SLOTS):

            @pl.when(flags[j, 11] > 0)
            def _():
                pack_tables(small, (j - 1) * main.shape[0], sacc.at[j - 1], smacc.at[j - 1])


def queries_kernel(flags, x, weight, bias, table, select, phi, scaled_out, chosen):
    pairs = table.shape[0]
    query = nn(x[...], weight[...]) + bias[...]
    chosen[...] = nn(x[...], select[...]).astype(BF16)
    for p in range(pairs):
        scaled = query[:, p * 128 : (p + 1) * 128] * 64 ** (-0.25)
        scaled_out[:, p * 128 : (p + 1) * 128] = scaled.astype(BF16)
        phi[:, p * 512 : (p + 1) * 512] = features(scaled, table[p]).astype(BF16)


def center(z):
    average = jnp.mean(z, axis=1, keepdims=True)
    centered = z - average
    inverse = lax.rsqrt(jnp.mean(centered * centered, axis=1, keepdims=True) + EPSILON)
    return centered * inverse, inverse


def center_back(e, normed, inverse):
    first = jnp.mean(e, axis=1, keepdims=True)
    second = jnp.mean(e * normed, axis=1, keepdims=True)
    return inverse * (e - first - normed * second)


def middle_kernel(
    flags, x, cot, slot, phi, main, small,
    out_weight, up_own, up_other, down_own, down_other, bias_own, bias_other, vectors,
    layer_out, hidden_grad, normed_out, inverse_out, att_out, invden_out,
    active_out, dup_out, hidden_out, dffn_out, sums, up_sum,
    tabs, spread, gates,
):
    t = pl.program_id(0)
    pairs = tabs.shape[0]
    width = pairs * 128
    subs = x.shape[0] // SUB

    @pl.when(t == 0)
    def _():
        fill_tables(tabs, main, True)
        sums[...] = jnp.zeros_like(sums)
        up_sum[...] = jnp.zeros_like(up_sum)

    for p in range(pairs):
        spread[:, p * 256 : (p + 1) * 256] = nt(phi[:, p * 512 : (p + 1) * 512], tabs[p])

    @pl.when(flags[t * subs, 10] == 0)
    def _():
        def body(rows, j):
            mask = slot[rows, :] == j
            wide = jnp.concatenate([mask] * 2, axis=1)
            for p in range(pairs):
                got = nt(phi[rows, p * 512 : (p + 1) * 512], small_table(small, j, p, pairs, True))
                old = spread[rows, p * 256 : (p + 1) * 256]
                spread[rows, p * 256 : (p + 1) * 256] = jnp.where(wide, got, old)

        each_small(flags, t, subs, body)

    live = slot[...] < SLOTS
    for p in range(pairs):
        numerator = spread[:, p * 256 : p * 256 + 128]
        denominator = spread[:, p * 256 + 128 : (p + 1) * 256]
        inverse = jnp.where(live, 1.0 / jnp.where(live, denominator, 1.0), 0.0)
        invden_out[:, p * 128 : (p + 1) * 128] = inverse
        att_out[:, p * 128 : (p + 1) * 128] = (numerator * inverse).astype(BF16)

    def vector(i):
        return vectors[i : i + 1, :]

    branch = nn(att_out[...], out_weight[...]) + vector(0)
    first, first_inverse = center(x[...].astype(F32) + branch)
    normed_out[...] = first
    inverse_out[...] = jnp.broadcast_to(first_inverse, inverse_out.shape)
    hidden = first * vector(1) + vector(2)
    hidden_low = hidden.astype(BF16)
    hidden_out[...] = hidden_low
    step = 512
    half = up_own.shape[1]
    chunks = [(up_own, down_own, bias_own, 0, c, c) for c in range(0, half, step)]
    chunks += [(up_other, down_other, bias_other, 1, c, half + c) for c in range(0, half, step)]
    total = hidden + vector(3)
    other_active = []
    for up, down, bias, which, c, place in chunks:
        value = nn(hidden_low, up[:, c : c + step]) + bias[:, c : c + step]
        cdf = 0.5 + 0.5 * lax.erf(value * math.sqrt(0.5))
        gates[:, place : place + step] = cdf + value * jnp.exp2(
            value * value * (-0.5 * LOG2E)
        ) * (1.0 / math.sqrt(2.0 * math.pi))
        active = (value * cdf).astype(BF16)
        if which == 0:
            active_out[:, c : c + step] = active
        total = total + nn(active, down[c : c + step, :])
    second, second_inverse = center(total)
    layer_out[...] = (second * vector(4) + vector(5)).astype(BF16)
    g = cot[...].astype(F32)
    sums[0:8, :] += fold_rows(g * second)
    sums[8:16, :] += fold_rows(g)
    dsecond = center_back(g * vector(4), second, second_inverse)
    dffn = dsecond.astype(BF16)
    dffn_out[...] = dffn
    sums[16:24, :] += fold_rows(dffn.astype(F32))
    for up, down, bias, which, c, place in chunks:
        dup = (nt(dffn, down[c : c + step, :]) * gates[:, place : place + step]).astype(BF16)
        if which == 0:
            dup_out[:, c : c + step] = dup
            up_sum[:, c : c + step] += fold_rows(dup.astype(F32))
        dsecond = dsecond + nt(dup, up[:, c : c + step])
    hidden_grad[...] = dsecond


def attention_back_kernel(
    flags, hidden_grad, normed, inverse, att, invden, phi, slot, out_weight, gain, select,
    dfirst_out, dbranch_out, mixed, chosen, sums, main, small,
    acc, sacc,
):
    t = pl.program_id(0)
    pairs = acc.shape[0]
    subs = att.shape[0] // SUB
    slow = flags[t * subs, 10] == 0

    @pl.when(t == 0)
    def _():
        acc[...] = jnp.zeros_like(acc)
        sums[...] = jnp.zeros_like(sums)

        for j in range(1, SLOTS):

            @pl.when(flags[j, 11] > 0)
            def _():
                sacc[j - 1] = jnp.zeros_like(sacc[j - 1])

    grad = hidden_grad[...]
    first = normed[...]
    sums[0:8, :] += fold_rows(grad * first)
    sums[8:16, :] += fold_rows(grad)
    dfirst = center_back(grad * gain[...], first, inverse[:, 0:1])
    dfirst_out[...] = dfirst
    dbranch = dfirst.astype(BF16)
    dbranch_out[...] = dbranch
    sums[16:24, :] += fold_rows(dbranch.astype(F32))
    chosen[...] = nn(att[...], select[...]).astype(BF16)
    datt = nt(dbranch, out_weight[...])
    ratio = datt * invden[...]
    dden = -ratio * att[...].astype(F32)
    for p in range(pairs):
        mixed[:, p * 256 : p * 256 + 128] = ratio[:, p * 128 : (p + 1) * 128].astype(BF16)
        mixed[:, p * 256 + 128 : (p + 1) * 256] = dden[:, p * 128 : (p + 1) * 128].astype(BF16)

    @pl.when(jnp.logical_not(slow))
    def _():
        for p in range(pairs):
            acc[p] += tn(mixed[:, p * 256 : (p + 1) * 256], phi[:, p * 512 : (p + 1) * 512])

    @pl.when(slow)
    def _():
        mask = slot[...] == 0
        for p in range(pairs):
            part = masked(mask, mixed[:, p * 256 : (p + 1) * 256]).astype(BF16)
            acc[p] += tn(part, phi[:, p * 512 : (p + 1) * 512])

        def body(rows, j):
            mask = slot[rows, :] == j
            for p in range(pairs):
                part = masked(mask, mixed[rows, p * 256 : (p + 1) * 256]).astype(BF16)
                sacc[j - 1, p] += tn(part, phi[rows, p * 512 : (p + 1) * 512])

        each_small(flags, t, subs, body)

    @pl.when(t == pl.num_programs(0) - 1)
    def _():
        pack_tables(main, 0, acc, None)

        for j in range(1, SLOTS):

            @pl.when(flags[j, 11] > 0)
            def _():
                pack_tables(small, (j - 1) * main.shape[0], sacc.at[j - 1], None)


def each_mixed_block(flags, t, subs, body):
    def block(i, carry):
        line = t * subs + i

        @pl.when(flags[line, 8] > 0)
        def _():
            body(pl.ds(pl.multiple_of(i * SUB, SUB), SUB), line)

        return carry

    lax.fori_loop(0, subs, block, 0)


def each_slot(flags, line, body):
    def one(j, carry):
        @pl.when(flags[line, j] > 0)
        def _():
            body(j)

        return carry

    lax.fori_loop(1, SLOTS, one, 0)


def feature_back(rows, p, grad, phi, scaled, table, out):
    span = slice(p * 128, (p + 1) * 128)
    e = (grad * phi[rows, p * 512 : (p + 1) * 512].astype(F32)).astype(BF16)
    back = nt(e, table[p])
    du = (back[:, :128] - scaled[rows, span].astype(F32) * back[:, 128:]) * 64 ** (-0.25)
    out[rows, span] = du.astype(BF16)


def queries_back_kernel(
    flags, mixed, phi, scaled, slot, main, small, table, weight, dfirst,
    dquery_out, partial_out, sums, tabs, work,
):
    t = pl.program_id(0)
    pairs = tabs.shape[0]
    subs = phi.shape[0] // SUB

    @pl.when(t == 0)
    def _():
        fill_tables(tabs, main, True)
        sums[...] = jnp.zeros_like(sums)

    everything = slice(None)
    for p in range(pairs):
        grad = nn(mixed[:, p * 256 : (p + 1) * 256], tabs[p])
        feature_back(everything, p, grad, phi, scaled, table, dquery_out)

    @pl.when(flags[t * subs, 10] == 0)
    def _():
        def body(rows, line):
            places = slot[rows, :]
            for p in range(pairs):
                part = mixed[rows, p * 256 : (p + 1) * 256]
                work[:, p * 512 : (p + 1) * 512] = nn(masked(places == 0, part).astype(BF16), tabs[p])

            def one(j):
                for p in range(pairs):
                    part = mixed[rows, p * 256 : (p + 1) * 256]
                    work[:, p * 512 : (p + 1) * 512] += nn(
                        masked(places == j, part).astype(BF16), small_table(small, j, p, pairs, True)
                    )

            each_slot(flags, line, one)
            for p in range(pairs):
                grad = work[:, p * 512 : (p + 1) * 512]
                feature_back(rows, p, grad, phi, scaled, table, dquery_out)

        each_mixed_block(flags, t, subs, body)

    sums[...] += fold_rows(dquery_out[...].astype(F32))
    partial_out[...] = dfirst[...] + nt(dquery_out[...], weight[...])


def keys_back_kernel(
    flags, phi, values, scaled, slot, main, small, table, key_weight, value_weight, partial_in,
    djoint_out, tokens_out, sums, tabs, work, vwork,
):
    t = pl.program_id(0)
    pairs = tabs.shape[0]
    width = pairs * 128
    subs = phi.shape[0] // SUB

    @pl.when(t == 0)
    def _():
        fill_tables(tabs, main, False)
        sums[...] = jnp.zeros_like(sums)

    def extended(rows, p):
        value = values[rows, p * 128 : (p + 1) * 128]
        return jnp.concatenate([value, jnp.ones_like(value)], axis=1)

    everything = slice(None)
    for p in range(pairs):
        grad = nn(extended(everything, p), tabs[p])
        feature_back(everything, p, grad, phi, scaled, table, djoint_out)
        dvalue = nt(phi[:, p * 512 : (p + 1) * 512], tabs[p, :128, :])
        djoint_out[:, width + p * 128 : width + (p + 1) * 128] = dvalue.astype(BF16)

    @pl.when(flags[t * subs, 10] == 0)
    def _():
        def body(rows, line):
            places = slot[rows, :]
            for p in range(pairs):
                part = extended(rows, p)
                features_part = phi[rows, p * 512 : (p + 1) * 512]
                work[:, p * 512 : (p + 1) * 512] = nn(masked(places == 0, part).astype(BF16), tabs[p])
                vwork[:, p * 128 : (p + 1) * 128] = masked(
                    places == 0, nt(features_part, tabs[p, :128, :])
                )

            def one(j):
                for p in range(pairs):
                    part = extended(rows, p)
                    features_part = phi[rows, p * 512 : (p + 1) * 512]
                    own = small_table(small, j, p, pairs, False)
                    work[:, p * 512 : (p + 1) * 512] += nn(masked(places == j, part).astype(BF16), own)
                    vwork[:, p * 128 : (p + 1) * 128] += masked(
                        places == j, nt(features_part, own[:128, :])
                    )

            each_slot(flags, line, one)
            for p in range(pairs):
                grad = work[:, p * 512 : (p + 1) * 512]
                feature_back(rows, p, grad, phi, scaled, table, djoint_out)
            djoint_out[rows, width:] = vwork[...].astype(BF16)

        each_mixed_block(flags, t, subs, body)

    sums[...] += fold_rows(djoint_out[...].astype(F32))
    tokens_out[...] = (
        partial_in[...]
        + nt(djoint_out[:, :width], key_weight[:, :width])
        + nt(djoint_out[:, width:], value_weight[...])
    ).astype(BF16)


def local(
    tokens, document_lengths, feature_maps, joint_weight, joint_bias, output_weight, output_bias,
    first_gain, first_shift, up_weight, up_bias, down_weight, down_bias, second_gain, second_shift,
    cotangent,
):
    count, width = tokens.shape
    heads, head_size, feature_count = feature_maps.shape
    pairs = heads // 2
    half = up_weight.shape[1]
    tile = 256
    tiles = count // tile
    rank = lax.axis_index("dp")
    dp = lax.axis_size("dp")
    mp = lax.axis_size("mp")
    mp_rank = lax.axis_index("mp")

    lengths = document_lengths[0]
    ends = jnp.cumsum(lengths)
    place = rank * count + jnp.arange(count, dtype=jnp.int32)
    document = jnp.sum((ends[None, :] <= place[:, None]).astype(jnp.int32), axis=1)
    longest = jnp.argmax(lengths).astype(jnp.int32)
    slot = jnp.where(
        document == longest,
        0,
        jnp.where(document >= SLOTS, SLOTS, jnp.where(document < longest, document + 1, document)),
    )
    slots = jnp.broadcast_to(slot[:, None], (count, 128))
    blocks = count // SUB
    present = jnp.max(
        (slot.reshape(blocks, SUB)[:, :, None] == jnp.arange(SLOTS)[None, None, :]).astype(jnp.int32),
        axis=1,
    )
    mixed_block = jnp.max(slot.reshape(blocks, SUB), axis=1, keepdims=True) > 0
    mixed_any = jnp.broadcast_to(jnp.max(slot) > 0, (blocks, 1))
    mixed_tile = jnp.repeat(jnp.max(slot.reshape(tiles, tile), axis=1) > 0, tile // SUB)[:, None]
    flags = jnp.concatenate(
        [
            present,
            mixed_block.astype(jnp.int32),
            mixed_any.astype(jnp.int32),
            1 - mixed_tile.astype(jnp.int32),
            jnp.pad(jnp.max(present, axis=0), (0, blocks - SLOTS))[:, None],
            jnp.zeros((blocks, 4), jnp.int32),
        ],
        axis=1,
    )

    shard = joint_weight.shape[0]
    small_vectors = jnp.concatenate(
        [joint_bias, output_bias, first_gain, first_shift, second_gain, second_shift]
    ).reshape(shard, -1)
    per_row = small_vectors.shape[1]
    small_vectors = jnp.pad(small_vectors, ((0, 0), (0, 128 - per_row)))
    shards = jnp.concatenate([joint_weight, output_weight, small_vectors], axis=1)
    shards = join_pair(shards, swap_mp(shards), mp_rank, 0).reshape(2 * shard, -1)
    key_chain = Gather(
        jnp.concatenate([shards[:, width : 2 * width], shards[:, 4 * width :]], axis=1), far_first()
    )
    value_chain = Gather(shards[:, 2 * width : 3 * width], near_first())
    query_chain = Gather(shards[:, :width], far_first())
    out_chain = Gather(shards[:, 3 * width : 4 * width], near_first())

    core = mine(1)

    def own_part(a):
        return lax.dynamic_slice_in_dim(a, core * (a.shape[0] // 2), a.shape[0] // 2, 0)

    while key_chain.order:
        key_chain.start()
        value_chain.start()
        if len(key_chain.order) == len(dp_bits()):
            up_part = swap_mp(after(own_part(up_weight), shards))
            down_part = swap_mp(after(own_part(down_weight), up_part))
        key_chain.finish()
        value_chain.finish()
        if len(key_chain.order) == 1:
            query_chain.start(key_chain.a, value_chain.a)
            out_chain.start(key_chain.a, value_chain.a)
    key_weight = key_chain.result()
    value_weight = value_chain.result()

    vectors_all = key_weight[:, width : width + per_row].reshape(dp * mp, -1)
    bias_part = joint_bias.shape[0]
    joint_offset = vectors_all[:, :bias_part].reshape(1, -1).astype(F32)
    parts = [
        vectors_all[:, bias_part + i * shard : bias_part + (i + 1) * shard].reshape(-1).astype(F32)
        for i in range(5)
    ]
    vectors = jnp.stack(
        [parts[0], parts[1], parts[2], down_bias.astype(F32), parts[3], parts[4], parts[4], parts[4]]
    )
    bias_own = up_bias[None, :].astype(F32)

    pair_maps = feature_maps.reshape(pairs, 2, head_size, feature_count)
    blank = jnp.zeros_like(pair_maps[:, 0])
    table = jnp.concatenate(
        [
            jnp.concatenate([pair_maps[:, 0], blank], axis=2),
            jnp.concatenate([blank, pair_maps[:, 1]], axis=2),
            jnp.concatenate([blank + 1, blank], axis=2),
            jnp.concatenate([blank, blank + 1], axis=2),
        ],
        axis=1,
    )
    own_rows = width // mp
    index = jnp.arange(own_rows, dtype=jnp.int32)
    source = index // shard * (shard * mp) + mp_rank * shard + index % shard
    select = (jnp.arange(width, dtype=jnp.int32)[:, None] == source[None, :]).astype(BF16)

    wide = pairs * 512
    table_spec = full((pairs, 256, 512))
    table_rows = width + 16
    small_rows = (SLOTS - 1) * table_rows
    table_outs = [
        (held((table_rows, 256)), (table_rows, 256), BF16),
        (held((small_rows, 256)), (small_rows, 256), BF16),
    ]
    moment_specs = [full((table_rows, 256)), full((small_rows, 256))]
    tabs_scratch = pltpu.VMEM((pairs, 256, 512), BF16)

    phi_k, values, scaled_k, moments, small_moments = call(
        keys_kernel,
        tiles,
        [
            rows(tile, width), full(key_weight.shape), full((width, width)), full((1, 2 * width)),
            table_spec, rows(tile, 128),
        ],
        [
            (rows(tile, wide), (count, wide), BF16),
            (rows(tile, width), (count, width), BF16),
            (rows(tile, width), (count, width), BF16),
        ]
        + table_outs,
        [
            pltpu.VMEM((pairs, 128, 512), F32),
            pltpu.VMEM((pairs, 8, 512), F32),
            pltpu.VMEM((SLOTS - 1, pairs, 128, 512), F32),
            pltpu.VMEM((SLOTS - 1, pairs, 8, 512), F32),
        ],
        10e9,
    )(flags, tokens, key_weight, value_weight, joint_offset[:, width:], table, slots)

    query_chain.finish(moments)
    out_chain.finish(moments)
    moments = sum_tables(moments)
    query_weight = query_chain.rest()
    out_weight = out_chain.rest()
    bias_other = swap_mp(up_bias[None, :]).astype(F32)
    up_other = join_pair(up_part, swap_dp(up_part, 1), core, 0).reshape(up_weight.shape)
    down_other = join_pair(down_part, swap_dp(down_part, 1), core, 0).reshape(down_weight.shape)

    phi_q, scaled_q, tokens_own = call(
        queries_kernel,
        tiles,
        [rows(tile, width), full((width, width)), full((1, width)), table_spec, full((width, own_rows))],
        [
            (rows(tile, wide), (count, wide), BF16),
            (rows(tile, width), (count, width), BF16),
            (rows(tile, own_rows), (count, own_rows), BF16),
        ],
        [],
        6e9,
    )(flags, tokens, query_weight, joint_offset[:, :width], table, select)

    (
        layer_output, hidden_grad, normed, inverse, att, invden, active, dup, hidden_low, dffn, sums, up_sum,
    ) = call(
        middle_kernel,
        tiles,
        [rows(tile, width), rows(tile, width), rows(tile, 128), rows(tile, wide)]
        + moment_specs
        + [
            full((width, width)),
            full((width, half)),
            full((width, half)),
            full((half, width)),
            full((half, width)),
            full((1, half)),
            full((1, half)),
            full((8, width)),
        ],
        [
            (rows(tile, width), (count, width), BF16),
            (rows(tile, width), (count, width), F32),
            (rows(tile, width), (count, width), F32),
            (rows(tile, 128), (count, 128), F32),
            (rows(tile, width), (count, width), BF16),
            (rows(tile, width), (count, width), F32),
            (rows(tile, half), (count, half), BF16),
            (rows(tile, half), (count, half), BF16),
            (rows(tile, width), (count, width), BF16),
            (rows(tile, width), (count, width), BF16),
            (held((24, width)), (24, width), F32),
            (held((8, half)), (8, half), F32),
        ],
        [tabs_scratch, pltpu.VMEM((tile, pairs * 256), F32), pltpu.VMEM((tile, 2 * half), F32)],
        30e9,
    )(
        flags, tokens, cotangent, slots, phi_q, moments, small_moments,
        out_weight, up_weight, up_other, down_weight, down_other, bias_own, bias_other, vectors,
    )

    down_grad = tn(active, dffn).astype(BF16)
    down_chain = Scatter(down_grad, reversed(dp_bits())).start()
    up_grad = tn(after(hidden_low, down_grad), dup).astype(BF16)
    up_order = dp_bits()
    up_order = up_order[-1:] + up_order[-3:-2] + up_order[:-3] + up_order[-2:-1]
    up_chain = Scatter(up_grad, up_order).start()
    down_chain.finish(up_grad).start()

    dfirst, dbranch, mixed, att_own, first_sums, dmoments, small_dmoments = call(
        attention_back_kernel,
        tiles,
        [
            rows(tile, width), rows(tile, width), rows(tile, 128), rows(tile, width), rows(tile, width),
            rows(tile, wide), rows(tile, 128), full((width, width)), full((1, width)), full((width, own_rows)),
        ],
        [
            (rows(tile, width), (count, width), F32),
            (rows(tile, width), (count, width), BF16),
            (rows(tile, 2 * width), (count, 2 * width), BF16),
            (rows(tile, own_rows), (count, own_rows), BF16),
            (held((24, width)), (24, width), F32),
        ]
        + table_outs,
        [
            pltpu.VMEM((pairs, 256, 512), F32),
            pltpu.VMEM((SLOTS - 1, pairs, 256, 512), F32),
        ],
        6e9,
    )(
        flags, after(hidden_grad, down_chain.a), normed, inverse, att, invden, phi_q, slots, out_weight,
        vectors[1:2], select,
    )

    dmoments = sum_tables(dmoments)
    up_chain.finish(dbranch).start()
    down_chain.finish(dbranch).start()

    dquery, partial_tokens, query_sums = call(
        queries_back_kernel,
        tiles,
        [rows(tile, 2 * width), rows(tile, wide), rows(tile, width), rows(tile, 128)]
        + moment_specs
        + [table_spec, full((width, width)), rows(tile, width)],
        [
            (rows(tile, width), (count, width), BF16),
            (rows(tile, width), (count, width), F32),
            (held((8, width)), (8, width), F32),
        ],
        [tabs_scratch, pltpu.VMEM((SUB, wide), F32)],
        8e9,
    )(
        flags, mixed, phi_q, scaled_q, slots, moments, small_moments, table, query_weight,
        after(dfirst, up_chain.a, down_chain.a),
    )

    up_chain.finish(dquery).start()
    down_chain.finish(dquery).start()
    out_grad = tn(att_own, dbranch).astype(BF16)
    query_grad = tn(tokens_own, dquery).astype(BF16)

    dkey_value, tokens_grad, key_sums = call(
        keys_back_kernel,
        tiles,
        [rows(tile, wide), rows(tile, width), rows(tile, width), rows(tile, 128)]
        + moment_specs
        + [table_spec, full(key_weight.shape), full((width, width)), rows(tile, width)],
        [
            (rows(tile, 2 * width), (count, 2 * width), BF16),
            (rows(tile, width), (count, width), BF16),
            (held((8, 2 * width)), (8, 2 * width), F32),
        ],
        [tabs_scratch, pltpu.VMEM((SUB, wide), F32), pltpu.VMEM((SUB, width), F32)],
        12e9,
    )(
        flags, phi_k, values, scaled_k, slots, dmoments, small_dmoments, table,
        key_weight, value_weight, after(partial_tokens, up_chain.a, down_chain.a),
    )
    key_value_grad = tn(tokens_own, dkey_value).astype(BF16)

    down_total = Gather(down_chain.rest(), dp_bits()).rest()
    up_total = Gather(up_chain.rest(), reversed(up_order)).rest()
    small_sums = jnp.concatenate(
        [
            jnp.sum(query_sums, axis=0),
            jnp.sum(key_sums, axis=0),
            jnp.sum(first_sums.reshape(3, 8, width), axis=1).reshape(-1),
            jnp.sum(sums.reshape(3, 8, width), axis=1).reshape(-1),
            jnp.sum(up_sum, axis=0),
        ]
    )
    pad = -small_sums.shape[0] % (8 * 128)
    small_sums = sum_small(jnp.pad(small_sums, (0, pad)).reshape(-1, 128)).reshape(-1)
    scatter_order = list(reversed(dp_bits()))
    attention_total = Scatter(
        jnp.concatenate([query_grad, key_value_grad, out_grad], axis=1), scatter_order
    ).rest().astype(F32)

    def owned(start, size):
        part = size // (dp * mp)
        return lax.dynamic_slice_in_dim(small_sums, start + (rank * mp + mp_rank) * part, part, 0)

    return (
        layer_output,
        tokens_grad,
        attention_total[:, : 3 * width],
        owned(0, 3 * width),
        attention_total[:, 3 * width :],
        owned(5 * width, width),
        owned(3 * width, width),
        owned(4 * width, width),
        up_total.astype(F32),
        small_sums[9 * width : 9 * width + half],
        down_total.astype(F32),
        small_sums[8 * width : 9 * width],
        owned(6 * width, width),
        owned(7 * width, width),
    )


def solution(mesh):
    shared = P(("dp", "mp"))
    in_specs = (
        P("dp", None), P(), P(), P(("dp", "mp"), None), shared, P(("dp", "mp"), None), shared, shared,
        shared, P(None, "mp"), P("mp"), P("mp", None), P(), shared, shared, P("dp", None),
    )
    out_specs = (
        P("dp", None), P("dp", None), P(("dp", "mp"), None), shared, P(("dp", "mp"), None), shared,
        shared, shared, P(None, "mp"), P("mp"), P("mp", None), P(), shared, shared,
    )
    return jax.shard_map(local, mesh=mesh, in_specs=in_specs, out_specs=out_specs, check_vma=False)
```

```python
from functools import partial
import math

import jax
import jax.numpy as jnp
from jax import lax
from jax.experimental import pallas as pl
from jax.experimental.pallas import tpu as pltpu
from jax.sharding import PartitionSpec as P

EPSILON = 1e-05
F32 = jnp.float32
BF16 = jnp.bfloat16
LOG2E = math.log2(math.e)
VMEM_LIMIT = 56 * 1024 * 1024
SLOTS = 8
WINDOW = 128
EXTRA = 32
TILE = 256


def nn(a, b):
    return lax.dot_general(a, b, (((1,), (0,)), ((), ())), preferred_element_type=F32)


def nt(a, b):
    return lax.dot_general(a, b, (((1,), (1,)), ((), ())), preferred_element_type=F32)


def tn(a, b):
    return lax.dot_general(a, b, (((0,), (0,)), ((), ())), preferred_element_type=F32)


def fold_rows(a):
    return jnp.sum(a.reshape(a.shape[0] // 8, 8, a.shape[1]), axis=0)


def after(value, *deps):
    return lax.optimization_barrier((value, deps))[0]


def dp_bits():
    count = lax.axis_size("dp")
    bits = []
    bit = count // 2
    while bit:
        bits.append(bit)
        bit //= 2
    return bits


def far_first():
    return dp_bits()


def near_first():
    bits = dp_bits()
    if len(bits) < 3:
        return bits
    return [bits[-2]] + bits[:-2] + [bits[-1]]


def swap_dp(a, bit):
    count = lax.axis_size("dp")
    return lax.ppermute(a, "dp", [(i, i ^ bit) for i in range(count)])


def swap_mp(a):
    return lax.ppermute(a, "mp", [(0, 1), (1, 0)])


def mine(bit):
    return (lax.axis_index("dp") // bit) % 2


def join_pair(own, other, bit, axis):
    low = jnp.stack([own, other], axis)
    high = jnp.stack([other, own], axis)
    return jnp.where(bit == 0, low, high)


class Gather:
    def __init__(self, a, order, done=()):
        self.a = a
        self.tail = a.shape[len(done) :]
        self.order = list(order)
        self.done = list(done)
        self.got = None

    def start(self, *deps):
        if deps:
            self.a = after(self.a, *deps)
        self.got = swap_dp(self.a, self.order[0])
        return self

    def finish(self, *deps):
        bit = self.order.pop(0)
        got = after(self.got, *deps) if deps else self.got
        place = sum(1 for d in self.done if d > bit)
        self.a = join_pair(self.a, got, mine(bit), place)
        self.done.append(bit)
        return self

    def rest(self):
        while self.order:
            self.start().finish()
        return self.result()

    def result(self):
        return self.a.reshape((-1,) + self.tail[1:])


class Scatter:
    def __init__(self, a, order):
        count = lax.axis_size("dp")
        self.left = dp_bits()
        self.a = a.reshape((2,) * len(self.left) + (a.shape[0] // count,) + a.shape[1:])
        self.order = list(order)

    def start(self, *deps):
        bit = self.order[0]
        axis = self.left.index(bit)
        a = after(self.a, *deps) if deps else self.a
        self.own = lax.dynamic_index_in_dim(a, mine(bit), axis, False)
        self.got = swap_dp(lax.dynamic_index_in_dim(a, 1 - mine(bit), axis, False), bit)
        return self

    def finish(self, *deps):
        self.left.remove(self.order.pop(0))
        got = after(self.got, *deps) if deps else self.got
        self.a = (self.own.astype(F32) + got.astype(F32)).astype(self.a.dtype)
        return self

    def rest(self):
        while self.order:
            self.start().finish()
        return self.a

    def start_swap(self, *deps):
        self.own = after(self.a, *deps) if deps else self.a
        self.bit = self.left[0]
        self.got = swap_dp(self.own, self.bit)
        return self

    def finish_swap(self, *deps):
        got = after(self.got, *deps) if deps else self.got
        self.a = (self.own.astype(F32) + got.astype(F32)).astype(self.a.dtype)
        return self

    def gather(self, order):
        return Gather(self.a, order, self.left)


class TableSum:
    def __init__(self, packed):
        self.core = mine(1)
        self.shape = packed.shape
        halves = packed.reshape(2, packed.shape[0] // 2, packed.shape[1])
        self.own = lax.dynamic_index_in_dim(halves, self.core, 0, False)
        self.got = swap_dp(lax.dynamic_index_in_dim(halves, 1 - self.core, 0, False), 1)

    def add(self, *deps):
        got = after(self.got, *deps) if deps else self.got
        self.own = (self.own.astype(F32) + got.astype(F32)).astype(self.own.dtype)
        return self

    def swap(self, bit):
        self.got = swap_dp(self.own, bit)
        return self

    def join(self, *deps):
        got = after(self.got, *deps) if deps else self.got
        return join_pair(self.own, got, self.core, 0).reshape(self.shape)


def full(shape):
    return pl.BlockSpec(shape, lambda t, *_: (0,) * len(shape), pipeline_mode=pl.Buffered(1))


def column(shape, place):
    return pl.BlockSpec(shape, lambda t, *_: (0, place), pipeline_mode=pl.Buffered(1))


def rows(tile, width):
    return pl.BlockSpec((tile, width), lambda t, *_: (t, 0))


def held(shape):
    return pl.BlockSpec(shape, lambda t, *_: (0,) * len(shape))


def call(kernel, tiles, in_specs, outs, scratch, flops):
    return pl.pallas_call(
        kernel,
        grid_spec=pltpu.PrefetchScalarGridSpec(
            num_scalar_prefetch=1,
            grid=(tiles,),
            in_specs=in_specs,
            out_specs=[spec for spec, _, _ in outs],
            scratch_shapes=scratch,
        ),
        out_shape=[jax.ShapeDtypeStruct(shape, kind) for _, shape, kind in outs],
        compiler_params=pltpu.CompilerParams(
            vmem_limit_bytes=VMEM_LIMIT, dimension_semantics=("arbitrary",)
        ),
        cost_estimate=pl.CostEstimate(flops=int(flops), bytes_accessed=20_000_000, transcendentals=0),
    )


def features(scaled, table):
    lhs = jnp.concatenate([scaled.astype(BF16), (-0.5 * scaled * scaled).astype(BF16)], axis=1)
    return jnp.exp2(nn(lhs, table) * LOG2E - 4.0)


def each_small(flags, t, slot, body):
    limit = slot.shape[0] - WINDOW

    def one(j, carry):
        first = flags[t, j]
        final = flags[t, SLOTS + j]
        begin = first // 16 * 16

        def window(i, carry):
            wanted = begin + i * WINDOW
            start = pl.multiple_of(jnp.minimum(wanted, limit), 16)
            rows = pl.ds(start, WINDOW)
            index = lax.broadcasted_iota(jnp.int32, (WINDOW, 128), 0) + start
            body(rows, jnp.logical_and(slot[rows, :] == j, index >= wanted), j)
            return carry

        count = jnp.where(final > first, (final - begin + WINDOW - 1) // WINDOW, 0)
        lax.fori_loop(0, count, window, 0)
        return carry

    lax.fori_loop(1, SLOTS, one, 0)


def pack_tables(table, base, acc, macc):
    pairs = acc.shape[0]
    masses = []
    for p in range(pairs):
        for k in range(2):
            head = 2 * p + k
            span = slice(k * 256, (k + 1) * 256)
            table[pl.ds(base + head * 64, 64), :] = acc[p, k * 64 : (k + 1) * 64, span].astype(BF16)
            source = macc[p, :, span] if macc is not None else acc[p, 128 + k * 64 : 192 + k * 64, span]
            masses.append(jnp.sum(source, axis=0, keepdims=True))
    masses.append(jnp.zeros((16 - 2 * pairs, 256), F32))
    table[pl.ds(base + pairs * 128, 16), :] = jnp.concatenate(masses, axis=0).astype(BF16)


def fill_tables(tabs, main, repeat):
    pairs = tabs.shape[0]
    tabs[...] = jnp.zeros_like(tabs)
    masses = main[pl.ds(pairs * 128, 16), :].astype(F32)
    for p in range(pairs):
        for k in range(2):
            head = 2 * p + k
            span = slice(k * 256, (k + 1) * 256)
            tabs[p, k * 64 : (k + 1) * 64, span] = main[pl.ds(head * 64, 64), :]
            mass = jnp.broadcast_to(masses[head : head + 1, :], (64, 256))
            if not repeat:
                mass = jnp.where(lax.broadcasted_iota(jnp.int32, (64, 256), 0) == 0, mass, 0.0)
            tabs[p, 128 + k * 64 : 192 + k * 64, span] = mass.astype(BF16)


def copy_small(flags, source, target, sems):
    stride = source.shape[0] // (SLOTS - 1)

    def part(j):
        span = pl.ds((j - 1) * stride, stride)
        return pltpu.make_async_copy(source.at[span], target.at[span], sems.at[j - 1])

    for j in range(1, SLOTS):

        @pl.when(flags[0, 2 * SLOTS + j] > 0)
        def _():
            part(j).start()

    for j in range(1, SLOTS):

        @pl.when(flags[0, 2 * SLOTS + j] > 0)
        def _():
            part(j).wait()


def small_table(small, j, p, pairs, repeat, with_masses=True):
    stride = pairs * 128 + 16
    base = (j - 1) * stride
    zero = jnp.zeros((64, 256), BF16)
    tops, bottoms = [], []
    if with_masses:
        masses = small[pl.ds(pl.multiple_of(base + pairs * 128, 16), 16), :].astype(F32)
    for k in range(2):
        head = 2 * p + k
        top = small[pl.ds(pl.multiple_of(base + head * 64, 16), 64), :]
        tops.append(jnp.concatenate([top, zero] if k == 0 else [zero, top], axis=1))
        if with_masses:
            mass = jnp.broadcast_to(masses[head : head + 1, :], (64, 256))
            if not repeat:
                mass = jnp.where(lax.broadcasted_iota(jnp.int32, (64, 256), 0) == 0, mass, 0.0)
            mass = mass.astype(BF16)
            bottoms.append(jnp.concatenate([mass, zero] if k == 0 else [zero, mass], axis=1))
    return jnp.concatenate(tops + bottoms, axis=0)


def masked(mask, value):
    wide = jnp.concatenate([mask] * (value.shape[1] // 128), axis=1)
    return jnp.where(wide, value.astype(F32), 0.0)


def keys_kernel(
    flags, x, key_weight, value_weight, bias, table, slot,
    phi, values, scaled_out, main, small_out,
    acc, macc, sacc, smacc, small, sems,
):
    t = pl.program_id(0)
    pairs = table.shape[0]
    width = pairs * 128
    slow = flags[t, 0] == 0

    @pl.when(t == 0)
    def _():
        acc[...] = jnp.zeros_like(acc)
        macc[...] = jnp.zeros_like(macc)

        for j in range(1, SLOTS):

            @pl.when(flags[0, 2 * SLOTS + j] > 0)
            def _():
                sacc[j - 1] = jnp.zeros_like(sacc[j - 1])
                smacc[j - 1] = jnp.zeros_like(smacc[j - 1])

    keys = nn(x[...], key_weight[:, :width]) + bias[:, :width]
    values[...] = (nn(x[...], value_weight[...]) + bias[:, width:]).astype(BF16)
    for p in range(pairs):
        scaled = keys[:, p * 128 : (p + 1) * 128] * 64 ** (-0.25)
        scaled_out[:, p * 128 : (p + 1) * 128] = scaled.astype(BF16)
        phi[:, p * 512 : (p + 1) * 512] = features(scaled, table[p]).astype(BF16)

    @pl.when(jnp.logical_not(slow))
    def _():
        for p in range(pairs):
            part = phi[:, p * 512 : (p + 1) * 512]
            acc[p] += tn(values[:, p * 128 : (p + 1) * 128], part)
            macc[p] += fold_rows(part.astype(F32))

    @pl.when(slow)
    def _():
        mask = slot[...] == 0
        for p in range(pairs):
            part = phi[:, p * 512 : (p + 1) * 512]
            acc[p] += tn(masked(mask, values[:, p * 128 : (p + 1) * 128]).astype(BF16), part)
            macc[p] += fold_rows(masked(mask, part))

        def body(rows, mask, j):
            for p in range(pairs):
                part = phi[rows, p * 512 : (p + 1) * 512]
                value = masked(mask, values[rows, p * 128 : (p + 1) * 128]).astype(BF16)
                sacc[j - 1, p] += tn(value, part)
                smacc[j - 1, p] += fold_rows(masked(mask, part))

        each_small(flags, t, slot, body)

    @pl.when(t == pl.num_programs(0) - 1)
    def _():
        pack_tables(main, 0, acc, macc)

        for j in range(1, SLOTS):

            @pl.when(flags[0, 2 * SLOTS + j] > 0)
            def _():
                pack_tables(small, (j - 1) * main.shape[0], sacc.at[j - 1], smacc.at[j - 1])

        copy_small(flags, small, small_out, sems)


def queries_kernel(flags, x, weight, bias, table, select, phi, scaled_out, chosen):
    pairs = table.shape[0]
    query = nn(x[...], weight[...]) + bias[...]
    chosen[...] = nn(x[...], select[...]).astype(BF16)
    for p in range(pairs):
        scaled = query[:, p * 128 : (p + 1) * 128] * 64 ** (-0.25)
        scaled_out[:, p * 128 : (p + 1) * 128] = scaled.astype(BF16)
        phi[:, p * 512 : (p + 1) * 512] = features(scaled, table[p]).astype(BF16)


def center(z):
    average = jnp.mean(z, axis=1, keepdims=True)
    centered = z - average
    inverse = lax.rsqrt(jnp.mean(centered * centered, axis=1, keepdims=True) + EPSILON)
    return centered * inverse, inverse


def center_back(e, normed, inverse):
    first = jnp.mean(e, axis=1, keepdims=True)
    second = jnp.mean(e * normed, axis=1, keepdims=True)
    return inverse * (e - first - normed * second)


def middle_kernel(
    flags, x, cot, slot, phi, main, small_in,
    out_weight, up_own, up_here, up_there, down_own, down_here, down_there, bias_own, bias_other, vectors,
    layer_out, hidden_grad, normed_out, inverse_out, att_out, invden_out,
    active_out, dup_out, hidden_out, dffn_out, sums, up_sum,
    tabs, spread, gates, other, up_other, down_other, small, sems, half_sems,
):
    t = pl.program_id(0)
    pairs = tabs.shape[0]
    width = pairs * 128
    core = flags[0, 3 * SLOTS]

    def halves():
        copies = []
        for target, here, there in [(up_other, up_here, up_there), (down_other, down_here, down_there)]:
            count = here.shape[0]
            for source, place in [(here, core), (there, 1 - core)]:
                span = pl.ds(pl.multiple_of(place * count, count), count)
                copies.append((source, target.at[span]))
        return [
            pltpu.make_async_copy(source, target, half_sems.at[i])
            for i, (source, target) in enumerate(copies)
        ]

    @pl.when(t == 0)
    def _():
        for copy in halves():
            copy.start()
        fill_tables(tabs, main, True)
        copy_small(flags, small_in, small, sems)
        sums[...] = jnp.zeros_like(sums)
        up_sum[...] = jnp.zeros_like(up_sum)

    for p in range(pairs):
        spread[:, p * 256 : (p + 1) * 256] = nt(phi[:, p * 512 : (p + 1) * 512], tabs[p])

    @pl.when(flags[t, 0] == 0)
    def _():
        def body(rows, mask, j):
            wide = jnp.concatenate([mask] * 2, axis=1)
            for p in range(pairs):
                got = nt(phi[rows, p * 512 : (p + 1) * 512], small_table(small, j, p, pairs, True))
                old = spread[rows, p * 256 : (p + 1) * 256]
                spread[rows, p * 256 : (p + 1) * 256] = jnp.where(wide, got, old)

        each_small(flags, t, slot, body)

    live = slot[...] < SLOTS
    for p in range(pairs):
        numerator = spread[:, p * 256 : p * 256 + 128]
        denominator = spread[:, p * 256 + 128 : (p + 1) * 256]
        inverse = jnp.where(live, 1.0 / jnp.where(live, denominator, 1.0), 0.0)
        invden_out[:, p * 128 : (p + 1) * 128] = inverse
        att_out[:, p * 128 : (p + 1) * 128] = (numerator * inverse).astype(BF16)

    def vector(i):
        return vectors[i : i + 1, :]

    branch = nn(att_out[...], out_weight[...]) + vector(0)
    first, first_inverse = center(x[...].astype(F32) + branch)
    normed_out[...] = first
    inverse_out[...] = jnp.broadcast_to(first_inverse, inverse_out.shape)
    hidden = first * vector(1) + vector(2)
    hidden_low = hidden.astype(BF16)
    hidden_out[...] = hidden_low
    step = 512
    half = up_own.shape[1]

    @pl.when(t == 0)
    def _():
        for copy in halves():
            copy.wait()

    for which, (up, bias, act) in enumerate(
        [(up_own, bias_own, active_out), (up_other, bias_other, other)]
    ):
        for c in range(0, half, step):
            value = nn(hidden_low, up[:, c : c + step]) + bias[:, c : c + step]
            cdf = 0.5 + 0.5 * lax.erf(value * math.sqrt(0.5))
            gates[:, which * half + c : which * half + c + step] = cdf + value * jnp.exp2(
                value * value * (-0.5 * LOG2E)
            ) * (1.0 / math.sqrt(2.0 * math.pi))
            act[:, c : c + step] = (value * cdf).astype(BF16)
    total = hidden + vector(3)
    total = total + nn(active_out[...], down_own[...])
    total = total + nn(other[...], down_other[...])
    second, second_inverse = center(total)
    layer_out[...] = (second * vector(4) + vector(5)).astype(BF16)
    g = cot[...].astype(F32)
    sums[0:8, :] += fold_rows(g * second)
    sums[8:16, :] += fold_rows(g)
    dsecond = center_back(g * vector(4), second, second_inverse)
    dffn = dsecond.astype(BF16)
    dffn_out[...] = dffn
    sums[16:24, :] += fold_rows(dffn.astype(F32))
    for which, (down, dup_ref) in enumerate([(down_own, dup_out), (down_other, other)]):
        for c in range(0, half, step):
            gate = gates[:, which * half + c : which * half + c + step]
            dup = (nt(dffn, down[c : c + step, :]) * gate).astype(BF16)
            dup_ref[:, c : c + step] = dup
            if which == 0:
                up_sum[:, c : c + step] += fold_rows(dup.astype(F32))
    dsecond = dsecond + nt(dup_out[...], up_own[...])
    dsecond = dsecond + nt(other[...], up_other[...])
    hidden_grad[...] = dsecond


def attention_back_kernel(
    flags, hidden_grad, normed, inverse, att, invden, phi, slot, out_weight, gain, select, more, up_sum,
    dfirst_out, dbranch_out, mixed, chosen, sums, main, small_out,
    acc, sacc, small, sems,
):
    t = pl.program_id(0)
    pairs = acc.shape[0]
    slow = flags[t, 0] == 0

    @pl.when(t == 0)
    def _():
        acc[...] = jnp.zeros_like(acc)
        sums[...] = jnp.zeros_like(sums)

        for j in range(1, SLOTS):

            @pl.when(flags[0, 2 * SLOTS + j] > 0)
            def _():
                sacc[j - 1] = jnp.zeros_like(sacc[j - 1])

    grad = hidden_grad[...]
    first = normed[...]
    sums[0:8, :] += fold_rows(grad * first)
    sums[8:16, :] += fold_rows(grad)
    dfirst = center_back(grad * gain[...], first, inverse[:, 0:1])
    dfirst_out[...] = dfirst
    dbranch = dfirst.astype(BF16)
    dbranch_out[...] = dbranch
    sums[16:24, :] += fold_rows(dbranch.astype(F32))
    chosen[...] = nn(att[...], select[...]).astype(BF16)
    datt = nt(dbranch, out_weight[...])
    ratio = datt * invden[...]
    dden = -ratio * att[...].astype(F32)
    for p in range(pairs):
        mixed[:, p * 256 : p * 256 + 128] = ratio[:, p * 128 : (p + 1) * 128].astype(BF16)
        mixed[:, p * 256 + 128 : (p + 1) * 256] = dden[:, p * 128 : (p + 1) * 128].astype(BF16)

    @pl.when(jnp.logical_not(slow))
    def _():
        for p in range(pairs):
            acc[p] += tn(mixed[:, p * 256 : (p + 1) * 256], phi[:, p * 512 : (p + 1) * 512])

    @pl.when(slow)
    def _():
        mask = slot[...] == 0
        for p in range(pairs):
            part = masked(mask, mixed[:, p * 256 : (p + 1) * 256]).astype(BF16)
            acc[p] += tn(part, phi[:, p * 512 : (p + 1) * 512])

        def body(rows, mask, j):
            for p in range(pairs):
                part = masked(mask, mixed[rows, p * 256 : (p + 1) * 256]).astype(BF16)
                sacc[j - 1, p] += tn(part, phi[rows, p * 512 : (p + 1) * 512])

        each_small(flags, t, slot, body)

    @pl.when(t == pl.num_programs(0) - 1)
    def _():
        pack_tables(main, 0, acc, None)
        lines = []
        for source in (sums, more, up_sum):
            for i in range(source.shape[0] // 8):
                line = jnp.sum(source[8 * i : 8 * i + 8, :], axis=0, keepdims=True)
                lines += [line[:, c : c + 256] for c in range(0, source.shape[1], 256)]
        lines.append(jnp.zeros((EXTRA - len(lines), 256), F32))
        main[pl.ds(pairs * 128 + 16, EXTRA), :] = jnp.concatenate(lines, axis=0).astype(BF16)

        for j in range(1, SLOTS):

            @pl.when(flags[0, 2 * SLOTS + j] > 0)
            def _():
                pack_tables(small, (j - 1) * (pairs * 128 + 16), sacc.at[j - 1], None)

        copy_small(flags, small, small_out, sems)


def feature_back(rows, p, grad, phi, scaled, table):
    span = slice(p * 128, (p + 1) * 128)
    e = (grad * phi[rows, p * 512 : (p + 1) * 512].astype(F32)).astype(BF16)
    back = nt(e, table[p])
    return (back[:, :128] - scaled[rows, span].astype(F32) * back[:, 128:]) * 64 ** (-0.25)


def store_some(ref, rows, span, mask, value):
    old = ref[rows, span].astype(F32)
    ref[rows, span] = jnp.where(mask, value, old).astype(ref.dtype)


def queries_back_kernel(
    flags, mixed, phi, scaled, slot, main, small_in, table, weight, dfirst,
    dquery_out, partial_out, sums, tabs, small, sems,
):
    t = pl.program_id(0)
    pairs = tabs.shape[0]

    @pl.when(t == 0)
    def _():
        fill_tables(tabs, main, True)
        copy_small(flags, small_in, small, sems)
        sums[...] = jnp.zeros_like(sums)

    for p in range(pairs):
        grad = nn(mixed[:, p * 256 : (p + 1) * 256], tabs[p])
        du = feature_back(slice(None), p, grad, phi, scaled, table)
        dquery_out[:, p * 128 : (p + 1) * 128] = du.astype(BF16)

    @pl.when(flags[t, 0] == 0)
    def _():
        def body(rows, mask, j):
            for p in range(pairs):
                own = small_table(small, j, p, pairs, True)
                grad = nn(mixed[rows, p * 256 : (p + 1) * 256], own)
                du = feature_back(rows, p, grad, phi, scaled, table)
                store_some(dquery_out, rows, slice(p * 128, (p + 1) * 128), mask, du)

        each_small(flags, t, slot, body)

    sums[...] += fold_rows(dquery_out[...].astype(F32))
    partial_out[...] = dfirst[...] + nt(dquery_out[...], weight[...])


def keys_back_kernel(
    flags, phi, values, scaled, slot, main, small_in, table, key_weight, value_weight, partial_in,
    djoint_out, tokens_out, sums, tabs, small, sems,
):
    t = pl.program_id(0)
    pairs = tabs.shape[0]
    width = pairs * 128

    @pl.when(t == 0)
    def _():
        fill_tables(tabs, main, False)
        copy_small(flags, small_in, small, sems)
        sums[...] = jnp.zeros_like(sums)

    def extended(rows, p):
        value = values[rows, p * 128 : (p + 1) * 128]
        return jnp.concatenate([value, jnp.ones_like(value)], axis=1)

    for p in range(pairs):
        grad = nn(extended(slice(None), p), tabs[p])
        du = feature_back(slice(None), p, grad, phi, scaled, table)
        djoint_out[:, p * 128 : (p + 1) * 128] = du.astype(BF16)
        dvalue = nt(phi[:, p * 512 : (p + 1) * 512], tabs[p, :128, :])
        djoint_out[:, width + p * 128 : width + (p + 1) * 128] = dvalue.astype(BF16)

    @pl.when(flags[t, 0] == 0)
    def _():
        live = slot[...] < SLOTS
        for p in range(2 * pairs):
            part = djoint_out[:, p * 128 : (p + 1) * 128]
            djoint_out[:, p * 128 : (p + 1) * 128] = masked(live, part).astype(BF16)

        def body(rows, mask, j):
            for p in range(pairs):
                own = small_table(small, j, p, pairs, False)
                grad = nn(extended(rows, p), own)
                du = feature_back(rows, p, grad, phi, scaled, table)
                store_some(djoint_out, rows, slice(p * 128, (p + 1) * 128), mask, du)
                dvalue = nt(phi[rows, p * 512 : (p + 1) * 512], own[:128, :])
                span = slice(width + p * 128, width + (p + 1) * 128)
                store_some(djoint_out, rows, span, mask, dvalue)

        each_small(flags, t, slot, body)

    sums[...] += fold_rows(djoint_out[...].astype(F32))
    tokens_out[...] = (
        partial_in[...]
        + nt(djoint_out[:, :width], key_weight[:, :width])
        + nt(djoint_out[:, width:], value_weight[...])
    ).astype(BF16)


def table_outs(width, extra=0):
    count = width + 16
    small = (SLOTS - 1) * count
    count = count + extra
    anywhere = pl.BlockSpec(memory_space=pl.ANY)
    return [(held((count, 256)), (count, 256), BF16), (anywhere, (small, 256), BF16)]


def table_ins(width):
    return [full((width + 16, 256)), pl.BlockSpec(memory_space=pl.ANY)]


def table_scratch(width):
    return pltpu.VMEM((width // 128, 256, 512), BF16)


def small_scratch(width):
    return pltpu.VMEM(((SLOTS - 1) * (width + 16), 256), BF16)


def run_keys(tile, flags, tokens, key_weight, value_weight, bias, table, slots):
    count, width = tokens.shape
    pairs = table.shape[0]
    wide = pairs * 512
    return call(
        keys_kernel,
        count // tile,
        [
            rows(tile, width), full(key_weight.shape), full((width, width)), full((1, 2 * width)),
            full(table.shape), rows(tile, 128),
        ],
        [
            (rows(tile, wide), (count, wide), BF16),
            (rows(tile, width), (count, width), BF16),
            (rows(tile, width), (count, width), BF16),
        ]
        + table_outs(width),
        [
            pltpu.VMEM((pairs, 128, 512), F32),
            pltpu.VMEM((pairs, 8, 512), F32),
            pltpu.VMEM((SLOTS - 1, pairs, 128, 512), F32),
            pltpu.VMEM((SLOTS - 1, pairs, 8, 512), F32),
            small_scratch(width),
            pltpu.SemaphoreType.DMA((SLOTS - 1,)),
        ],
        10e9,
    )(flags, tokens, key_weight, value_weight, bias, table, slots)


def run_queries(tile, flags, tokens, weight, bias, table, select):
    count, width = tokens.shape
    wide = table.shape[0] * 512
    own_rows = select.shape[1]
    return call(
        queries_kernel,
        count // tile,
        [
            rows(tile, width), column((width, width), 0), full((1, width)), full(table.shape),
            full((width, own_rows)),
        ],
        [
            (rows(tile, wide), (count, wide), BF16),
            (rows(tile, width), (count, width), BF16),
            (rows(tile, own_rows), (count, own_rows), BF16),
        ],
        [],
        6e9,
    )(flags, tokens, weight, bias, table, select)


def run_middle(
    tile, flags, tokens, cotangent, slots, phi, moments, small, query_out, up_own, up_here, up_there,
    down_own, down_here, down_there, bias_own, bias_other, vectors,
):
    count, width = tokens.shape
    half = up_own.shape[1]
    wide = phi.shape[1]
    pairs = width // 128
    return call(
        middle_kernel,
        count // tile,
        [rows(tile, width), rows(tile, width), rows(tile, 128), rows(tile, wide)]
        + table_ins(width)
        + [
            column((width, width), 1),
            full((width, half)),
            pl.BlockSpec(memory_space=pl.ANY),
            pl.BlockSpec(memory_space=pl.ANY),
            full((half, width)),
            pl.BlockSpec(memory_space=pl.ANY),
            pl.BlockSpec(memory_space=pl.ANY),
            full((1, half)),
            full((1, half)),
            full((8, width)),
        ],
        [
            (rows(tile, width), (count, width), BF16),
            (rows(tile, width), (count, width), F32),
            (rows(tile, width), (count, width), F32),
            (rows(tile, 128), (count, 128), F32),
            (rows(tile, width), (count, width), BF16),
            (rows(tile, width), (count, width), F32),
            (rows(tile, half), (count, half), BF16),
            (rows(tile, half), (count, half), BF16),
            (rows(tile, width), (count, width), BF16),
            (rows(tile, width), (count, width), BF16),
            (held((24, width)), (24, width), F32),
            (held((8, half)), (8, half), F32),
        ],
        [
            table_scratch(width),
            pltpu.VMEM((tile, pairs * 256), F32),
            pltpu.VMEM((tile, 2 * half), F32),
            pltpu.VMEM((tile, half), BF16),
            pltpu.VMEM((width, half), BF16),
            pltpu.VMEM((half, width), BF16),
            small_scratch(width),
            pltpu.SemaphoreType.DMA((SLOTS - 1,)),
            pltpu.SemaphoreType.DMA((4,)),
        ],
        30e9,
    )(
        flags, tokens, cotangent, slots, phi, moments, small, query_out, up_own, up_here, up_there,
        down_own, down_here, down_there, bias_own, bias_other, vectors,
    )


def run_attention_back(
    tile, flags, hidden_grad, normed, inverse, att, invden, phi, slots, query_out, gain, select, sums, up_sum
):
    count, width = att.shape
    wide = phi.shape[1]
    pairs = width // 128
    own_rows = select.shape[1]
    half = up_sum.shape[1]
    return call(
        attention_back_kernel,
        count // tile,
        [
            rows(tile, width), rows(tile, width), rows(tile, 128), rows(tile, width), rows(tile, width),
            rows(tile, wide), rows(tile, 128), column((width, width), 1), full((1, width)), full((width, own_rows)),
            full((24, width)), full((8, half)),
        ],
        [
            (rows(tile, width), (count, width), F32),
            (rows(tile, width), (count, width), BF16),
            (rows(tile, 2 * width), (count, 2 * width), BF16),
            (rows(tile, own_rows), (count, own_rows), BF16),
            (held((24, width)), (24, width), F32),
        ]
        + table_outs(width, EXTRA),
        [
            pltpu.VMEM((pairs, 256, 512), F32),
            pltpu.VMEM((SLOTS - 1, pairs, 256, 512), F32),
            small_scratch(width),
            pltpu.SemaphoreType.DMA((SLOTS - 1,)),
        ],
        6e9,
    )(
        flags, hidden_grad, normed, inverse, att, invden, phi, slots, query_out, gain, select, sums, up_sum
    )


def run_queries_back(tile, flags, mixed, phi, scaled, slots, moments, small, table, weight, dfirst):
    count, width = scaled.shape
    wide = phi.shape[1]
    return call(
        queries_back_kernel,
        count // tile,
        [rows(tile, 2 * width), rows(tile, wide), rows(tile, width), rows(tile, 128)]
        + table_ins(width)
        + [full(table.shape), column((width, width), 0), rows(tile, width)],
        [
            (rows(tile, width), (count, width), BF16),
            (rows(tile, width), (count, width), F32),
            (held((8, width)), (8, width), F32),
        ],
        [table_scratch(width), small_scratch(width), pltpu.SemaphoreType.DMA((SLOTS - 1,))],
        8e9,
    )(flags, mixed, phi, scaled, slots, moments, small, table, weight, dfirst)


def run_keys_back(
    tile, flags, phi, values, scaled, slots, moments, small, table, key_weight, value_weight, partial
):
    count, width = scaled.shape
    wide = phi.shape[1]
    return call(
        keys_back_kernel,
        count // tile,
        [rows(tile, wide), rows(tile, width), rows(tile, width), rows(tile, 128)]
        + table_ins(width)
        + [full(table.shape), full(key_weight.shape), full((width, width)), rows(tile, width)],
        [
            (rows(tile, 2 * width), (count, 2 * width), BF16),
            (rows(tile, width), (count, width), BF16),
            (held((8, 2 * width)), (8, 2 * width), F32),
        ],
        [
            table_scratch(width),
            small_scratch(width),
            pltpu.SemaphoreType.DMA((SLOTS - 1,)),
        ],
        12e9,
    )(
        flags, phi, values, scaled, slots, moments, small, table, key_weight, value_weight, partial,
    )


def local(
    tokens, document_lengths, feature_maps, joint_weight, joint_bias, output_weight, output_bias,
    first_gain, first_shift, up_weight, up_bias, down_weight, down_bias, second_gain, second_shift,
    cotangent,
):
    count, width = tokens.shape
    heads, head_size, feature_count = feature_maps.shape
    pairs = heads // 2
    half = up_weight.shape[1]
    tile = TILE
    tiles = count // tile
    rank = lax.axis_index("dp")
    dp = lax.axis_size("dp")
    mp = lax.axis_size("mp")
    mp_rank = lax.axis_index("mp")

    lengths = document_lengths[0]
    ends = jnp.cumsum(lengths)
    place = rank * count + jnp.arange(count, dtype=jnp.int32)
    document = jnp.sum((ends[None, :] <= place[:, None]).astype(jnp.int32), axis=1)
    longest = jnp.argmax(lengths).astype(jnp.int32)
    slot = jnp.where(
        document == longest,
        0,
        jnp.where(document >= SLOTS, SLOTS, jnp.where(document < longest, document + 1, document)),
    )
    slots = jnp.broadcast_to(slot[:, None], (count, 128))
    order = jnp.arange(SLOTS, dtype=jnp.int32)
    which = jnp.where(order - 1 < longest, order - 1, order)
    starts = jnp.where(which > 0, ends[jnp.maximum(which - 1, 0)], 0)
    stops = ends[jnp.maximum(which, 0)]
    base = rank * count + jnp.arange(tiles, dtype=jnp.int32)[:, None] * tile
    all_main = jnp.max(slot.reshape(tiles, tile), axis=1, keepdims=True) == 0
    starts_in = jnp.clip(starts[None, :] - base, 0, tile)
    stops_in = jnp.clip(stops[None, :] - base, 0, tile)
    present = jnp.max((stops_in > starts_in).astype(jnp.int32), axis=0, keepdims=True)
    flags = jnp.concatenate(
        [
            all_main.astype(jnp.int32),
            starts_in[:, 1:],
            stops_in,
            jnp.broadcast_to(present, (tiles, SLOTS)),
            jnp.broadcast_to(mine(1).astype(jnp.int32), (tiles, SLOTS)),
        ],
        axis=1,
    )

    shard = joint_weight.shape[0]
    small_vectors = jnp.concatenate(
        [joint_bias, output_bias, first_gain, first_shift, second_gain, second_shift]
    )
    vector_size = small_vectors.shape[0]
    lines = -(-vector_size // 128)
    small_vectors = jnp.pad(small_vectors, (0, lines * 128 - vector_size)).reshape(lines, 128)
    small_vectors = jnp.pad(small_vectors, ((0, shard - lines), (0, 0)))
    shards = jnp.concatenate([joint_weight[:, width:], small_vectors], axis=1)
    query_out = lax.all_gather(
        jnp.concatenate([joint_weight[:, :width], output_weight], axis=1), ("dp", "mp"), axis=0, tiled=True
    )
    shards = join_pair(shards, swap_mp(shards), mp_rank, 0).reshape(2 * shard, -1)
    key_chain = Gather(
        jnp.concatenate([shards[:, :width], shards[:, 2 * width :]], axis=1), far_first()
    )
    value_chain = Gather(shards[:, width : 2 * width], near_first())

    core = mine(1)

    def own_part(a):
        return lax.dynamic_slice_in_dim(a, core * (a.shape[0] // 2), a.shape[0] // 2, 0)

    while key_chain.order:
        key_chain.start()
        value_chain.start()
        if len(key_chain.order) == len(dp_bits()):
            up_here = swap_mp(after(own_part(up_weight), shards))
            down_here = swap_mp(after(own_part(down_weight), up_here))
        key_chain.finish()
        value_chain.finish()
    key_weight = key_chain.result()
    value_weight = value_chain.result()

    vectors_all = key_weight[:, width:].reshape(dp * mp, shard, 128)[:, :lines].reshape(dp * mp, -1)
    bias_part = joint_bias.shape[0]
    joint_offset = vectors_all[:, :bias_part].reshape(1, -1).astype(F32)
    bias_own = up_bias[None, :].astype(F32)

    pair_maps = feature_maps.reshape(pairs, 2, head_size, feature_count)
    blank = jnp.zeros_like(pair_maps[:, 0])
    table = jnp.concatenate(
        [
            jnp.concatenate([pair_maps[:, 0], blank], axis=2),
            jnp.concatenate([blank, pair_maps[:, 1]], axis=2),
            jnp.concatenate([blank + 1, blank], axis=2),
            jnp.concatenate([blank, blank + 1], axis=2),
        ],
        axis=1,
    )
    own_rows = width // mp
    index = jnp.arange(own_rows, dtype=jnp.int32)
    source = index // shard * (shard * mp) + mp_rank * shard + index % shard
    select = (jnp.arange(width, dtype=jnp.int32)[:, None] == source[None, :]).astype(BF16)

    phi_k, values, scaled_k, moments, small_moments = run_keys(
        TILE, flags, tokens, key_weight, value_weight, joint_offset[:, width:], table, slots
    )

    up_there = swap_dp(after(up_here, moments), 1)
    down_there = swap_dp(after(down_here, up_there), 1)
    bias_other = swap_mp(after(up_bias, moments)[None, :]).astype(F32)
    vectors_all = after(vectors_all, moments)
    parts = [
        vectors_all[:, bias_part + i * shard : bias_part + (i + 1) * shard].reshape(-1).astype(F32)
        for i in range(5)
    ]
    vectors = jnp.stack(
        [parts[0], parts[1], parts[2], down_bias.astype(F32), parts[3], parts[4], parts[4], parts[4]]
    )
    bits = dp_bits()
    far, others = bits[0], bits[1:-1]
    moments_sum = TableSum(moments).add()
    for bit in reversed(others):
        moments_sum.swap(bit).add()
    moments_sum.swap(far)
    phi_q, scaled_q, tokens_own = run_queries(
        TILE, flags, after(tokens, moments_sum.own), query_out, joint_offset[:, :width], table, select
    )
    moments = moments_sum.add(phi_q).swap(1).join()
    (
        layer_output, hidden_grad, normed, inverse, att, invden, active, dup, hidden_low, dffn, sums, up_sum,
    ) = run_middle(
        TILE, flags, tokens, cotangent, slots, phi_q, moments, small_moments, query_out, up_weight,
        up_here, up_there, down_weight, down_here, down_there, bias_own, bias_other, vectors,
    )

    near = others[-1:]
    middle_bits = others[:-1]
    down_order = [1] + near + middle_bits
    up_order = [1] + middle_bits + near
    down_grad = tn(active, dffn).astype(BF16)
    down = Scatter(down_grad, down_order).start()
    up_grad = tn(after(hidden_low, down_grad), dup).astype(BF16)
    down.finish(up_grad)
    up = Scatter(up_grad, up_order).start(down.a)
    down.start()
    up.finish(down.a).start()

    dfirst, dbranch, mixed, att_own, first_sums, dmoments, small_dmoments = run_attention_back(
        TILE, flags, after(hidden_grad, up.a, down.a), normed, inverse, att, invden, phi_q, slots,
        query_out, vectors[1:2], select, sums, up_sum,
    )

    dmoments_sum = TableSum(dmoments)
    down.finish(dmoments)
    up.finish(down.a)
    dmoments_sum.add(up.a)
    for place, bit in enumerate(middle_bits):
        dmoments_sum.swap(bit)
        if place == 0:
            down.start(dmoments_sum.own)
            up.start(dmoments_sum.own)
            out_grad = tn(after(att_own, dmoments_sum.own), dbranch).astype(BF16)
            dmoments_sum.add(out_grad)
        else:
            dmoments_sum.add()
    dmoments_sum.swap(far)
    dquery, partial_tokens, query_sums = run_queries_back(
        TILE, flags, mixed, phi_q, scaled_q, slots, moments, small_moments, table, query_out,
        after(dfirst, dmoments_sum.own),
    )
    dmoments_sum.add(dquery).swap(near[0])
    down.finish(dmoments_sum.own)
    up.finish(down.a)
    while down.order:
        down.start().finish()
        up.start().finish()
    down.start_swap()
    up.start_swap(down.a)
    query_grad = tn(after(tokens_own, dmoments_sum.own), dquery).astype(BF16)
    query_out_grad = Scatter(jnp.concatenate([query_grad, out_grad], axis=1), down_order + [far])
    query_out_grad.start(dmoments_sum.add(query_grad).own)
    dmoments_sum.swap(1)
    query_out_grad.finish(dmoments_sum.own).start()
    dmoments = dmoments_sum.join(query_out_grad.a)
    dkey_value, tokens_grad, key_sums = run_keys_back(
        TILE, flags, phi_k, values, scaled_k, slots, dmoments, small_dmoments, table, key_weight,
        value_weight, after(partial_tokens, query_out_grad.a),
    )
    key_value_grad = tn(tokens_own, dkey_value).astype(BF16)
    biases = jnp.concatenate([jnp.sum(query_sums, axis=0), jnp.sum(key_sums, axis=0)])
    biases = biases.reshape(dp * shard, -1)
    bias_columns = biases.shape[1]
    biases = jnp.pad(biases, ((0, 0), (0, 128 - bias_columns))).astype(BF16)
    key_value_sum = Scatter(jnp.concatenate([key_value_grad, biases], axis=1), up_order + [far]).start()

    down.finish_swap(dkey_value)
    up.finish_swap(down.a)
    down = down.gather(middle_bits[::-1] + near + [1]).start()
    up = up.gather(near + middle_bits[::-1] + [1]).start()
    key_value_sum.finish(up.a, down.a).start()
    query_out_grad.finish(key_value_sum.a).start()
    down.finish(query_out_grad.a).start()
    up.finish(down.a).start()
    key_value_sum.finish(up.a)
    query_out_grad.finish(key_value_sum.a)
    while down.order:
        if key_value_sum.order:
            key_value_sum.start()
        if query_out_grad.order:
            query_out_grad.start()
        down.finish(key_value_sum.a)
        up.finish(down.a)
        if down.order:
            down.start()
            up.start()
        if query_out_grad.got is not None and query_out_grad.order:
            query_out_grad.finish(up.a)
        if key_value_sum.order:
            key_value_sum.finish(up.a)
    down_total = down.result()
    up_total = up.result()
    query_out_total = query_out_grad.rest().astype(F32)
    key_value_total = key_value_sum.rest().astype(F32)

    extra = dmoments[width + 16 :].reshape(-1).astype(F32)

    def owned(place, size=width):
        part = size // (dp * mp)
        start = place * width + (rank * mp + mp_rank) * part
        return lax.dynamic_slice_in_dim(extra, start, part, 0)

    bias_total = key_value_total[:, 2 * width : 2 * width + bias_columns].reshape(mp, -1)
    bias_total = lax.dynamic_index_in_dim(bias_total, mp_rank, 0, False)

    return (
        layer_output,
        tokens_grad,
        jnp.concatenate([query_out_total[:, :width], key_value_total[:, : 2 * width]], axis=1),
        bias_total,
        query_out_total[:, width:],
        owned(2),
        owned(0),
        owned(1),
        up_total.astype(F32),
        extra[6 * width : 6 * width + half],
        down_total.astype(F32),
        extra[5 * width : 6 * width],
        owned(3),
        owned(4),
    )


def solution(mesh):
    shared = P(("dp", "mp"))
    in_specs = (
        P("dp", None), P(), P(), P(("dp", "mp"), None), shared, P(("dp", "mp"), None), shared, shared,
        shared, P(None, "mp"), P("mp"), P("mp", None), P(), shared, shared, P("dp", None),
    )
    out_specs = (
        P("dp", None), P("dp", None), P(("dp", "mp"), None), shared, P(("dp", "mp"), None), shared,
        shared, shared, P(None, "mp"), P("mp"), P("mp", None), P(), shared, shared,
    )
    return jax.shard_map(local, mesh=mesh, in_specs=in_specs, out_specs=out_specs, check_vma=False)
```

```python
from functools import partial
import math

import jax
import jax.numpy as jnp
from jax import lax
from jax.experimental import pallas as pl
from jax.experimental.pallas import tpu as pltpu
from jax.sharding import PartitionSpec as P

EPSILON = 1e-05
F32 = jnp.float32
BF16 = jnp.bfloat16
LOG2E = math.log2(math.e)
VMEM_LIMIT = 56 * 1024 * 1024
SLOTS = 8
WINDOW = 128
EXTRA = 32
TILE = 256


def nn(a, b):
    return lax.dot_general(a, b, (((1,), (0,)), ((), ())), preferred_element_type=F32)


def nt(a, b):
    return lax.dot_general(a, b, (((1,), (1,)), ((), ())), preferred_element_type=F32)


def tn(a, b):
    return lax.dot_general(a, b, (((0,), (0,)), ((), ())), preferred_element_type=F32)


def fold_rows(a):
    return jnp.sum(a.reshape(a.shape[0] // 8, 8, a.shape[1]), axis=0)


def after(value, *deps):
    return lax.optimization_barrier((value, deps))[0]


def dp_bits():
    count = lax.axis_size("dp")
    bits = []
    bit = count // 2
    while bit:
        bits.append(bit)
        bit //= 2
    return bits


def far_first():
    return dp_bits()


def near_first():
    bits = dp_bits()
    if len(bits) < 3:
        return bits
    return [bits[-2]] + bits[:-2] + [bits[-1]]


def swap_dp(a, bit):
    count = lax.axis_size("dp")
    return lax.ppermute(a, "dp", [(i, i ^ bit) for i in range(count)])


def swap_mp(a):
    return lax.ppermute(a, "mp", [(0, 1), (1, 0)])


def mine(bit):
    return (lax.axis_index("dp") // bit) % 2


def join_pair(own, other, bit, axis):
    low = jnp.stack([own, other], axis)
    high = jnp.stack([other, own], axis)
    return jnp.where(bit == 0, low, high)


class Gather:
    def __init__(self, a, order, done=()):
        self.a = a
        self.tail = a.shape[len(done) :]
        self.order = list(order)
        self.done = list(done)
        self.got = None

    def start(self, *deps):
        if deps:
            self.a = after(self.a, *deps)
        self.got = swap_dp(self.a, self.order[0])
        return self

    def finish(self, *deps):
        bit = self.order.pop(0)
        got = after(self.got, *deps) if deps else self.got
        place = sum(1 for d in self.done if d > bit)
        self.a = join_pair(self.a, got, mine(bit), place)
        self.done.append(bit)
        return self

    def rest(self):
        while self.order:
            self.start().finish()
        return self.result()

    def result(self):
        return self.a.reshape((-1,) + self.tail[1:])


class Sum:
    def __init__(self, a, order):
        self.a = a
        self.order = list(order)
        self.done = []

    def start(self, *deps):
        bit = self.order[0]
        a = after(self.a, *deps) if deps else self.a
        count = a.shape[0] // 2
        self.own = lax.dynamic_slice_in_dim(a, mine(bit) * count, count, 0)
        self.got = swap_dp(lax.dynamic_slice_in_dim(a, (1 - mine(bit)) * count, count, 0), bit)
        return self

    def finish(self, *deps):
        self.done.append(self.order.pop(0))
        got = after(self.got, *deps) if deps else self.got
        self.a = (self.own.astype(F32) + got.astype(F32)).astype(self.a.dtype)
        return self

    def rest(self):
        while self.order:
            self.start().finish()
        return self.a

    def start_swap(self, bit, *deps):
        self.own = after(self.a, *deps) if deps else self.a
        self.got = swap_dp(self.own, bit)
        return self

    def finish_swap(self, *deps):
        got = after(self.got, *deps) if deps else self.got
        self.a = (self.own.astype(F32) + got.astype(F32)).astype(self.a.dtype)
        return self

    def start_back(self):
        self.got = swap_dp(self.a, self.done[-1])
        return self

    def finish_back(self, *deps):
        got = after(self.got, *deps) if deps else self.got
        a = join_pair(self.a, got, mine(self.done.pop()), 0)
        self.a = a.reshape((-1,) + a.shape[2:])
        return self


class TableSum:
    def __init__(self, packed):
        self.core = mine(1)
        self.shape = packed.shape
        halves = packed.reshape(2, packed.shape[0] // 2, packed.shape[1])
        self.own = lax.dynamic_index_in_dim(halves, self.core, 0, False)
        self.got = swap_dp(lax.dynamic_index_in_dim(halves, 1 - self.core, 0, False), 1)

    def add(self, *deps):
        got = after(self.got, *deps) if deps else self.got
        self.own = (self.own.astype(F32) + got.astype(F32)).astype(self.own.dtype)
        return self

    def swap(self, bit):
        self.got = swap_dp(self.own, bit)
        return self

    def join(self, *deps):
        got = after(self.got, *deps) if deps else self.got
        return join_pair(self.own, got, self.core, 0).reshape(self.shape)


def full(shape):
    return pl.BlockSpec(shape, lambda t, *_: (0,) * len(shape), pipeline_mode=pl.Buffered(1))


def column(shape, place):
    return pl.BlockSpec(shape, lambda t, *_: (0, place), pipeline_mode=pl.Buffered(1))


def rows(tile, width):
    return pl.BlockSpec((tile, width), lambda t, *_: (t, 0))


def held(shape):
    return pl.BlockSpec(shape, lambda t, *_: (0,) * len(shape))


def call(kernel, tiles, in_specs, outs, scratch, flops):
    return pl.pallas_call(
        kernel,
        grid_spec=pltpu.PrefetchScalarGridSpec(
            num_scalar_prefetch=1,
            grid=(tiles,),
            in_specs=in_specs,
            out_specs=[spec for spec, _, _ in outs],
            scratch_shapes=scratch,
        ),
        out_shape=[jax.ShapeDtypeStruct(shape, kind) for _, shape, kind in outs],
        compiler_params=pltpu.CompilerParams(
            vmem_limit_bytes=VMEM_LIMIT, dimension_semantics=("arbitrary",)
        ),
        cost_estimate=pl.CostEstimate(flops=int(flops), bytes_accessed=20_000_000, transcendentals=0),
    )


def features(scaled, table):
    lhs = jnp.concatenate([scaled.astype(BF16), (-0.5 * scaled * scaled).astype(BF16)], axis=1)
    return jnp.exp2(nn(lhs, table) * LOG2E - 4.0)


class Documents:
    def __init__(self, meta, info, tile):
        self.meta, self.info, self.tile = meta, info, tile
        self.t = pl.program_id(0)

    def setup(self):
        meta, info = self.meta, self.info
        edges = [-meta[SLOTS]]
        for d in range(SLOTS):
            edges.append(edges[-1] + meta[d])
        most, longest = meta[0], jnp.int32(0)
        for d in range(1, SLOTS):
            longest = jnp.where(meta[d] > most, d, longest)
            most = jnp.maximum(most, meta[d])
        start, stop = edges[0], edges[1]
        for d in range(1, SLOTS):
            start = jnp.where(longest == d, edges[d], start)
            stop = jnp.where(longest == d, edges[d + 1], stop)
        info[0] = start
        info[SLOTS] = stop
        for j in range(1, SLOTS):
            before = longest > j - 1
            info[j] = jnp.where(before, edges[j - 1], edges[j])
            info[SLOTS + j] = jnp.where(before, edges[j], edges[j + 1])
        info[2 * SLOTS] = edges[SLOTS]

    def slow(self):
        first = self.t * self.tile
        inside = jnp.logical_and(self.info[0] <= first, self.info[SLOTS] >= first + self.tile)
        return jnp.logical_not(inside)

    def present(self, j):
        rows = self.tile * pl.num_programs(0)
        return jnp.maximum(self.info[j], 0) < jnp.minimum(self.info[SLOTS + j], rows)

    def places(self, first, rows):
        return lax.broadcasted_iota(jnp.int32, (rows, 128), 0) + (self.t * self.tile + first)

    def main(self):
        place = self.places(0, self.tile)
        return jnp.logical_and(place >= self.info[0], place < self.info[SLOTS])

    def live(self):
        return self.places(0, self.tile) < self.info[2 * SLOTS]

    def each_small(self, body):
        limit = self.tile - WINDOW
        base = self.t * self.tile

        def one(j, carry):
            first = jnp.clip(self.info[j] - base, 0, self.tile)
            final = jnp.clip(self.info[SLOTS + j] - base, 0, self.tile)
            begin = first // 16 * 16

            def window(i, carry):
                wanted = begin + i * WINDOW
                start = pl.multiple_of(jnp.minimum(wanted, limit), 16)
                place = lax.broadcasted_iota(jnp.int32, (WINDOW, 128), 0) + start
                low = jnp.maximum(first, wanted)
                body(pl.ds(start, WINDOW), jnp.logical_and(place >= low, place < final), j)
                return carry

            count = jnp.where(final > first, (final - begin + WINDOW - 1) // WINDOW, 0)
            lax.fori_loop(0, count, window, 0)
            return carry

        lax.fori_loop(1, SLOTS, one, 0)


def pack_tables(table, base, acc, macc):
    pairs = acc.shape[0]
    masses = []
    for p in range(pairs):
        for k in range(2):
            head = 2 * p + k
            span = slice(k * 256, (k + 1) * 256)
            table[pl.ds(base + head * 64, 64), :] = acc[p, k * 64 : (k + 1) * 64, span].astype(BF16)
            source = macc[p, :, span] if macc is not None else acc[p, 128 + k * 64 : 192 + k * 64, span]
            masses.append(jnp.sum(source, axis=0, keepdims=True))
    masses.append(jnp.zeros((16 - 2 * pairs, 256), F32))
    table[pl.ds(base + pairs * 128, 16), :] = jnp.concatenate(masses, axis=0).astype(BF16)


def fill_tables(tabs, main, repeat):
    pairs = tabs.shape[0]
    tabs[...] = jnp.zeros_like(tabs)
    masses = main[pl.ds(pairs * 128, 16), :].astype(F32)
    for p in range(pairs):
        for k in range(2):
            head = 2 * p + k
            span = slice(k * 256, (k + 1) * 256)
            tabs[p, k * 64 : (k + 1) * 64, span] = main[pl.ds(head * 64, 64), :]
            mass = jnp.broadcast_to(masses[head : head + 1, :], (64, 256))
            if not repeat:
                mass = jnp.where(lax.broadcasted_iota(jnp.int32, (64, 256), 0) == 0, mass, 0.0)
            tabs[p, 128 + k * 64 : 192 + k * 64, span] = mass.astype(BF16)


def copy_small(docs, source, target, sems):
    stride = source.shape[0] // (SLOTS - 1)

    def part(j):
        span = pl.ds((j - 1) * stride, stride)
        return pltpu.make_async_copy(source.at[span], target.at[span], sems.at[j - 1])

    for j in range(1, SLOTS):

        @pl.when(docs.present(j))
        def _():
            part(j).start()

    for j in range(1, SLOTS):

        @pl.when(docs.present(j))
        def _():
            part(j).wait()


def small_table(small, j, p, pairs, repeat, with_masses=True):
    stride = pairs * 128 + 16
    base = (j - 1) * stride
    zero = jnp.zeros((64, 256), BF16)
    tops, bottoms = [], []
    if with_masses:
        masses = small[pl.ds(pl.multiple_of(base + pairs * 128, 16), 16), :].astype(F32)
    for k in range(2):
        head = 2 * p + k
        top = small[pl.ds(pl.multiple_of(base + head * 64, 16), 64), :]
        tops.append(jnp.concatenate([top, zero] if k == 0 else [zero, top], axis=1))
        if with_masses:
            mass = jnp.broadcast_to(masses[head : head + 1, :], (64, 256))
            if not repeat:
                mass = jnp.where(lax.broadcasted_iota(jnp.int32, (64, 256), 0) == 0, mass, 0.0)
            mass = mass.astype(BF16)
            bottoms.append(jnp.concatenate([mass, zero] if k == 0 else [zero, mass], axis=1))
    return jnp.concatenate(tops + bottoms, axis=0)


def masked(mask, value):
    wide = jnp.concatenate([mask] * (value.shape[1] // 128), axis=1)
    return jnp.where(wide, value.astype(F32), 0.0)


def keys_kernel(
    meta, x, key_weight, value_weight, bias, table,
    phi, values, scaled_out, main, small_out,
    acc, macc, sacc, smacc, small, sems, info,
):
    t = pl.program_id(0)
    docs = Documents(meta, info, x.shape[0])
    pairs = table.shape[0]
    width = pairs * 128

    @pl.when(t == 0)
    def _():
        docs.setup()
        acc[...] = jnp.zeros_like(acc)
        macc[...] = jnp.zeros_like(macc)

        for j in range(1, SLOTS):

            @pl.when(docs.present(j))
            def _():
                sacc[j - 1] = jnp.zeros_like(sacc[j - 1])
                smacc[j - 1] = jnp.zeros_like(smacc[j - 1])

    slow = docs.slow()
    keys = nn(x[...], key_weight[:, :width]) + bias[:, width : 2 * width]
    values[...] = (nn(x[...], value_weight[...]) + bias[:, 2 * width :]).astype(BF16)
    for p in range(pairs):
        scaled = keys[:, p * 128 : (p + 1) * 128] * 64 ** (-0.25)
        scaled_out[:, p * 128 : (p + 1) * 128] = scaled.astype(BF16)
        phi[:, p * 512 : (p + 1) * 512] = features(scaled, table[p]).astype(BF16)

    @pl.when(jnp.logical_not(slow))
    def _():
        for p in range(pairs):
            part = phi[:, p * 512 : (p + 1) * 512]
            acc[p] += tn(values[:, p * 128 : (p + 1) * 128], part)
            macc[p] += fold_rows(part.astype(F32))

    @pl.when(slow)
    def _():
        mask = docs.main()
        for p in range(pairs):
            part = phi[:, p * 512 : (p + 1) * 512]
            acc[p] += tn(masked(mask, values[:, p * 128 : (p + 1) * 128]).astype(BF16), part)
            macc[p] += fold_rows(masked(mask, part))

        def body(rows, mask, j):
            for p in range(pairs):
                part = phi[rows, p * 512 : (p + 1) * 512]
                value = masked(mask, values[rows, p * 128 : (p + 1) * 128]).astype(BF16)
                sacc[j - 1, p] += tn(value, part)
                smacc[j - 1, p] += fold_rows(masked(mask, part))

        docs.each_small(body)

    @pl.when(t == pl.num_programs(0) - 1)
    def _():
        pack_tables(main, 0, acc, macc)

        for j in range(1, SLOTS):

            @pl.when(docs.present(j))
            def _():
                pack_tables(small, (j - 1) * main.shape[0], sacc.at[j - 1], smacc.at[j - 1])

        copy_small(docs, small, small_out, sems)


def queries_kernel(meta, x, weight, bias, table, select, phi, scaled_out, chosen):
    pairs = table.shape[0]
    query = nn(x[...], weight[...]) + bias[:, : pairs * 128]
    chosen[...] = nn(x[...], select[...]).astype(BF16)
    for p in range(pairs):
        scaled = query[:, p * 128 : (p + 1) * 128] * 64 ** (-0.25)
        scaled_out[:, p * 128 : (p + 1) * 128] = scaled.astype(BF16)
        phi[:, p * 512 : (p + 1) * 512] = features(scaled, table[p]).astype(BF16)


def center(z):
    average = jnp.mean(z, axis=1, keepdims=True)
    centered = z - average
    inverse = lax.rsqrt(jnp.mean(centered * centered, axis=1, keepdims=True) + EPSILON)
    return centered * inverse, inverse


def center_back(e, normed, inverse):
    first = jnp.mean(e, axis=1, keepdims=True)
    second = jnp.mean(e * normed, axis=1, keepdims=True)
    return inverse * (e - first - normed * second)


def middle_kernel(
    meta, x, cot, phi, main, small_in,
    out_weight, up_own, up_here, up_there, down_own, down_here, down_there, bias_own, bias_other, vectors,
    layer_out, hidden_grad, normed_out, inverse_out, att_out, invden_out,
    active_out, dup_out, hidden_out, dffn_out, sums, up_sum,
    tabs, spread, gates, other, up_other, down_other, small, sems, half_sems, info,
):
    t = pl.program_id(0)
    docs = Documents(meta, info, x.shape[0])
    pairs = tabs.shape[0]
    width = pairs * 128
    core = meta[SLOTS + 1]

    def halves():
        copies = []
        for target, here, there in [(up_other, up_here, up_there), (down_other, down_here, down_there)]:
            count = here.shape[0]
            for source, place in [(here, core), (there, 1 - core)]:
                span = pl.ds(pl.multiple_of(place * count, count), count)
                copies.append((source, target.at[span]))
        return [
            pltpu.make_async_copy(source, target, half_sems.at[i])
            for i, (source, target) in enumerate(copies)
        ]

    @pl.when(t == 0)
    def _():
        for copy in halves():
            copy.start()
        docs.setup()
        fill_tables(tabs, main, True)
        copy_small(docs, small_in, small, sems)
        sums[...] = jnp.zeros_like(sums)
        up_sum[...] = jnp.zeros_like(up_sum)

    for p in range(pairs):
        spread[:, p * 256 : (p + 1) * 256] = nt(phi[:, p * 512 : (p + 1) * 512], tabs[p])

    @pl.when(docs.slow())
    def _():
        def body(rows, mask, j):
            wide = jnp.concatenate([mask] * 2, axis=1)
            for p in range(pairs):
                got = nt(phi[rows, p * 512 : (p + 1) * 512], small_table(small, j, p, pairs, True))
                old = spread[rows, p * 256 : (p + 1) * 256]
                spread[rows, p * 256 : (p + 1) * 256] = jnp.where(wide, got, old)

        docs.each_small(body)

    live = docs.live()
    for p in range(pairs):
        numerator = spread[:, p * 256 : p * 256 + 128]
        denominator = spread[:, p * 256 + 128 : (p + 1) * 256]
        inverse = jnp.where(live, 1.0 / jnp.where(live, denominator, 1.0), 0.0)
        invden_out[:, p * 128 : (p + 1) * 128] = inverse
        att_out[:, p * 128 : (p + 1) * 128] = (numerator * inverse).astype(BF16)

    def vector(i):
        return vectors[i : i + 1, :]

    branch = nn(att_out[...], out_weight[...]) + vector(0)
    first, first_inverse = center(x[...].astype(F32) + branch)
    normed_out[...] = first
    inverse_out[...] = jnp.broadcast_to(first_inverse, inverse_out.shape)
    hidden = first * vector(1) + vector(2)
    hidden_low = hidden.astype(BF16)
    hidden_out[...] = hidden_low
    step = 512
    half = up_own.shape[1]

    @pl.when(t == 0)
    def _():
        for copy in halves():
            copy.wait()

    for which, (up, bias, act) in enumerate(
        [(up_own, bias_own, active_out), (up_other, bias_other, other)]
    ):
        for c in range(0, half, step):
            value = nn(hidden_low, up[:, c : c + step]) + bias[:, c : c + step]
            cdf = 0.5 + 0.5 * lax.erf(value * math.sqrt(0.5))
            gates[:, which * half + c : which * half + c + step] = cdf + value * jnp.exp2(
                value * value * (-0.5 * LOG2E)
            ) * (1.0 / math.sqrt(2.0 * math.pi))
            act[:, c : c + step] = (value * cdf).astype(BF16)
    total = hidden + vector(3)
    total = total + nn(active_out[...], down_own[...])
    total = total + nn(other[...], down_other[...])
    second, second_inverse = center(total)
    layer_out[...] = (second * vector(4) + vector(5)).astype(BF16)
    g = cot[...].astype(F32)
    sums[0:8, :] += fold_rows(g * second)
    sums[8:16, :] += fold_rows(g)
    dsecond = center_back(g * vector(4), second, second_inverse)
    dffn = dsecond.astype(BF16)
    dffn_out[...] = dffn
    sums[16:24, :] += fold_rows(dffn.astype(F32))
    for which, (down, dup_ref) in enumerate([(down_own, dup_out), (down_other, other)]):
        for c in range(0, half, step):
            gate = gates[:, which * half + c : which * half + c + step]
            dup = (nt(dffn, down[c : c + step, :]) * gate).astype(BF16)
            dup_ref[:, c : c + step] = dup
            if which == 0:
                up_sum[:, c : c + step] += fold_rows(dup.astype(F32))
    dsecond = dsecond + nt(dup_out[...], up_own[...])
    dsecond = dsecond + nt(other[...], up_other[...])
    hidden_grad[...] = dsecond


def attention_back_kernel(
    meta, hidden_grad, normed, inverse, att, invden, phi, out_weight, gain, select, more, up_sum,
    dfirst_out, dbranch_out, mixed, chosen, sums, main, small_out,
    acc, sacc, small, sems, info,
):
    t = pl.program_id(0)
    docs = Documents(meta, info, att.shape[0])
    pairs = acc.shape[0]

    @pl.when(t == 0)
    def _():
        docs.setup()
        acc[...] = jnp.zeros_like(acc)
        sums[...] = jnp.zeros_like(sums)

        for j in range(1, SLOTS):

            @pl.when(docs.present(j))
            def _():
                sacc[j - 1] = jnp.zeros_like(sacc[j - 1])

    grad = hidden_grad[...]
    first = normed[...]
    sums[0:8, :] += fold_rows(grad * first)
    sums[8:16, :] += fold_rows(grad)
    dfirst = center_back(grad * gain[...], first, inverse[:, 0:1])
    dfirst_out[...] = dfirst
    dbranch = dfirst.astype(BF16)
    dbranch_out[...] = dbranch
    sums[16:24, :] += fold_rows(dbranch.astype(F32))
    chosen[...] = nn(att[...], select[...]).astype(BF16)
    slow = docs.slow()
    datt = nt(dbranch, out_weight[...])
    ratio = datt * invden[...]
    dden = -ratio * att[...].astype(F32)
    for p in range(pairs):
        mixed[:, p * 256 : p * 256 + 128] = ratio[:, p * 128 : (p + 1) * 128].astype(BF16)
        mixed[:, p * 256 + 128 : (p + 1) * 256] = dden[:, p * 128 : (p + 1) * 128].astype(BF16)

    @pl.when(jnp.logical_not(slow))
    def _():
        for p in range(pairs):
            acc[p] += tn(mixed[:, p * 256 : (p + 1) * 256], phi[:, p * 512 : (p + 1) * 512])

    @pl.when(slow)
    def _():
        mask = docs.main()
        for p in range(pairs):
            part = masked(mask, mixed[:, p * 256 : (p + 1) * 256]).astype(BF16)
            acc[p] += tn(part, phi[:, p * 512 : (p + 1) * 512])

        def body(rows, mask, j):
            for p in range(pairs):
                part = masked(mask, mixed[rows, p * 256 : (p + 1) * 256]).astype(BF16)
                sacc[j - 1, p] += tn(part, phi[rows, p * 512 : (p + 1) * 512])

        docs.each_small(body)

    @pl.when(t == pl.num_programs(0) - 1)
    def _():
        pack_tables(main, 0, acc, None)
        lines = []
        for source in (sums, more, up_sum):
            for i in range(source.shape[0] // 8):
                line = jnp.sum(source[8 * i : 8 * i + 8, :], axis=0, keepdims=True)
                lines += [line[:, c : c + 256] for c in range(0, source.shape[1], 256)]
        lines.append(jnp.zeros((EXTRA - len(lines), 256), F32))
        main[pl.ds(pairs * 128 + 16, EXTRA), :] = jnp.concatenate(lines, axis=0).astype(BF16)

        for j in range(1, SLOTS):

            @pl.when(docs.present(j))
            def _():
                pack_tables(small, (j - 1) * (pairs * 128 + 16), sacc.at[j - 1], None)

        copy_small(docs, small, small_out, sems)


def feature_back(rows, p, grad, phi, scaled, table):
    span = slice(p * 128, (p + 1) * 128)
    e = (grad * phi[rows, p * 512 : (p + 1) * 512].astype(F32)).astype(BF16)
    back = nt(e, table[p])
    return (back[:, :128] - scaled[rows, span].astype(F32) * back[:, 128:]) * 64 ** (-0.25)


def store_some(ref, rows, span, mask, value):
    old = ref[rows, span].astype(F32)
    ref[rows, span] = jnp.where(mask, value, old).astype(ref.dtype)


def queries_back_kernel(
    meta, mixed, phi, scaled, main, small_in, table, weight, dfirst,
    dquery_out, partial_out, sums, tabs, small, sems, info,
):
    t = pl.program_id(0)
    docs = Documents(meta, info, phi.shape[0])
    pairs = tabs.shape[0]

    @pl.when(t == 0)
    def _():
        docs.setup()
        fill_tables(tabs, main, True)
        copy_small(docs, small_in, small, sems)
        sums[...] = jnp.zeros_like(sums)

    for p in range(pairs):
        grad = nn(mixed[:, p * 256 : (p + 1) * 256], tabs[p])
        du = feature_back(slice(None), p, grad, phi, scaled, table)
        dquery_out[:, p * 128 : (p + 1) * 128] = du.astype(BF16)

    @pl.when(docs.slow())
    def _():
        def body(rows, mask, j):
            for p in range(pairs):
                own = small_table(small, j, p, pairs, True)
                grad = nn(mixed[rows, p * 256 : (p + 1) * 256], own)
                du = feature_back(rows, p, grad, phi, scaled, table)
                store_some(dquery_out, rows, slice(p * 128, (p + 1) * 128), mask, du)

        docs.each_small(body)

    sums[...] += fold_rows(dquery_out[...].astype(F32))
    partial_out[...] = dfirst[...] + nt(dquery_out[...], weight[...])


def keys_back_kernel(
    meta, phi, values, scaled, main, small_in, table, key_weight, value_weight, partial_in,
    djoint_out, tokens_out, sums, tabs, small, sems, info,
):
    t = pl.program_id(0)
    docs = Documents(meta, info, phi.shape[0])
    pairs = tabs.shape[0]
    width = pairs * 128

    @pl.when(t == 0)
    def _():
        docs.setup()
        fill_tables(tabs, main, False)
        copy_small(docs, small_in, small, sems)
        sums[...] = jnp.zeros_like(sums)

    def extended(rows, p):
        value = values[rows, p * 128 : (p + 1) * 128]
        return jnp.concatenate([value, jnp.ones_like(value)], axis=1)

    for p in range(pairs):
        grad = nn(extended(slice(None), p), tabs[p])
        du = feature_back(slice(None), p, grad, phi, scaled, table)
        djoint_out[:, p * 128 : (p + 1) * 128] = du.astype(BF16)
        dvalue = nt(phi[:, p * 512 : (p + 1) * 512], tabs[p, :128, :])
        djoint_out[:, width + p * 128 : width + (p + 1) * 128] = dvalue.astype(BF16)

    @pl.when(docs.slow())
    def _():
        live = docs.live()
        for p in range(2 * pairs):
            part = djoint_out[:, p * 128 : (p + 1) * 128]
            djoint_out[:, p * 128 : (p + 1) * 128] = masked(live, part).astype(BF16)

        def body(rows, mask, j):
            for p in range(pairs):
                own = small_table(small, j, p, pairs, False)
                grad = nn(extended(rows, p), own)
                du = feature_back(rows, p, grad, phi, scaled, table)
                store_some(djoint_out, rows, slice(p * 128, (p + 1) * 128), mask, du)
                dvalue = nt(phi[rows, p * 512 : (p + 1) * 512], own[:128, :])
                span = slice(width + p * 128, width + (p + 1) * 128)
                store_some(djoint_out, rows, span, mask, dvalue)

        docs.each_small(body)

    sums[...] += fold_rows(djoint_out[...].astype(F32))
    tokens_out[...] = (
        partial_in[...]
        + nt(djoint_out[:, :width], key_weight[:, :width])
        + nt(djoint_out[:, width:], value_weight[...])
    ).astype(BF16)


def table_outs(width, extra=0):
    count = width + 16
    small = (SLOTS - 1) * count
    count = count + extra
    anywhere = pl.BlockSpec(memory_space=pl.ANY)
    return [(held((count, 256)), (count, 256), BF16), (anywhere, (small, 256), BF16)]


def table_ins(width):
    return [full((width + 16, 256)), pl.BlockSpec(memory_space=pl.ANY)]


def table_scratch(width):
    return pltpu.VMEM((width // 128, 256, 512), BF16)


def small_scratch(width):
    return pltpu.VMEM(((SLOTS - 1) * (width + 16), 256), BF16)


def run_keys(tile, meta, tokens, key_weight, value_weight, bias, table):
    count, width = tokens.shape
    pairs = table.shape[0]
    wide = pairs * 512
    return call(
        keys_kernel,
        count // tile,
        [
            rows(tile, width), full(key_weight.shape), full((width, width)), full(bias.shape),
            full(table.shape),
        ],
        [
            (rows(tile, wide), (count, wide), BF16),
            (rows(tile, width), (count, width), BF16),
            (rows(tile, width), (count, width), BF16),
        ]
        + table_outs(width),
        [
            pltpu.VMEM((pairs, 128, 512), F32),
            pltpu.VMEM((pairs, 8, 512), F32),
            pltpu.VMEM((SLOTS - 1, pairs, 128, 512), F32),
            pltpu.VMEM((SLOTS - 1, pairs, 8, 512), F32),
            small_scratch(width),
            pltpu.SemaphoreType.DMA((SLOTS - 1,)),
            pltpu.SMEM((3 * SLOTS,), jnp.int32),
        ],
        10e9,
    )(meta, tokens, key_weight, value_weight, bias, table)


def run_queries(tile, meta, tokens, weight, bias, table, select):
    count, width = tokens.shape
    wide = table.shape[0] * 512
    own_rows = select.shape[1]
    return call(
        queries_kernel,
        count // tile,
        [
            rows(tile, width), column((width, width), 0), full(bias.shape), full(table.shape),
            full((width, own_rows)),
        ],
        [
            (rows(tile, wide), (count, wide), BF16),
            (rows(tile, width), (count, width), BF16),
            (rows(tile, own_rows), (count, own_rows), BF16),
        ],
        [],
        6e9,
    )(meta, tokens, weight, bias, table, select)


def run_middle(
    tile, meta, tokens, cotangent, phi, moments, small, query_out, up_own, up_here, up_there,
    down_own, down_here, down_there, bias_own, bias_other, vectors,
):
    count, width = tokens.shape
    half = up_own.shape[1]
    wide = phi.shape[1]
    pairs = width // 128
    return call(
        middle_kernel,
        count // tile,
        [rows(tile, width), rows(tile, width), rows(tile, wide)]
        + table_ins(width)
        + [
            column((width, width), 1),
            full((width, half)),
            pl.BlockSpec(memory_space=pl.ANY),
            pl.BlockSpec(memory_space=pl.ANY),
            full((half, width)),
            pl.BlockSpec(memory_space=pl.ANY),
            pl.BlockSpec(memory_space=pl.ANY),
            full((1, half)),
            full((1, half)),
            full((8, width)),
        ],
        [
            (rows(tile, width), (count, width), BF16),
            (rows(tile, width), (count, width), F32),
            (rows(tile, width), (count, width), F32),
            (rows(tile, 128), (count, 128), F32),
            (rows(tile, width), (count, width), BF16),
            (rows(tile, width), (count, width), F32),
            (rows(tile, half), (count, half), BF16),
            (rows(tile, half), (count, half), BF16),
            (rows(tile, width), (count, width), BF16),
            (rows(tile, width), (count, width), BF16),
            (held((24, width)), (24, width), F32),
            (held((8, half)), (8, half), F32),
        ],
        [
            table_scratch(width),
            pltpu.VMEM((tile, pairs * 256), F32),
            pltpu.VMEM((tile, 2 * half), F32),
            pltpu.VMEM((tile, half), BF16),
            pltpu.VMEM((width, half), BF16),
            pltpu.VMEM((half, width), BF16),
            small_scratch(width),
            pltpu.SemaphoreType.DMA((SLOTS - 1,)),
            pltpu.SemaphoreType.DMA((4,)),
            pltpu.SMEM((3 * SLOTS,), jnp.int32),
        ],
        30e9,
    )(
        meta, tokens, cotangent, phi, moments, small, query_out, up_own, up_here, up_there,
        down_own, down_here, down_there, bias_own, bias_other, vectors,
    )


def run_attention_back(
    tile, meta, hidden_grad, normed, inverse, att, invden, phi, query_out, gain, select, sums, up_sum
):
    count, width = att.shape
    wide = phi.shape[1]
    pairs = width // 128
    own_rows = select.shape[1]
    half = up_sum.shape[1]
    return call(
        attention_back_kernel,
        count // tile,
        [
            rows(tile, width), rows(tile, width), rows(tile, 128), rows(tile, width), rows(tile, width),
            rows(tile, wide), column((width, width), 1), full((1, width)), full((width, own_rows)),
            full((24, width)), full((8, half)),
        ],
        [
            (rows(tile, width), (count, width), F32),
            (rows(tile, width), (count, width), BF16),
            (rows(tile, 2 * width), (count, 2 * width), BF16),
            (rows(tile, own_rows), (count, own_rows), BF16),
            (held((24, width)), (24, width), F32),
        ]
        + table_outs(width, EXTRA),
        [
            pltpu.VMEM((pairs, 256, 512), F32),
            pltpu.VMEM((SLOTS - 1, pairs, 256, 512), F32),
            small_scratch(width),
            pltpu.SemaphoreType.DMA((SLOTS - 1,)),
            pltpu.SMEM((3 * SLOTS,), jnp.int32),
        ],
        6e9,
    )(
        meta, hidden_grad, normed, inverse, att, invden, phi, query_out, gain, select, sums, up_sum
    )


def run_queries_back(tile, meta, mixed, phi, scaled, moments, small, table, weight, dfirst):
    count, width = scaled.shape
    wide = phi.shape[1]
    return call(
        queries_back_kernel,
        count // tile,
        [rows(tile, 2 * width), rows(tile, wide), rows(tile, width)]
        + table_ins(width)
        + [full(table.shape), column((width, width), 0), rows(tile, width)],
        [
            (rows(tile, width), (count, width), BF16),
            (rows(tile, width), (count, width), F32),
            (held((8, width)), (8, width), F32),
        ],
        [
            table_scratch(width),
            small_scratch(width),
            pltpu.SemaphoreType.DMA((SLOTS - 1,)),
            pltpu.SMEM((3 * SLOTS,), jnp.int32),
        ],
        8e9,
    )(meta, mixed, phi, scaled, moments, small, table, weight, dfirst)


def run_keys_back(
    tile, meta, phi, values, scaled, moments, small, table, key_weight, value_weight, partial
):
    count, width = scaled.shape
    wide = phi.shape[1]
    return call(
        keys_back_kernel,
        count // tile,
        [rows(tile, wide), rows(tile, width), rows(tile, width)]
        + table_ins(width)
        + [full(table.shape), full(key_weight.shape), full((width, width)), rows(tile, width)],
        [
            (rows(tile, 2 * width), (count, 2 * width), BF16),
            (rows(tile, width), (count, width), BF16),
            (held((8, 2 * width)), (8, 2 * width), F32),
        ],
        [
            table_scratch(width),
            small_scratch(width),
            pltpu.SemaphoreType.DMA((SLOTS - 1,)),
            pltpu.SMEM((3 * SLOTS,), jnp.int32),
        ],
        12e9,
    )(
        meta, phi, values, scaled, moments, small, table, key_weight, value_weight, partial,
    )


def local(
    tokens, document_lengths, feature_maps, joint_weight, joint_bias, output_weight, output_bias,
    first_gain, first_shift, up_weight, up_bias, down_weight, down_bias, second_gain, second_shift,
    cotangent,
):
    count, width = tokens.shape
    heads, head_size, feature_count = feature_maps.shape
    pairs = heads // 2
    half = up_weight.shape[1]
    rank = lax.axis_index("dp")
    dp = lax.axis_size("dp")
    mp = lax.axis_size("mp")
    mp_rank = lax.axis_index("mp")

    shard = joint_weight.shape[0]
    small_vectors = [joint_bias, output_bias, first_gain, first_shift, second_gain, second_shift]
    stacks = -(-len(small_vectors) // shard)
    small_vectors = jnp.stack([jnp.pad(v, (0, 128 - v.shape[0])) for v in small_vectors])
    small_vectors = jnp.pad(small_vectors, ((0, stacks * shard - small_vectors.shape[0]), (0, 0)))
    small_vectors = jnp.concatenate(
        [small_vectors[i * shard : (i + 1) * shard] for i in range(stacks)], axis=1
    )
    core = mine(1)

    def own_part(a):
        return lax.dynamic_slice_in_dim(a, core * (a.shape[0] // 2), a.shape[0] // 2, 0)

    far_weight = swap_mp(joint_weight)
    far_vectors = swap_mp(small_vectors)

    def over_x(own, other):
        return join_pair(own, other, mp_rank, 0).reshape(2 * shard, -1)

    value_chain = Gather(
        over_x(joint_weight[:, 2 * width :], far_weight[:, 2 * width :]), near_first()
    ).start()
    key_chain = Gather(
        jnp.concatenate(
            [
                over_x(joint_weight[:, width : 2 * width], far_weight[:, width : 2 * width]),
                over_x(small_vectors, far_vectors),
            ],
            axis=1,
        ),
        far_first(),
    ).start()
    early = key_chain.a
    query_out = lax.all_gather(
        after(jnp.concatenate([joint_weight[:, :width], output_weight], axis=1), early),
        ("dp", "mp"),
        axis=0,
        tiled=True,
    )
    up_here = swap_mp(after(own_part(up_weight), early))
    down_here = swap_mp(after(own_part(down_weight), early))
    meta = jnp.concatenate(
        [
            document_lengths[0],
            jnp.stack([rank * count, core]).astype(jnp.int32),
            jnp.zeros((SLOTS - 2,), jnp.int32),
        ]
    )

    key_chain.finish()
    value_chain.finish()
    while key_chain.order:
        value_chain.start()
        key_chain.start()
        key_chain.finish()
        value_chain.finish()
    key_weight = key_chain.result()
    value_weight = value_chain.result()

    vectors_all = key_weight[:, width:].reshape(dp * mp, shard, stacks * 128)

    def vector(i, size):
        start = i // shard * 128
        return vectors_all[:, i % shard, start : start + size].reshape(-1).astype(F32)

    joint_offset = vector(0, joint_bias.shape[0])[None, :]
    bias_own = up_bias[None, :].astype(F32)

    pair_maps = feature_maps.reshape(pairs, 2, head_size, feature_count)
    blank = jnp.zeros_like(pair_maps[:, 0])
    table = jnp.concatenate(
        [
            jnp.concatenate([pair_maps[:, 0], blank], axis=2),
            jnp.concatenate([blank, pair_maps[:, 1]], axis=2),
            jnp.concatenate([blank + 1, blank], axis=2),
            jnp.concatenate([blank, blank + 1], axis=2),
        ],
        axis=1,
    )
    bits = dp_bits()
    far, middle_bits, near = bits[0], bits[1:-2], bits[-2:-1]
    owner_order = [1] + near + middle_bits + [far]
    own_rows = width // mp
    index = jnp.arange(own_rows, dtype=jnp.int32)
    owner = sum(
        (index // shard // (dp // 2 >> place)) % 2 * bit for place, bit in enumerate(owner_order)
    )
    source = owner * (shard * mp) + mp_rank * shard + index % shard
    select = (jnp.arange(width, dtype=jnp.int32)[:, None] == source[None, :]).astype(BF16)

    phi_k, values, scaled_k, moments, small_moments = run_keys(
        TILE, meta, tokens, key_weight, value_weight, joint_offset, table
    )

    up_there = swap_dp(after(up_here, moments), 1)
    down_there = swap_dp(after(down_here, up_there), 1)
    bias_other = swap_mp(after(up_bias, moments)[None, :]).astype(F32)
    vectors_all = after(vectors_all, moments)
    parts = [vector(i, shard) for i in range(1, 6)]
    vectors = jnp.stack(
        [parts[0], parts[1], parts[2], down_bias.astype(F32), parts[3], parts[4], parts[4], parts[4]]
    )
    others = middle_bits + near
    moments_sum = TableSum(moments).add()
    for bit in reversed(others):
        moments_sum.swap(bit).add()
    moments_sum.swap(far)
    phi_q, scaled_q, tokens_own = run_queries(
        TILE, meta, after(tokens, moments_sum.own), query_out, joint_offset, table, select
    )
    moments = moments_sum.add(phi_q).swap(1).join()
    (
        layer_output, hidden_grad, normed, inverse, att, invden, active, dup, hidden_low, dffn, sums, up_sum,
    ) = run_middle(
        TILE, meta, tokens, cotangent, phi_q, moments, small_moments, query_out, up_weight,
        up_here, up_there, down_weight, down_here, down_there, bias_own, bias_other, vectors,
    )

    dfirst, dbranch, mixed, att_own, first_sums, dmoments, small_dmoments = run_attention_back(
        TILE, meta, hidden_grad, normed, inverse, att, invden, phi_q, query_out, vectors[1:2],
        select, sums, up_sum,
    )

    dmoments_sum = TableSum(dmoments)
    down_grad = tn(after(active, dmoments), dffn).astype(BF16)
    down = Sum(down_grad, [1] + near + middle_bits)
    dmoments_sum.add(down_grad)
    first_bit = True
    for bit in middle_bits:
        dmoments_sum.swap(bit)
        if first_bit:
            down.start(dmoments_sum.own)
            up_grad = tn(after(hidden_low, dmoments_sum.own), dup).astype(BF16)
            up = Sum(up_grad, [1] + middle_bits + near)
            down.finish(up_grad)
            up.start(down.a)
            down.start()
            out_grad = tn(after(att_own, up_grad), dbranch).astype(BF16)
            up.finish(out_grad)
            dmoments_sum.add(up.a)
            first_bit = False
        else:
            dmoments_sum.add()
    dmoments_sum.swap(far)
    up.start(dmoments_sum.own)
    dquery, partial_tokens, query_sums = run_queries_back(
        TILE, meta, mixed, phi_q, scaled_q, moments, small_moments, table, query_out,
        after(dfirst, dmoments_sum.own, up.own),
    )
    dmoments_sum.add(dquery).swap(near[0])
    down.finish(dmoments_sum.own).start()
    up.finish(down.a).start()
    query_grad = tn(after(tokens_own, up.a), dquery).astype(BF16)
    dmoments_sum.add(query_grad).swap(1)
    query_out_sum = Sum(jnp.concatenate([query_grad, out_grad], axis=1), owner_order)
    query_out_sum.start(dmoments_sum.own)
    dmoments = dmoments_sum.join(query_out_sum.own)
    down.finish(query_out_sum.own)
    up.finish(down.a)
    while down.order:
        down.start().finish()
        up.start().finish()
    down.start_swap(far)
    up.start_swap(far, down.a)
    query_out_sum.finish(up.a).start()
    dkey_value, tokens_grad, key_sums = run_keys_back(
        TILE, meta, phi_k, values, scaled_k, dmoments, small_dmoments, table, key_weight,
        value_weight, after(partial_tokens, query_out_sum.own, up.own, down.own),
    )
    down.finish_swap(dkey_value).start_back()
    up.finish_swap(down.a).start_back()
    key_value_grad = tn(after(tokens_own, up.a), dkey_value).astype(BF16)
    biases = jnp.concatenate([jnp.sum(query_sums, axis=0), jnp.sum(key_sums, axis=0)])
    per_owner = biases.shape[0] // dp
    biases = biases.reshape((2,) * len(bits) + (-1,))
    biases = biases.transpose([bits.index(bit) for bit in owner_order] + [len(bits)])
    biases = biases.reshape(dp * shard, -1)
    bias_columns = biases.shape[1]
    biases = jnp.pad(biases, ((0, 0), (0, 128 - bias_columns))).astype(BF16)
    key_value_sum = Sum(jnp.concatenate([key_value_grad, biases], axis=1), owner_order).start()
    query_out_sum.finish(key_value_sum.own).start()
    key_value_sum.finish(query_out_sum.own).start()
    while len(down.done) > 1:
        down.finish_back(key_value_sum.own).start_back()
        up.finish_back(down.a).start_back()
        if query_out_sum.order:
            query_out_sum.finish(up.a)
            if query_out_sum.order:
                query_out_sum.start()
        key_value_sum.finish(up.a)
        if key_value_sum.order:
            key_value_sum.start()
    down_total = down.finish_back(key_value_sum.own).a
    up_total = up.finish_back(down_total).a
    if query_out_sum.order:
        query_out_sum.finish(up.a)
    query_out_total = query_out_sum.rest().astype(F32)
    if key_value_sum.order:
        key_value_sum.finish(up.a)
    key_value_total = key_value_sum.rest().astype(F32)

    extra = dmoments[width + 16 :].reshape(-1).astype(F32)

    def owned(place, size=width):
        part = size // (dp * mp)
        start = place * width + (rank * mp + mp_rank) * part
        return lax.dynamic_slice_in_dim(extra, start, part, 0)

    bias_total = key_value_total[:, 2 * width : 2 * width + bias_columns].reshape(mp, -1)
    bias_total = lax.dynamic_index_in_dim(bias_total, mp_rank, 0, False)

    return (
        layer_output,
        tokens_grad,
        jnp.concatenate([query_out_total[:, :width], key_value_total[:, : 2 * width]], axis=1),
        bias_total,
        query_out_total[:, width:],
        owned(2),
        owned(0),
        owned(1),
        up_total.astype(F32),
        extra[6 * width : 6 * width + half],
        down_total.astype(F32),
        extra[5 * width : 6 * width],
        owned(3),
        owned(4),
    )


def solution(mesh):
    shared = P(("dp", "mp"))
    in_specs = (
        P("dp", None), P(), P(), P(("dp", "mp"), None), shared, P(("dp", "mp"), None), shared, shared,
        shared, P(None, "mp"), P("mp"), P("mp", None), P(), shared, shared, P("dp", None),
    )
    out_specs = (
        P("dp", None), P("dp", None), P(("dp", "mp"), None), shared, P(("dp", "mp"), None), shared,
        shared, shared, P(None, "mp"), P("mp"), P("mp", None), P(), shared, shared,
    )
    return jax.shard_map(local, mesh=mesh, in_specs=in_specs, out_specs=out_specs, check_vma=False)
```

```python
from functools import partial
import math

import jax
import jax.numpy as jnp
from jax import lax
from jax.experimental import pallas as pl
from jax.experimental.pallas import tpu as pltpu
from jax.sharding import PartitionSpec as P

EPSILON = 1e-05
F32 = jnp.float32
BF16 = jnp.bfloat16
LOG2E = math.log2(math.e)
VMEM_LIMIT = 56 * 1024 * 1024
SLOTS = 8
WINDOW = 128
EXTRA = 32
TILE = 256


def nn(a, b):
    return lax.dot_general(a, b, (((1,), (0,)), ((), ())), preferred_element_type=F32)


def nt(a, b):
    return lax.dot_general(a, b, (((1,), (1,)), ((), ())), preferred_element_type=F32)


def tn(a, b):
    return lax.dot_general(a, b, (((0,), (0,)), ((), ())), preferred_element_type=F32)


def fold_rows(a):
    return jnp.sum(a.reshape(a.shape[0] // 8, 8, a.shape[1]), axis=0)


def after(value, *deps):
    return lax.optimization_barrier((value, deps))[0]


def dp_bits():
    count = lax.axis_size("dp")
    bits = []
    bit = count // 2
    while bit:
        bits.append(bit)
        bit //= 2
    return bits


def far_first():
    return dp_bits()


def near_first():
    bits = dp_bits()
    if len(bits) < 3:
        return bits
    return [bits[-2]] + bits[:-2] + [bits[-1]]


def swap_dp(a, bit):
    count = lax.axis_size("dp")
    return lax.ppermute(a, "dp", [(i, i ^ bit) for i in range(count)])


def swap_mp(a):
    return lax.ppermute(a, "mp", [(0, 1), (1, 0)])


def mine(bit):
    return (lax.axis_index("dp") // bit) % 2


def join_pair(own, other, bit, axis):
    low = jnp.stack([own, other], axis)
    high = jnp.stack([other, own], axis)
    return jnp.where(bit == 0, low, high)


class Gather:
    def __init__(self, a, order, done=()):
        self.a = a
        self.tail = a.shape[len(done) :]
        self.order = list(order)
        self.done = list(done)
        self.got = None

    def start(self, *deps):
        if deps:
            self.a = after(self.a, *deps)
        self.got = swap_dp(self.a, self.order[0])
        return self

    def finish(self, *deps):
        bit = self.order.pop(0)
        got = after(self.got, *deps) if deps else self.got
        place = sum(1 for d in self.done if d > bit)
        self.a = join_pair(self.a, got, mine(bit), place)
        self.done.append(bit)
        return self

    def rest(self):
        while self.order:
            self.start().finish()
        return self.result()

    def result(self):
        return self.a.reshape((-1,) + self.tail[1:])


class Sum:
    def __init__(self, a, order):
        self.a = a
        self.order = list(order)
        self.done = []

    def start(self, *deps):
        bit = self.order[0]
        a = after(self.a, *deps) if deps else self.a
        count = a.shape[0] // 2
        self.own = lax.dynamic_slice_in_dim(a, mine(bit) * count, count, 0)
        self.got = swap_dp(lax.dynamic_slice_in_dim(a, (1 - mine(bit)) * count, count, 0), bit)
        return self

    def finish(self, *deps):
        self.done.append(self.order.pop(0))
        got = after(self.got, *deps) if deps else self.got
        self.a = (self.own.astype(F32) + got.astype(F32)).astype(self.a.dtype)
        return self

    def rest(self):
        while self.order:
            self.start().finish()
        return self.a

    def start_swap(self, bit, *deps):
        self.own = after(self.a, *deps) if deps else self.a
        self.got = swap_dp(self.own, bit)
        return self

    def finish_swap(self, *deps):
        got = after(self.got, *deps) if deps else self.got
        self.a = (self.own.astype(F32) + got.astype(F32)).astype(self.a.dtype)
        return self

    def start_back(self):
        self.got = swap_dp(self.a, self.done[-1])
        return self

    def finish_back(self, *deps):
        got = after(self.got, *deps) if deps else self.got
        a = join_pair(self.a, got, mine(self.done.pop()), 0)
        self.a = a.reshape((-1,) + a.shape[2:])
        return self


class TableSum:
    def __init__(self, packed):
        self.core = mine(1)
        self.shape = packed.shape
        halves = packed.reshape(2, packed.shape[0] // 2, packed.shape[1])
        self.own = lax.dynamic_index_in_dim(halves, self.core, 0, False)
        self.got = swap_dp(lax.dynamic_index_in_dim(halves, 1 - self.core, 0, False), 1)

    def add(self, *deps):
        got = after(self.got, *deps) if deps else self.got
        self.own = (self.own.astype(F32) + got.astype(F32)).astype(self.own.dtype)
        return self

    def swap(self, bit):
        self.got = swap_dp(self.own, bit)
        return self

    def join(self, *deps):
        got = after(self.got, *deps) if deps else self.got
        return join_pair(self.own, got, self.core, 0).reshape(self.shape)


def full(shape):
    return pl.BlockSpec(shape, lambda t, *_: (0,) * len(shape), pipeline_mode=pl.Buffered(1))


def column(shape, place):
    return pl.BlockSpec(shape, lambda t, *_: (0, place), pipeline_mode=pl.Buffered(1))


def rows(tile, width):
    return pl.BlockSpec((tile, width), lambda t, *_: (t, 0))


def held(shape):
    return pl.BlockSpec(shape, lambda t, *_: (0,) * len(shape))


def call(kernel, tiles, in_specs, outs, scratch, flops):
    return pl.pallas_call(
        kernel,
        grid_spec=pltpu.PrefetchScalarGridSpec(
            num_scalar_prefetch=1,
            grid=(tiles,),
            in_specs=in_specs,
            out_specs=[spec for spec, _, _ in outs],
            scratch_shapes=scratch,
        ),
        out_shape=[jax.ShapeDtypeStruct(shape, kind) for _, shape, kind in outs],
        compiler_params=pltpu.CompilerParams(
            vmem_limit_bytes=VMEM_LIMIT, dimension_semantics=("arbitrary",)
        ),
        cost_estimate=pl.CostEstimate(flops=int(flops), bytes_accessed=20_000_000, transcendentals=0),
    )


def features(scaled, table):
    lhs = jnp.concatenate([scaled.astype(BF16), (-0.5 * scaled * scaled).astype(BF16)], axis=1)
    return jnp.exp2(nn(lhs, table) * LOG2E - 4.0)


class Documents:
    def __init__(self, meta, info, tile):
        self.meta, self.info, self.tile = meta, info, tile
        self.t = pl.program_id(0)

    def setup(self):
        meta, info = self.meta, self.info
        edges = [-meta[SLOTS]]
        for d in range(SLOTS):
            edges.append(edges[-1] + meta[d])
        most, longest = meta[0], jnp.int32(0)
        for d in range(1, SLOTS):
            longest = jnp.where(meta[d] > most, d, longest)
            most = jnp.maximum(most, meta[d])
        start, stop = edges[0], edges[1]
        for d in range(1, SLOTS):
            start = jnp.where(longest == d, edges[d], start)
            stop = jnp.where(longest == d, edges[d + 1], stop)
        info[0] = start
        info[SLOTS] = stop
        for j in range(1, SLOTS):
            before = longest > j - 1
            info[j] = jnp.where(before, edges[j - 1], edges[j])
            info[SLOTS + j] = jnp.where(before, edges[j], edges[j + 1])
        info[2 * SLOTS] = edges[SLOTS]

    def slow(self):
        first = self.t * self.tile
        inside = jnp.logical_and(self.info[0] <= first, self.info[SLOTS] >= first + self.tile)
        return jnp.logical_not(inside)

    def present(self, j):
        rows = self.tile * pl.num_programs(0)
        return jnp.maximum(self.info[j], 0) < jnp.minimum(self.info[SLOTS + j], rows)

    def places(self, first, rows):
        return lax.broadcasted_iota(jnp.int32, (rows, 128), 0) + (self.t * self.tile + first)

    def main(self):
        place = self.places(0, self.tile)
        return jnp.logical_and(place >= self.info[0], place < self.info[SLOTS])

    def live(self):
        return self.places(0, self.tile) < self.info[2 * SLOTS]

    def each_small(self, body):
        limit = self.tile - WINDOW
        base = self.t * self.tile

        def one(j, carry):
            first = jnp.clip(self.info[j] - base, 0, self.tile)
            final = jnp.clip(self.info[SLOTS + j] - base, 0, self.tile)
            begin = first // 16 * 16

            def window(i, carry):
                wanted = begin + i * WINDOW
                start = pl.multiple_of(jnp.minimum(wanted, limit), 16)
                place = lax.broadcasted_iota(jnp.int32, (WINDOW, 128), 0) + start
                low = jnp.maximum(first, wanted)
                body(pl.ds(start, WINDOW), jnp.logical_and(place >= low, place < final), j)
                return carry

            count = jnp.where(final > first, (final - begin + WINDOW - 1) // WINDOW, 0)
            lax.fori_loop(0, count, window, 0)
            return carry

        lax.fori_loop(1, SLOTS, one, 0)


def pack_tables(table, base, acc, macc):
    pairs = acc.shape[0]
    masses = []
    for p in range(pairs):
        for k in range(2):
            head = 2 * p + k
            span = slice(k * 256, (k + 1) * 256)
            table[pl.ds(base + head * 64, 64), :] = acc[p, k * 64 : (k + 1) * 64, span].astype(BF16)
            source = macc[p, :, span] if macc is not None else acc[p, 128 + k * 64 : 192 + k * 64, span]
            masses.append(jnp.sum(source, axis=0, keepdims=True))
    masses.append(jnp.zeros((16 - 2 * pairs, 256), F32))
    table[pl.ds(base + pairs * 128, 16), :] = jnp.concatenate(masses, axis=0).astype(BF16)


def fill_tables(tabs, main, repeat):
    pairs = tabs.shape[0]
    tabs[...] = jnp.zeros_like(tabs)
    masses = main[pl.ds(pairs * 128, 16), :].astype(F32)
    for p in range(pairs):
        for k in range(2):
            head = 2 * p + k
            span = slice(k * 256, (k + 1) * 256)
            tabs[p, k * 64 : (k + 1) * 64, span] = main[pl.ds(head * 64, 64), :]
            mass = jnp.broadcast_to(masses[head : head + 1, :], (64, 256))
            if not repeat:
                mass = jnp.where(lax.broadcasted_iota(jnp.int32, (64, 256), 0) == 0, mass, 0.0)
            tabs[p, 128 + k * 64 : 192 + k * 64, span] = mass.astype(BF16)


def copy_small(docs, source, target, sems):
    stride = source.shape[0] // (SLOTS - 1)

    def part(j):
        span = pl.ds((j - 1) * stride, stride)
        return pltpu.make_async_copy(source.at[span], target.at[span], sems.at[j - 1])

    for j in range(1, SLOTS):

        @pl.when(docs.present(j))
        def _():
            part(j).start()

    for j in range(1, SLOTS):

        @pl.when(docs.present(j))
        def _():
            part(j).wait()


def small_table(small, j, p, pairs, repeat, with_masses=True):
    stride = pairs * 128 + 16
    base = (j - 1) * stride
    zero = jnp.zeros((64, 256), BF16)
    tops, bottoms = [], []
    if with_masses:
        masses = small[pl.ds(pl.multiple_of(base + pairs * 128, 16), 16), :].astype(F32)
    for k in range(2):
        head = 2 * p + k
        top = small[pl.ds(pl.multiple_of(base + head * 64, 16), 64), :]
        tops.append(jnp.concatenate([top, zero] if k == 0 else [zero, top], axis=1))
        if with_masses:
            mass = jnp.broadcast_to(masses[head : head + 1, :], (64, 256))
            if not repeat:
                mass = jnp.where(lax.broadcasted_iota(jnp.int32, (64, 256), 0) == 0, mass, 0.0)
            mass = mass.astype(BF16)
            bottoms.append(jnp.concatenate([mass, zero] if k == 0 else [zero, mass], axis=1))
    return jnp.concatenate(tops + bottoms, axis=0)


def masked(mask, value):
    wide = jnp.concatenate([mask] * (value.shape[1] // 128), axis=1)
    return jnp.where(wide, value.astype(F32), 0.0)


def keys_kernel(
    meta, x, key_weight, value_weight, bias, table,
    phi, values, scaled_out, main, small_out,
    acc, macc, sacc, smacc, small, sems, info,
):
    t = pl.program_id(0)
    docs = Documents(meta, info, x.shape[0])
    pairs = table.shape[0]
    width = pairs * 128

    @pl.when(t == 0)
    def _():
        docs.setup()
        acc[...] = jnp.zeros_like(acc)
        macc[...] = jnp.zeros_like(macc)

        for j in range(1, SLOTS):

            @pl.when(docs.present(j))
            def _():
                sacc[j - 1] = jnp.zeros_like(sacc[j - 1])
                smacc[j - 1] = jnp.zeros_like(smacc[j - 1])

    slow = docs.slow()
    keys = nn(x[...], key_weight[:, :width]) + bias[:, width : 2 * width]
    values[...] = (nn(x[...], value_weight[...]) + bias[:, 2 * width :]).astype(BF16)
    for p in range(pairs):
        scaled = keys[:, p * 128 : (p + 1) * 128] * 64 ** (-0.25)
        scaled_out[:, p * 128 : (p + 1) * 128] = scaled.astype(BF16)
        phi[:, p * 512 : (p + 1) * 512] = features(scaled, table[p]).astype(BF16)

    @pl.when(jnp.logical_not(slow))
    def _():
        for p in range(pairs):
            part = phi[:, p * 512 : (p + 1) * 512]
            acc[p] += tn(values[:, p * 128 : (p + 1) * 128], part)
            macc[p] += fold_rows(part.astype(F32))

    @pl.when(slow)
    def _():
        mask = docs.main()
        for p in range(pairs):
            part = phi[:, p * 512 : (p + 1) * 512]
            acc[p] += tn(masked(mask, values[:, p * 128 : (p + 1) * 128]).astype(BF16), part)
            macc[p] += fold_rows(masked(mask, part))

        def body(rows, mask, j):
            for p in range(pairs):
                part = phi[rows, p * 512 : (p + 1) * 512]
                value = masked(mask, values[rows, p * 128 : (p + 1) * 128]).astype(BF16)
                sacc[j - 1, p] += tn(value, part)
                smacc[j - 1, p] += fold_rows(masked(mask, part))

        docs.each_small(body)

    @pl.when(t == pl.num_programs(0) - 1)
    def _():
        pack_tables(main, 0, acc, macc)

        for j in range(1, SLOTS):

            @pl.when(docs.present(j))
            def _():
                pack_tables(small, (j - 1) * main.shape[0], sacc.at[j - 1], smacc.at[j - 1])

        copy_small(docs, small, small_out, sems)


def queries_kernel(meta, x, weight, bias, table, select, phi, scaled_out, chosen):
    pairs = table.shape[0]
    query = nn(x[...], weight[...]) + bias[:, : pairs * 128]
    chosen[...] = nn(x[...], select[...]).astype(BF16)
    for p in range(pairs):
        scaled = query[:, p * 128 : (p + 1) * 128] * 64 ** (-0.25)
        scaled_out[:, p * 128 : (p + 1) * 128] = scaled.astype(BF16)
        phi[:, p * 512 : (p + 1) * 512] = features(scaled, table[p]).astype(BF16)


def center(z):
    average = jnp.mean(z, axis=1, keepdims=True)
    centered = z - average
    inverse = lax.rsqrt(jnp.mean(centered * centered, axis=1, keepdims=True) + EPSILON)
    return centered * inverse, inverse


def center_back(e, normed, inverse):
    first = jnp.mean(e, axis=1, keepdims=True)
    second = jnp.mean(e * normed, axis=1, keepdims=True)
    return inverse * (e - first - normed * second)


def middle_kernel(
    meta, x, cot, phi, main, small_in,
    out_weight, up_own, up_here, up_there, down_own, down_here, down_there, bias_own, bias_other, vectors,
    layer_out, hidden_grad, normed_out, inverse_out, att_out, invden_out,
    active_out, dup_out, hidden_out, dffn_out, sums, up_sum,
    tabs, spread, gates, other, up_other, down_other, small, sems, half_sems, info,
):
    t = pl.program_id(0)
    docs = Documents(meta, info, x.shape[0])
    pairs = tabs.shape[0]
    width = pairs * 128
    core = meta[SLOTS + 1]

    def halves():
        copies = []
        for target, here, there in [(up_other, up_here, up_there), (down_other, down_here, down_there)]:
            count = here.shape[0]
            for source, place in [(here, core), (there, 1 - core)]:
                span = pl.ds(pl.multiple_of(place * count, count), count)
                copies.append((source, target.at[span]))
        return [
            pltpu.make_async_copy(source, target, half_sems.at[i])
            for i, (source, target) in enumerate(copies)
        ]

    @pl.when(t == 0)
    def _():
        for copy in halves():
            copy.start()
        docs.setup()
        fill_tables(tabs, main, True)
        copy_small(docs, small_in, small, sems)
        sums[...] = jnp.zeros_like(sums)
        up_sum[...] = jnp.zeros_like(up_sum)

    for p in range(pairs):
        spread[:, p * 256 : (p + 1) * 256] = nt(phi[:, p * 512 : (p + 1) * 512], tabs[p])

    @pl.when(docs.slow())
    def _():
        def body(rows, mask, j):
            wide = jnp.concatenate([mask] * 2, axis=1)
            for p in range(pairs):
                got = nt(phi[rows, p * 512 : (p + 1) * 512], small_table(small, j, p, pairs, True))
                old = spread[rows, p * 256 : (p + 1) * 256]
                spread[rows, p * 256 : (p + 1) * 256] = jnp.where(wide, got, old)

        docs.each_small(body)

    live = docs.live()
    for p in range(pairs):
        numerator = spread[:, p * 256 : p * 256 + 128]
        denominator = spread[:, p * 256 + 128 : (p + 1) * 256]
        inverse = jnp.where(live, 1.0 / jnp.where(live, denominator, 1.0), 0.0)
        invden_out[:, p * 128 : (p + 1) * 128] = inverse
        att_out[:, p * 128 : (p + 1) * 128] = (numerator * inverse).astype(BF16)

    def vector(i):
        return vectors[i : i + 1, :]

    branch = nn(att_out[...], out_weight[...]) + vector(0)
    first, first_inverse = center(x[...].astype(F32) + branch)
    normed_out[...] = first
    inverse_out[...] = jnp.broadcast_to(first_inverse, inverse_out.shape)
    hidden = first * vector(1) + vector(2)
    hidden_low = hidden.astype(BF16)
    hidden_out[...] = hidden_low
    step = 512
    half = up_own.shape[1]

    @pl.when(t == 0)
    def _():
        for copy in halves():
            copy.wait()

    for which, (up, bias, act) in enumerate(
        [(up_own, bias_own, active_out), (up_other, bias_other, other)]
    ):
        for c in range(0, half, step):
            value = nn(hidden_low, up[:, c : c + step]) + bias[:, c : c + step]
            cdf = 0.5 + 0.5 * lax.erf(value * math.sqrt(0.5))
            gates[:, which * half + c : which * half + c + step] = cdf + value * jnp.exp2(
                value * value * (-0.5 * LOG2E)
            ) * (1.0 / math.sqrt(2.0 * math.pi))
            act[:, c : c + step] = (value * cdf).astype(BF16)
    total = hidden + vector(3)
    total = total + nn(active_out[...], down_own[...])
    total = total + nn(other[...], down_other[...])
    second, second_inverse = center(total)
    layer_out[...] = (second * vector(4) + vector(5)).astype(BF16)
    g = cot[...].astype(F32)
    sums[0:8, :] += fold_rows(g * second)
    sums[8:16, :] += fold_rows(g)
    dsecond = center_back(g * vector(4), second, second_inverse)
    dffn = dsecond.astype(BF16)
    dffn_out[...] = dffn
    sums[16:24, :] += fold_rows(dffn.astype(F32))
    for which, (down, dup_ref) in enumerate([(down_own, dup_out), (down_other, other)]):
        for c in range(0, half, step):
            gate = gates[:, which * half + c : which * half + c + step]
            dup = (nt(dffn, down[c : c + step, :]) * gate).astype(BF16)
            dup_ref[:, c : c + step] = dup
            if which == 0:
                up_sum[:, c : c + step] += fold_rows(dup.astype(F32))
    dsecond = dsecond + nt(dup_out[...], up_own[...])
    dsecond = dsecond + nt(other[...], up_other[...])
    hidden_grad[...] = dsecond


def attention_back_kernel(
    meta, hidden_grad, normed, inverse, att, invden, phi, out_weight, gain, select, more, up_sum,
    dfirst_out, dbranch_out, mixed, chosen, sums, main, small_out,
    acc, sacc, small, sems, info,
):
    t = pl.program_id(0)
    docs = Documents(meta, info, att.shape[0])
    pairs = acc.shape[0]

    @pl.when(t == 0)
    def _():
        docs.setup()
        acc[...] = jnp.zeros_like(acc)
        sums[...] = jnp.zeros_like(sums)

        for j in range(1, SLOTS):

            @pl.when(docs.present(j))
            def _():
                sacc[j - 1] = jnp.zeros_like(sacc[j - 1])

    grad = hidden_grad[...]
    first = normed[...]
    sums[0:8, :] += fold_rows(grad * first)
    sums[8:16, :] += fold_rows(grad)
    dfirst = center_back(grad * gain[...], first, inverse[:, 0:1])
    dfirst_out[...] = dfirst
    dbranch = dfirst.astype(BF16)
    dbranch_out[...] = dbranch
    sums[16:24, :] += fold_rows(dbranch.astype(F32))
    chosen[...] = nn(att[...], select[...]).astype(BF16)
    slow = docs.slow()
    datt = nt(dbranch, out_weight[...])
    ratio = datt * invden[...]
    dden = -ratio * att[...].astype(F32)
    for p in range(pairs):
        mixed[:, p * 256 : p * 256 + 128] = ratio[:, p * 128 : (p + 1) * 128].astype(BF16)
        mixed[:, p * 256 + 128 : (p + 1) * 256] = dden[:, p * 128 : (p + 1) * 128].astype(BF16)

    @pl.when(jnp.logical_not(slow))
    def _():
        for p in range(pairs):
            acc[p] += tn(mixed[:, p * 256 : (p + 1) * 256], phi[:, p * 512 : (p + 1) * 512])

    @pl.when(slow)
    def _():
        mask = docs.main()
        for p in range(pairs):
            part = masked(mask, mixed[:, p * 256 : (p + 1) * 256]).astype(BF16)
            acc[p] += tn(part, phi[:, p * 512 : (p + 1) * 512])

        def body(rows, mask, j):
            for p in range(pairs):
                part = masked(mask, mixed[rows, p * 256 : (p + 1) * 256]).astype(BF16)
                sacc[j - 1, p] += tn(part, phi[rows, p * 512 : (p + 1) * 512])

        docs.each_small(body)

    @pl.when(t == pl.num_programs(0) - 1)
    def _():
        pack_tables(main, 0, acc, None)
        lines = []
        for source in (sums, more, up_sum):
            for i in range(source.shape[0] // 8):
                line = jnp.sum(source[8 * i : 8 * i + 8, :], axis=0, keepdims=True)
                lines += [line[:, c : c + 256] for c in range(0, source.shape[1], 256)]
        lines.append(jnp.zeros((EXTRA - len(lines), 256), F32))
        main[pl.ds(pairs * 128 + 16, EXTRA), :] = jnp.concatenate(lines, axis=0).astype(BF16)

        for j in range(1, SLOTS):

            @pl.when(docs.present(j))
            def _():
                pack_tables(small, (j - 1) * (pairs * 128 + 16), sacc.at[j - 1], None)

        copy_small(docs, small, small_out, sems)


def feature_back(rows, p, grad, phi, scaled, table):
    span = slice(p * 128, (p + 1) * 128)
    e = (grad * phi[rows, p * 512 : (p + 1) * 512].astype(F32)).astype(BF16)
    back = nt(e, table[p])
    return (back[:, :128] - scaled[rows, span].astype(F32) * back[:, 128:]) * 64 ** (-0.25)


def store_some(ref, rows, span, mask, value):
    old = ref[rows, span].astype(F32)
    ref[rows, span] = jnp.where(mask, value, old).astype(ref.dtype)


def queries_back_kernel(
    meta, mixed, phi, scaled, main, small_in, table, weight, dfirst,
    dquery_out, partial_out, sums, tabs, small, sems, info,
):
    t = pl.program_id(0)
    docs = Documents(meta, info, phi.shape[0])
    pairs = tabs.shape[0]

    @pl.when(t == 0)
    def _():
        docs.setup()
        fill_tables(tabs, main, True)
        copy_small(docs, small_in, small, sems)
        sums[...] = jnp.zeros_like(sums)

    for p in range(pairs):
        grad = nn(mixed[:, p * 256 : (p + 1) * 256], tabs[p])
        du = feature_back(slice(None), p, grad, phi, scaled, table)
        dquery_out[:, p * 128 : (p + 1) * 128] = du.astype(BF16)

    @pl.when(docs.slow())
    def _():
        def body(rows, mask, j):
            for p in range(pairs):
                own = small_table(small, j, p, pairs, True)
                grad = nn(mixed[rows, p * 256 : (p + 1) * 256], own)
                du = feature_back(rows, p, grad, phi, scaled, table)
                store_some(dquery_out, rows, slice(p * 128, (p + 1) * 128), mask, du)

        docs.each_small(body)

    sums[...] += fold_rows(dquery_out[...].astype(F32))
    partial_out[...] = dfirst[...] + nt(dquery_out[...], weight[...])


def keys_back_kernel(
    meta, phi, values, scaled, main, small_in, table, key_weight, value_weight, partial_in,
    djoint_out, tokens_out, sums, tabs, small, sems, info,
):
    t = pl.program_id(0)
    docs = Documents(meta, info, phi.shape[0])
    pairs = tabs.shape[0]
    width = pairs * 128

    @pl.when(t == 0)
    def _():
        docs.setup()
        fill_tables(tabs, main, False)
        copy_small(docs, small_in, small, sems)
        sums[...] = jnp.zeros_like(sums)

    def extended(rows, p):
        value = values[rows, p * 128 : (p + 1) * 128]
        return jnp.concatenate([value, jnp.ones_like(value)], axis=1)

    for p in range(pairs):
        grad = nn(extended(slice(None), p), tabs[p])
        du = feature_back(slice(None), p, grad, phi, scaled, table)
        djoint_out[:, p * 128 : (p + 1) * 128] = du.astype(BF16)
        dvalue = nt(phi[:, p * 512 : (p + 1) * 512], tabs[p, :128, :])
        djoint_out[:, width + p * 128 : width + (p + 1) * 128] = dvalue.astype(BF16)

    @pl.when(docs.slow())
    def _():
        live = docs.live()
        for p in range(2 * pairs):
            part = djoint_out[:, p * 128 : (p + 1) * 128]
            djoint_out[:, p * 128 : (p + 1) * 128] = masked(live, part).astype(BF16)

        def body(rows, mask, j):
            for p in range(pairs):
                own = small_table(small, j, p, pairs, False)
                grad = nn(extended(rows, p), own)
                du = feature_back(rows, p, grad, phi, scaled, table)
                store_some(djoint_out, rows, slice(p * 128, (p + 1) * 128), mask, du)
                dvalue = nt(phi[rows, p * 512 : (p + 1) * 512], own[:128, :])
                span = slice(width + p * 128, width + (p + 1) * 128)
                store_some(djoint_out, rows, span, mask, dvalue)

        docs.each_small(body)

    sums[...] += fold_rows(djoint_out[...].astype(F32))
    tokens_out[...] = (
        partial_in[...]
        + nt(djoint_out[:, :width], key_weight[:, :width])
        + nt(djoint_out[:, width:], value_weight[...])
    ).astype(BF16)


def table_outs(width, extra=0):
    count = width + 16
    small = (SLOTS - 1) * count
    count = count + extra
    anywhere = pl.BlockSpec(memory_space=pl.ANY)
    return [(held((count, 256)), (count, 256), BF16), (anywhere, (small, 256), BF16)]


def table_ins(width):
    return [full((width + 16, 256)), pl.BlockSpec(memory_space=pl.ANY)]


def table_scratch(width):
    return pltpu.VMEM((width // 128, 256, 512), BF16)


def small_scratch(width):
    return pltpu.VMEM(((SLOTS - 1) * (width + 16), 256), BF16)


def run_keys(tile, meta, tokens, key_weight, value_weight, bias, table):
    count, width = tokens.shape
    pairs = table.shape[0]
    wide = pairs * 512
    return call(
        keys_kernel,
        count // tile,
        [
            rows(tile, width), full(key_weight.shape), full((width, width)), full(bias.shape),
            full(table.shape),
        ],
        [
            (rows(tile, wide), (count, wide), BF16),
            (rows(tile, width), (count, width), BF16),
            (rows(tile, width), (count, width), BF16),
        ]
        + table_outs(width),
        [
            pltpu.VMEM((pairs, 128, 512), F32),
            pltpu.VMEM((pairs, 8, 512), F32),
            pltpu.VMEM((SLOTS - 1, pairs, 128, 512), F32),
            pltpu.VMEM((SLOTS - 1, pairs, 8, 512), F32),
            small_scratch(width),
            pltpu.SemaphoreType.DMA((SLOTS - 1,)),
            pltpu.SMEM((3 * SLOTS,), jnp.int32),
        ],
        10e9,
    )(meta, tokens, key_weight, value_weight, bias, table)


def run_queries(tile, meta, tokens, weight, bias, table, select):
    count, width = tokens.shape
    wide = table.shape[0] * 512
    own_rows = select.shape[1]
    return call(
        queries_kernel,
        count // tile,
        [
            rows(tile, width), column((width, width), 0), full(bias.shape), full(table.shape),
            full((width, own_rows)),
        ],
        [
            (rows(tile, wide), (count, wide), BF16),
            (rows(tile, width), (count, width), BF16),
            (rows(tile, own_rows), (count, own_rows), BF16),
        ],
        [],
        6e9,
    )(meta, tokens, weight, bias, table, select)


def run_middle(
    tile, meta, tokens, cotangent, phi, moments, small, query_out, up_own, up_here, up_there,
    down_own, down_here, down_there, bias_own, bias_other, vectors,
):
    count, width = tokens.shape
    half = up_own.shape[1]
    wide = phi.shape[1]
    pairs = width // 128
    return call(
        middle_kernel,
        count // tile,
        [rows(tile, width), rows(tile, width), rows(tile, wide)]
        + table_ins(width)
        + [
            column((width, width), 1),
            full((width, half)),
            pl.BlockSpec(memory_space=pl.ANY),
            pl.BlockSpec(memory_space=pl.ANY),
            full((half, width)),
            pl.BlockSpec(memory_space=pl.ANY),
            pl.BlockSpec(memory_space=pl.ANY),
            full((1, half)),
            full((1, half)),
            full((8, width)),
        ],
        [
            (rows(tile, width), (count, width), BF16),
            (rows(tile, width), (count, width), F32),
            (rows(tile, width), (count, width), F32),
            (rows(tile, 128), (count, 128), F32),
            (rows(tile, width), (count, width), BF16),
            (rows(tile, width), (count, width), F32),
            (rows(tile, half), (count, half), BF16),
            (rows(tile, half), (count, half), BF16),
            (rows(tile, width), (count, width), BF16),
            (rows(tile, width), (count, width), BF16),
            (held((24, width)), (24, width), F32),
            (held((8, half)), (8, half), F32),
        ],
        [
            table_scratch(width),
            pltpu.VMEM((tile, pairs * 256), F32),
            pltpu.VMEM((tile, 2 * half), F32),
            pltpu.VMEM((tile, half), BF16),
            pltpu.VMEM((width, half), BF16),
            pltpu.VMEM((half, width), BF16),
            small_scratch(width),
            pltpu.SemaphoreType.DMA((SLOTS - 1,)),
            pltpu.SemaphoreType.DMA((4,)),
            pltpu.SMEM((3 * SLOTS,), jnp.int32),
        ],
        30e9,
    )(
        meta, tokens, cotangent, phi, moments, small, query_out, up_own, up_here, up_there,
        down_own, down_here, down_there, bias_own, bias_other, vectors,
    )


def run_attention_back(
    tile, meta, hidden_grad, normed, inverse, att, invden, phi, query_out, gain, select, sums, up_sum
):
    count, width = att.shape
    wide = phi.shape[1]
    pairs = width // 128
    own_rows = select.shape[1]
    half = up_sum.shape[1]
    return call(
        attention_back_kernel,
        count // tile,
        [
            rows(tile, width), rows(tile, width), rows(tile, 128), rows(tile, width), rows(tile, width),
            rows(tile, wide), column((width, width), 1), full((1, width)), full((width, own_rows)),
            full((24, width)), full((8, half)),
        ],
        [
            (rows(tile, width), (count, width), F32),
            (rows(tile, width), (count, width), BF16),
            (rows(tile, 2 * width), (count, 2 * width), BF16),
            (rows(tile, own_rows), (count, own_rows), BF16),
            (held((24, width)), (24, width), F32),
        ]
        + table_outs(width, EXTRA),
        [
            pltpu.VMEM((pairs, 256, 512), F32),
            pltpu.VMEM((SLOTS - 1, pairs, 256, 512), F32),
            small_scratch(width),
            pltpu.SemaphoreType.DMA((SLOTS - 1,)),
            pltpu.SMEM((3 * SLOTS,), jnp.int32),
        ],
        6e9,
    )(
        meta, hidden_grad, normed, inverse, att, invden, phi, query_out, gain, select, sums, up_sum
    )


def run_queries_back(tile, meta, mixed, phi, scaled, moments, small, table, weight, dfirst):
    count, width = scaled.shape
    wide = phi.shape[1]
    return call(
        queries_back_kernel,
        count // tile,
        [rows(tile, 2 * width), rows(tile, wide), rows(tile, width)]
        + table_ins(width)
        + [full(table.shape), column((width, width), 0), rows(tile, width)],
        [
            (rows(tile, width), (count, width), BF16),
            (rows(tile, width), (count, width), F32),
            (held((8, width)), (8, width), F32),
        ],
        [
            table_scratch(width),
            small_scratch(width),
            pltpu.SemaphoreType.DMA((SLOTS - 1,)),
            pltpu.SMEM((3 * SLOTS,), jnp.int32),
        ],
        8e9,
    )(meta, mixed, phi, scaled, moments, small, table, weight, dfirst)


def run_keys_back(
    tile, meta, phi, values, scaled, moments, small, table, key_weight, value_weight, partial
):
    count, width = scaled.shape
    wide = phi.shape[1]
    return call(
        keys_back_kernel,
        count // tile,
        [rows(tile, wide), rows(tile, width), rows(tile, width)]
        + table_ins(width)
        + [full(table.shape), full(key_weight.shape), full((width, width)), rows(tile, width)],
        [
            (rows(tile, 2 * width), (count, 2 * width), BF16),
            (rows(tile, width), (count, width), BF16),
            (held((8, 2 * width)), (8, 2 * width), F32),
        ],
        [
            table_scratch(width),
            small_scratch(width),
            pltpu.SemaphoreType.DMA((SLOTS - 1,)),
            pltpu.SMEM((3 * SLOTS,), jnp.int32),
        ],
        12e9,
    )(
        meta, phi, values, scaled, moments, small, table, key_weight, value_weight, partial,
    )


def local(
    tokens, document_lengths, feature_maps, joint_weight, joint_bias, output_weight, output_bias,
    first_gain, first_shift, up_weight, up_bias, down_weight, down_bias, second_gain, second_shift,
    cotangent,
):
    count, width = tokens.shape
    heads, head_size, feature_count = feature_maps.shape
    pairs = heads // 2
    half = up_weight.shape[1]
    rank = lax.axis_index("dp")
    dp = lax.axis_size("dp")
    mp = lax.axis_size("mp")
    mp_rank = lax.axis_index("mp")

    shard = joint_weight.shape[0]
    small_vectors = [joint_bias, output_bias, first_gain, first_shift, second_gain, second_shift]
    stacks = -(-len(small_vectors) // shard)
    small_vectors = jnp.stack([jnp.pad(v, (0, 128 - v.shape[0])) for v in small_vectors])
    small_vectors = jnp.pad(small_vectors, ((0, stacks * shard - small_vectors.shape[0]), (0, 0)))
    small_vectors = jnp.concatenate(
        [small_vectors[i * shard : (i + 1) * shard] for i in range(stacks)], axis=1
    )
    core = mine(1)

    def own_part(a):
        return lax.dynamic_slice_in_dim(a, core * (a.shape[0] // 2), a.shape[0] // 2, 0)

    far_weight = swap_mp(joint_weight)
    far_vectors = swap_mp(small_vectors)

    def over_x(own, other):
        return join_pair(own, other, mp_rank, 0).reshape(2 * shard, -1)

    value_chain = Gather(
        over_x(joint_weight[:, 2 * width :], far_weight[:, 2 * width :]), near_first()
    ).start()
    key_chain = Gather(
        jnp.concatenate(
            [
                over_x(joint_weight[:, width : 2 * width], far_weight[:, width : 2 * width]),
                over_x(small_vectors, far_vectors),
            ],
            axis=1,
        ),
        far_first(),
    ).start()
    early = key_chain.a
    query_out = lax.all_gather(
        after(jnp.concatenate([joint_weight[:, :width], output_weight], axis=1), early),
        ("dp", "mp"),
        axis=0,
        tiled=True,
    )
    up_here = swap_mp(after(own_part(up_weight), early))
    down_here = swap_mp(after(own_part(down_weight), early))
    meta = jnp.concatenate(
        [
            document_lengths[0],
            jnp.stack([rank * count, core]).astype(jnp.int32),
            jnp.zeros((SLOTS - 2,), jnp.int32),
        ]
    )

    key_chain.finish()
    value_chain.finish()
    while key_chain.order:
        value_chain.start()
        key_chain.start()
        key_chain.finish()
        value_chain.finish()
    key_weight = key_chain.result()
    value_weight = value_chain.result()

    vectors_all = key_weight[:, width:].reshape(dp * mp, shard, stacks * 128)

    def vector(i, size):
        start = i // shard * 128
        return vectors_all[:, i % shard, start : start + size].reshape(-1).astype(F32)

    joint_offset = vector(0, joint_bias.shape[0])[None, :]
    bias_own = up_bias[None, :].astype(F32)

    pair_maps = feature_maps.reshape(pairs, 2, head_size, feature_count)
    blank = jnp.zeros_like(pair_maps[:, 0])
    table = jnp.concatenate(
        [
            jnp.concatenate([pair_maps[:, 0], blank], axis=2),
            jnp.concatenate([blank, pair_maps[:, 1]], axis=2),
            jnp.concatenate([blank + 1, blank], axis=2),
            jnp.concatenate([blank, blank + 1], axis=2),
        ],
        axis=1,
    )
    bits = dp_bits()
    far, middle_bits, near = bits[0], bits[1:-2], bits[-2:-1]
    owner_order = [1] + near + middle_bits + [far]
    own_rows = width // mp
    index = jnp.arange(own_rows, dtype=jnp.int32)
    owner = sum(
        (index // shard // (dp // 2 >> place)) % 2 * bit for place, bit in enumerate(owner_order)
    )
    source = owner * (shard * mp) + mp_rank * shard + index % shard
    select = (jnp.arange(width, dtype=jnp.int32)[:, None] == source[None, :]).astype(BF16)

    phi_k, values, scaled_k, moments, small_moments = run_keys(
        2 * TILE, meta, tokens, key_weight, value_weight, joint_offset, table
    )

    up_there = swap_dp(after(up_here, moments), 1)
    down_there = swap_dp(after(down_here, up_there), 1)
    bias_other = swap_mp(after(up_bias, moments)[None, :]).astype(F32)
    vectors_all = after(vectors_all, moments)
    parts = [vector(i, shard) for i in range(1, 6)]
    vectors = jnp.stack(
        [parts[0], parts[1], parts[2], down_bias.astype(F32), parts[3], parts[4], parts[4], parts[4]]
    )
    others = middle_bits + near
    moments_sum = TableSum(moments).add()
    for bit in reversed(others):
        moments_sum.swap(bit).add()
    moments_sum.swap(far)
    phi_q, scaled_q, tokens_own = run_queries(
        TILE, meta, after(tokens, moments_sum.own), query_out, joint_offset, table, select
    )
    moments = moments_sum.add(phi_q).swap(1).join()
    (
        layer_output, hidden_grad, normed, inverse, att, invden, active, dup, hidden_low, dffn, sums, up_sum,
    ) = run_middle(
        TILE, meta, tokens, cotangent, phi_q, moments, small_moments, query_out, up_weight,
        up_here, up_there, down_weight, down_here, down_there, bias_own, bias_other, vectors,
    )

    dfirst, dbranch, mixed, att_own, first_sums, dmoments, small_dmoments = run_attention_back(
        TILE, meta, hidden_grad, normed, inverse, att, invden, phi_q, query_out, vectors[1:2],
        select, sums, up_sum,
    )

    dmoments_sum = TableSum(dmoments)
    down_grad = tn(after(active, dmoments), dffn).astype(BF16)
    down = Sum(down_grad, [1] + near + middle_bits)
    dmoments_sum.add(down_grad)
    first_bit = True
    for bit in middle_bits:
        dmoments_sum.swap(bit)
        if first_bit:
            down.start(dmoments_sum.own)
            up_grad = tn(after(hidden_low, dmoments_sum.own), dup).astype(BF16)
            up = Sum(up_grad, [1] + middle_bits + near)
            down.finish(up_grad)
            up.start(down.a)
            down.start()
            out_grad = tn(after(att_own, up_grad), dbranch).astype(BF16)
            up.finish(out_grad)
            dmoments_sum.add(up.a)
            first_bit = False
        else:
            dmoments_sum.add()
    dmoments_sum.swap(far)
    up.start(dmoments_sum.own)
    dquery, partial_tokens, query_sums = run_queries_back(
        2 * TILE, meta, mixed, phi_q, scaled_q, moments, small_moments, table, query_out,
        after(dfirst, dmoments_sum.own, up.own),
    )
    dmoments_sum.add(dquery).swap(near[0])
    down.finish(dmoments_sum.own).start()
    up.finish(down.a).start()
    query_grad = tn(after(tokens_own, up.a), dquery).astype(BF16)
    dmoments_sum.add(query_grad).swap(1)
    query_out_sum = Sum(jnp.concatenate([query_grad, out_grad], axis=1), owner_order)
    query_out_sum.start(dmoments_sum.own)
    dmoments = dmoments_sum.join(query_out_sum.own)
    down.finish(query_out_sum.own)
    up.finish(down.a)
    while down.order:
        down.start().finish()
        up.start().finish()
    down.start_swap(far)
    up.start_swap(far, down.a)
    query_out_sum.finish(up.a).start()
    dkey_value, tokens_grad, key_sums = run_keys_back(
        2 * TILE, meta, phi_k, values, scaled_k, dmoments, small_dmoments, table, key_weight,
        value_weight, after(partial_tokens, query_out_sum.own, up.own, down.own),
    )
    down.finish_swap(dkey_value).start_back()
    up.finish_swap(down.a).start_back()
    key_value_grad = tn(after(tokens_own, up.a), dkey_value).astype(BF16)
    biases = jnp.concatenate([jnp.sum(query_sums, axis=0), jnp.sum(key_sums, axis=0)])
    per_owner = biases.shape[0] // dp
    biases = biases.reshape((2,) * len(bits) + (-1,))
    biases = biases.transpose([bits.index(bit) for bit in owner_order] + [len(bits)])
    biases = biases.reshape(dp * shard, -1)
    bias_columns = biases.shape[1]
    biases = jnp.pad(biases, ((0, 0), (0, 128 - bias_columns))).astype(BF16)
    key_value_sum = Sum(jnp.concatenate([key_value_grad, biases], axis=1), owner_order).start()
    query_out_sum.finish(key_value_sum.own).start()
    key_value_sum.finish(query_out_sum.own).start()
    while len(down.done) > 1:
        down.finish_back(key_value_sum.own).start_back()
        up.finish_back(down.a).start_back()
        if query_out_sum.order:
            query_out_sum.finish(up.a)
            if query_out_sum.order:
                query_out_sum.start()
        key_value_sum.finish(up.a)
        if key_value_sum.order:
            key_value_sum.start()
    down_total = down.finish_back(key_value_sum.own).a
    up_total = up.finish_back(down_total).a
    if query_out_sum.order:
        query_out_sum.finish(up.a)
    query_out_total = query_out_sum.rest().astype(F32)
    if key_value_sum.order:
        key_value_sum.finish(up.a)
    key_value_total = key_value_sum.rest().astype(F32)

    extra = dmoments[width + 16 :].reshape(-1).astype(F32)

    def owned(place, size=width):
        part = size // (dp * mp)
        start = place * width + (rank * mp + mp_rank) * part
        return lax.dynamic_slice_in_dim(extra, start, part, 0)

    bias_total = key_value_total[:, 2 * width : 2 * width + bias_columns].reshape(mp, -1)
    bias_total = lax.dynamic_index_in_dim(bias_total, mp_rank, 0, False)

    return (
        layer_output,
        tokens_grad,
        jnp.concatenate([query_out_total[:, :width], key_value_total[:, : 2 * width]], axis=1),
        bias_total,
        query_out_total[:, width:],
        owned(2),
        owned(0),
        owned(1),
        up_total.astype(F32),
        extra[6 * width : 6 * width + half],
        down_total.astype(F32),
        extra[5 * width : 6 * width],
        owned(3),
        owned(4),
    )


def solution(mesh):
    shared = P(("dp", "mp"))
    in_specs = (
        P("dp", None), P(), P(), P(("dp", "mp"), None), shared, P(("dp", "mp"), None), shared, shared,
        shared, P(None, "mp"), P("mp"), P("mp", None), P(), shared, shared, P("dp", None),
    )
    out_specs = (
        P("dp", None), P("dp", None), P(("dp", "mp"), None), shared, P(("dp", "mp"), None), shared,
        shared, shared, P(None, "mp"), P("mp"), P("mp", None), P(), shared, shared,
    )
    return jax.shard_map(local, mesh=mesh, in_specs=in_specs, out_specs=out_specs, check_vma=False)
```
